256 devices in a mesh: seq: 32 (over y, z), exp: 8 (over x, core).
Axes of the slice: x: 4, y: 4, z: 8, core: 2. Of those that a mesh axis runs over, the one named last changes fastest.
Arguments:
- block_in: bfloat16 [49152, 1024], P(('seq', 'exp')), may hold values from -24 to 24
- out_grad: bfloat16 [49152, 1024], P(('seq', 'exp')), may hold values from -6 to 6
- gate_values: bfloat16 [49152, 2], P(('seq', 'exp')), may hold values from 0.099609375 to 1
- expert_ids: int32 [49152, 2], P(('seq', 'exp')), may hold values from 0 to 7, all different within a row; in each aligned block of 192 rows (0 to 191, 192 to 383, ...) at most 60 rows name the same one
- conv_kernel: bfloat16 [31, 1024], replicated, may hold values from -1 to 1
- expert_weights: bfloat16 [8, 1024, 6144], P('exp', 'seq'), may hold values from -0.1875 to 0.1875
Outputs:
- input_grad: bfloat16 [49152, 1024], P(('seq', 'exp'))
- weight_grad: bfloat16 [8, 1024, 6144], P('exp', 'seq')
- gate_grad: bfloat16 [49152, 2], P(('seq', 'exp'))
The draws below stay inside these ranges and needn't reach their ends.
Inputs may be any that keep to these rules, and one draw needn't show every extreme that they name: `expert_ids`: each frame names two different experts. Among the frames of one device (aligned blocks of 192 frames) no expert is named more than 60 times, a bound that some block reaches.
All inputs are finite; a program needn't handle non-finite values.
Results may differ from the reference program's by a relative error of at most 0.02.
Values may be sent and summed in bfloat16 or wider, within the bound.
No kernel may reach another device: no remote copies, remote signals or barrier semaphores. Data moves between devices by JAX's collectives and lax.ppermute only.
A program may use at most 128 MiB of HBM per device.

```python
import math
import jax
import jax.numpy as jnp
import numpy as np
from jax import lax

D = 1024
FF = 2048
TAPS = 31
HALF = 15
TOK_DEV = 192
EXPERTS = 8
CAP = 60
FRAMES = 49152
N_SEQ = 32
N_EXP = 8


def with_spikes(result, own_key, source, target, blocks, factor):
    owner, partner = [(jnp.arange(result.shape[axis_at]) // (result.shape[axis_at] // blocks)).reshape([-1 if axis == axis_at else 1 for axis in range(result.ndim)]) for axis_at in (source, target)]
    chosen = jax.random.permutation(own_key, blocks)[partner]
    strong = (owner == chosen) | (owner == (partner + blocks // 2) % blocks)
    return jnp.where(strong, factor * result, result)


def steps_of(own_key, extent, cuts, smallest, high):
    def one(position, parts):
        heights = jax.random.uniform(jax.random.fold_in(jax.random.fold_in(own_key, 6), position), (parts,), jnp.float32, smallest / len(cuts), high / len(cuts))
        return jnp.repeat(jnp.exp(heights), extent[position] // parts).reshape((-1,) + (1,) * (len(extent) - position - 1))

    loudness = one(*cuts[0])
    for cut in cuts[1:]:
        loudness = loudness * one(*cut)
    return loudness


def assign_block(stream_key, own, number, rows, number_of, top, most, skew):
    ranking = jax.random.permutation(stream_key, number_of)
    heavy_load, common = load_shares(number_of, rows * top, most, skew, True), load_shares(number_of, rows * top, most, skew, False)
    places = jnp.arange(number_of)

    def named(tallies, offset_by):
        used = int((tallies > 0).sum())
        fixed = max(1, used // 4)
        shifted = fixed + (places - fixed + offset_by * (used - fixed)) % max(1, number_of - fixed)
        return jnp.zeros((number_of,), jnp.int32).at[ranking[jnp.where(places < fixed, places, shifted)]].set(jnp.asarray(tallies, jnp.int32))

    tallies = jnp.where(number % 4 == 0, named(heavy_load, number // 4), named(common, number - number // 4 - 1))
    mixed = jax.random.permutation(jax.random.fold_in(own, 3), number_of)
    source_of, taker = mixed[0:number_of // 2 * 2:2], mixed[1:number_of // 2 * 2:2]
    slack = jnp.minimum(tallies[source_of] - 1, most - tallies[taker]) // 2
    slack = jnp.where((source_of == ranking[0]) | (taker == ranking[0]) | (tallies[taker] == 0), 0, jnp.maximum(slack, 0))
    shifted = jax.random.randint(jax.random.fold_in(own, 4), (number_of // 2,), 0, 1 << 20) % (slack + 1)
    tallies = tallies.at[source_of].add(-shifted).at[taker].add(shifted)
    members = jnp.searchsorted(jnp.cumsum(tallies), jnp.arange(rows * top), side="right").astype(jnp.int32)
    table = members.reshape(top, rows).T
    table = table[jax.random.permutation(jax.random.fold_in(own, 1), rows)]
    offset_by = jax.random.randint(jax.random.fold_in(own, 2), (rows, 1), 0, top)
    return jnp.take_along_axis(table, (jnp.arange(top)[None, :] + offset_by) % top, axis=1)


def load_shares(amount, total, reach, slope, full):
    weights = [(1 << 20) // math.isqrt(standing ** slope) + 1 for standing in range(1, amount + 1)]
    largest = reach if full else min(reach, max(-(-total // amount), total * weights[0] // sum(weights)))
    least = 1 if total - largest >= amount - 1 else 0
    counts, rest = [largest] + [least] * (amount - 1), total - largest - least * (amount - 1)
    while rest > 0:
        free = [i for i in range(1, amount) if counts[i] < largest] or [i for i in range(1, amount) if counts[i] < reach]
        whole, budget = sum([weights[i] for i in free]), rest
        for i in free:
            addition = min(reach - counts[i], max(1, budget * weights[i] // whole), rest)
            counts[i] = counts[i] + addition
            rest = rest - addition
    return np.array(counts)


def centred(stream_key, extent, spread, most, split=(), held_as=jnp.bfloat16):
    result = jax.random.normal(stream_key, extent, jnp.float32) * spread
    if len(split) > 0:
        result = steps_of(stream_key, extent, split, -0.22, 0.18) * result
    return jnp.clip(result, min=-most, max=most).astype(held_as)


def gaussian_with(stream_key, shape, scale, limit, cuts, heavy, held_as=jnp.bfloat16):
    values = scale * jax.random.normal(stream_key, shape, jnp.float32)
    if cuts:
        values = values * steps_of(stream_key, shape, cuts, -0.22, 0.18)
    return jnp.clip(with_spikes(values, jax.random.fold_in(stream_key, 3), *heavy), -limit, limit).astype(held_as)


def setup_inputs(seed: int = 0) -> dict:
    seeds = jax.random.split(jax.random.key(seed), 7)
    block_in = gaussian_with(seeds[0], (FRAMES, D), 1.0, 24.0, ((0, 256),), (0, 1, 256, 6.0))
    out_grad = centred(seeds[1], (FRAMES, D), 1.0, 6.0, ((0, 256),))
    gate_values = jnp.clip(0.099609375 + 0.9003906 * jax.random.uniform(seeds[2], (FRAMES, 2), jnp.float32) ** steps_of(seeds[2], (FRAMES, 2), ((0, 256),), -0.2, 0.2), 0.099609375, 1.0).astype(jnp.bfloat16)
    expert_ids_keys = jax.random.split(jax.random.fold_in(seeds[3], 1), FRAMES // TOK_DEV)
    expert_ids_turns = jax.random.permutation(jax.random.fold_in(seeds[3], 3), FRAMES // TOK_DEV)
    expert_ids = jax.vmap(lambda own, number: assign_block(jax.random.fold_in(seeds[3], 2), own, number, TOK_DEV, EXPERTS, 2, CAP, 2))(expert_ids_keys, expert_ids_turns).reshape((FRAMES, 2))
    conv_kernel = centred(seeds[4], (TAPS, D), TAPS ** -0.5, 1.0)
    expert_weights = centred(seeds[5], (EXPERTS, D, 3 * FF), D ** -0.5, 0.1875, ((0, 8), (1, 32)))
    return dict(block_in=block_in, out_grad=out_grad, gate_values=gate_values, expert_ids=expert_ids, conv_kernel=conv_kernel, expert_weights=expert_weights)


def silu_pair(inputs):
    sigmoid = jax.nn.sigmoid(inputs)
    return inputs * sigmoid, sigmoid * (1.0 + inputs * (1.0 - sigmoid))


def expert_backward(rows_in, rows_grad, rows_gate, weights):
    hidden_width = weights.shape[1] // 3
    in_weights = weights[:, :2 * hidden_width]
    down_weights = weights[:, 2 * hidden_width:]
    projected = jnp.dot(rows_in, in_weights, preferred_element_type=jnp.float32)
    gate_input = projected[:, :hidden_width]
    up_input = projected[:, hidden_width:]
    activated, derivative = silu_pair(gate_input)
    hidden = (activated * up_input).astype(jnp.bfloat16)
    expert_out = lax.dot_general(hidden, down_weights, (((1,), (1,)), ((), ())), preferred_element_type=jnp.float32)
    gate_grad = jnp.sum(rows_grad.astype(jnp.float32) * expert_out, axis=1).astype(jnp.bfloat16)
    out_scaled = (rows_gate.astype(jnp.float32)[:, None] * rows_grad.astype(jnp.float32)).astype(jnp.bfloat16)
    hidden_grad = jnp.dot(out_scaled, down_weights, preferred_element_type=jnp.float32)
    pre_grads = jnp.concatenate([(hidden_grad * up_input * derivative).astype(jnp.bfloat16),
                                 (hidden_grad * activated).astype(jnp.bfloat16)], axis=1)
    row_grad = lax.dot_general(pre_grads, in_weights, (((1,), (1,)), ((), ())),
                               preferred_element_type=jnp.float32).astype(jnp.bfloat16)
    return row_grad, gate_grad, pre_grads, out_scaled, hidden


def weight_term(rows_in, pre_grads, out_scaled, hidden):
    contract = (((0,), (0,)), ((), ()))
    return jnp.concatenate([lax.dot_general(rows_in, pre_grads, contract, preferred_element_type=jnp.float32),
                            lax.dot_general(out_scaled, hidden, contract, preferred_element_type=jnp.float32)], axis=1)


def reference(block_in, out_grad, gate_values, expert_ids, conv_kernel, expert_weights):
    group_size = N_EXP * TOK_DEV
    slot_count = N_EXP * CAP

    def one_group(running, group_index):
        first_row = (group_index * group_size).astype(jnp.int32)
        frames_in = lax.dynamic_slice_in_dim(block_in, first_row, group_size, 0)
        frames_grad = lax.dynamic_slice_in_dim(out_grad, first_row, group_size, 0)
        gate_rows = lax.dynamic_slice_in_dim(gate_values, first_row, group_size, 0).reshape(-1)
        owners = lax.dynamic_slice_in_dim(expert_ids, first_row, group_size, 0).reshape(-1)
        rows_in = jnp.repeat(frames_in, 2, axis=0)
        rows_grad = jnp.repeat(frames_grad, 2, axis=0)

        def one_expert(expert):
            picked = jnp.argsort((owners != expert).astype(jnp.int32), stable=True)[:slot_count].astype(jnp.int32)
            is_owner = owners[picked] == expert
            chosen_gate = jnp.where(is_owner, gate_rows[picked], jnp.zeros_like(gate_rows[picked]))
            picked_in = rows_in[picked]
            row_grad, gate_grad, pre_grads, out_scaled, hidden = expert_backward(
                picked_in, rows_grad[picked], chosen_gate, expert_weights[expert])
            expert_term = weight_term(picked_in, pre_grads, out_scaled, hidden)
            gate_grad = jnp.where(is_owner, gate_grad.astype(jnp.float32), jnp.zeros((), jnp.float32))
            return picked, row_grad, gate_grad, expert_term

        picks, row_grads, gate_grads, expert_terms = lax.map(one_expert, jnp.arange(EXPERTS, dtype=jnp.int32))
        picked_all = picks.reshape(-1)
        summed = jnp.zeros((2 * group_size, D), jnp.float32).at[picked_all].add(
            row_grads.reshape(-1, D).astype(jnp.float32))
        frame_grad = frames_grad.astype(jnp.float32) + summed.reshape(group_size, 2, D).sum(axis=1)
        gate_out = jnp.zeros((2 * group_size,), jnp.float32).at[picked_all].add(gate_grads.reshape(-1))
        rounded = lax.optimization_barrier(expert_terms.astype(jnp.bfloat16))
        return running + rounded.astype(jnp.float32), (frame_grad, gate_out.reshape(group_size, 2))

    summed_terms, (frame_grads, gate_outs) = lax.scan(
        one_group, jnp.zeros((EXPERTS, D, 3 * FF), jnp.float32), jnp.arange(N_SEQ, dtype=jnp.int32))
    frame_grads = frame_grads.reshape(-1, D)
    padded = jnp.pad(frame_grads, ((HALF, HALF), (0, 0)))
    input_grad = frame_grads
    for offset in range(TAPS):
        input_grad = input_grad + conv_kernel[offset].astype(jnp.float32) * padded[2 * HALF - offset:2 * HALF - offset + FRAMES]
    return input_grad.astype(jnp.bfloat16), summed_terms.astype(jnp.bfloat16), gate_outs.reshape(-1, 2).astype(jnp.bfloat16)
```

```python
import jax
import jax.numpy as jnp
from jax import lax
from jax.sharding import Mesh, PartitionSpec as P

BF = jnp.bfloat16
F32 = jnp.float32
SLOTS = 64
SPARE = 60
META = 16


def dot(a, b, contract, batch=((), ())):
    return lax.dot_general(a, b, (contract, batch), preferred_element_type=F32)


def ring_gather(shard, axis, place, buffer):
    count = lax.axis_size(axis)
    me = lax.axis_index(axis)
    up = [(i, (i + 1) % count) for i in range(count)]
    down = [(target, source) for source, target in up]
    buffer = place(buffer, shard, me)
    right = left = shard
    for step in range(1, count // 2 + 1):
        right = lax.ppermute(right, axis, up)
        buffer = place(buffer, right, (me - step) % count)
        if step < count - step:
            left = lax.ppermute(left, axis, down)
            buffer = place(buffer, left, (me + step) % count)
    return buffer


def gather_weights(expert_weights):
    ny, nz = lax.axis_size("y"), lax.axis_size("z")
    rows, width = expert_weights.shape[1], expert_weights.shape[2]
    part = width // (3 * ny)
    sliced = expert_weights[0].reshape(rows, 3, ny, part).transpose(2, 0, 1, 3)
    sliced = sliced.reshape(ny, rows, 3 * part)
    mine = lax.all_to_all(sliced, "y", 0, 0, tiled=True)

    def place(buffer, shard, z):
        return lax.dynamic_update_slice(buffer, shard[:, None], (0, z, 0, 0))

    buffer = ring_gather(mine, "z", place, jnp.zeros((ny, nz, rows, 3 * part), BF))
    return buffer.reshape(ny * nz * rows, 3 * part)


def scatter_weight_grad(term):
    ny, nz = lax.axis_size("y"), lax.axis_size("z")
    rows = term.shape[0] // (ny * nz)
    part = term.shape[1] // 3
    blocks = term.reshape(ny, nz, rows, 3 * part).transpose(1, 0, 2, 3)
    mine = lax.psum_scatter(blocks.reshape(nz * ny * rows, 3 * part), "z", scatter_dimension=0, tiled=True)
    back = lax.all_to_all(mine.reshape(ny, rows, 3 * part), "y", 0, 0, tiled=True)
    back = back.reshape(ny, rows, 3, part).transpose(1, 2, 0, 3)
    return back.reshape(1, rows, 3 * ny * part)


def slots_of(chosen):
    frames = chosen.shape[-1]
    before = (jnp.arange(frames)[:, None] < jnp.arange(frames)[None, :]).astype(BF)
    ranks = dot(chosen.astype(BF), before, ((chosen.ndim - 1,), (0,))).astype(jnp.int32)
    return chosen[..., None, :] & (ranks[..., None, :] == jnp.arange(SLOTS)[:, None])


def with_halo(block, width):
    axes = ("y", "z", "x", "c")
    count = 1
    for axis in axes:
        count *= lax.axis_size(axis)
    forward = [(i, i + 1) for i in range(count - 1)]
    backward = [(target, source) for source, target in forward]
    low = lax.ppermute(block[block.shape[0] - width :], axes, forward)
    high = lax.ppermute(block[:width], axes, backward)
    return jnp.concatenate([low, block, high], axis=0)


def local(block_in, out_grad, gate_values, expert_ids, conv_kernel, expert_weights):
    frames, width = block_in.shape
    ny, experts = lax.axis_size("y"), lax.axis_size("x") * lax.axis_size("c")
    group = ("y", "x", "c")
    expert = lax.axis_index("x") * lax.axis_size("c") + lax.axis_index("c")

    meta = jnp.concatenate([expert_ids.astype(BF).T, gate_values.T], axis=0)
    meta = jnp.pad(meta, ((0, META - 4), (0, width - frames)))
    packed = jnp.concatenate([block_in, meta], axis=0)
    all_in = lax.all_gather(packed, group, axis=0, tiled=False)
    all_grad = lax.all_gather(out_grad, group, axis=0, tiled=False)
    blocks = all_in.shape[0]
    weights = gather_weights(expert_weights)
    part = weights.shape[1] // 3
    in_weights, down_weights = weights[:, : 2 * part], weights[:, 2 * part :]

    ids = all_in[:, frames : frames + 2, :frames].astype(jnp.int32) == expert
    gates = all_in[:, frames + 2 : frames + 4, :frames]
    gate = jnp.where(ids[:, 0], gates[:, 0], gates[:, 1])
    chosen = slots_of(ids[:, 0] | ids[:, 1])
    placing = chosen.astype(BF)
    placing_gate = jnp.where(chosen, gate[:, None, :], jnp.zeros((), BF))

    rows_in = dot(placing, all_in[:, :frames], ((2,), (1,)), ((0,), (0,))).astype(BF)
    rows_in = rows_in.reshape(blocks * SLOTS, width)
    projected = dot(rows_in, in_weights, ((1,), (0,)))
    gate_in, up_in = projected[:, :part], projected[:, part:]
    sigmoid = jax.nn.sigmoid(gate_in)
    activated = gate_in * sigmoid
    derivative = sigmoid * (1.0 + gate_in * (1.0 - sigmoid))
    hidden = (activated * up_in).astype(BF)

    rows_q = dot(placing_gate, all_grad, ((2,), (1,)), ((0,), (0,))).astype(BF)
    rows_q = rows_q.reshape(blocks * SLOTS, width)
    hidden_grad = dot(rows_q, down_weights, ((1,), (0,)))
    gate_part = jnp.sum(hidden.astype(F32) * hidden_grad, axis=1).reshape(blocks, 1, SLOTS)
    pre_grads = jnp.concatenate(
        [(hidden_grad * up_in * derivative).astype(BF), (hidden_grad * activated).astype(BF)], axis=1
    )
    row_grad = dot(pre_grads, in_weights, ((1,), (1,))).reshape(blocks, SLOTS, width)
    gate_rows = jnp.pad(gate_part, ((0, 0), (0, 0), (0, width - SLOTS)))
    spare = (jnp.arange(SLOTS) == SPARE)[None, :, None]
    row_grad = jnp.where(spare, gate_rows, row_grad).astype(BF)

    parts = lax.all_to_all(row_grad.reshape(ny, experts * SLOTS, width), "y", 0, 0, tiled=True)
    summed = jnp.sum(parts.astype(F32), axis=0).astype(BF)
    returned = lax.all_to_all(summed.reshape(experts, SLOTS, width), ("x", "c"), 0, 0, tiled=True)

    term = jnp.concatenate(
        [dot(rows_in, pre_grads, ((0,), (0,))), dot(rows_q, hidden, ((0,), (0,)))], axis=1
    ).astype(BF)
    weight_grad = scatter_weight_grad(term)

    own_ids = expert_ids.T[None] == jnp.arange(experts, dtype=jnp.int32)[:, None, None]
    own = slots_of(own_ids[:, 0] | own_ids[:, 1])
    own_placing = own.astype(BF)
    flat = own_placing.reshape(experts * SLOTS, frames)
    frame_grad = out_grad.astype(F32) + dot(
        flat, returned.reshape(experts * SLOTS, width), ((0,), (0,))
    )
    gate_sums = jnp.einsum(
        "es,est,ekt->tk",
        returned[:, SPARE, :SLOTS].astype(F32),
        own.astype(F32),
        own_ids.astype(F32),
        precision="highest",
    )
    gate_out = (gate_sums / gate_values.astype(F32)).astype(BF)

    taps = conv_kernel.shape[0]
    half = (taps - 1) // 2
    kernel_rows = conv_kernel.astype(F32)
    padded = with_halo(frame_grad.astype(BF), half).astype(F32)
    conv_part = jnp.zeros((frames, width), F32)
    for offset in range(taps):
        conv_part = conv_part + kernel_rows[offset] * padded[2 * half - offset : 2 * half - offset + frames]
    input_grad = (frame_grad + conv_part).astype(BF)
    return input_grad, weight_grad, gate_out


def solution(mesh):
    grid = Mesh(mesh.devices.reshape(4, 8, 4, 2), ("y", "z", "x", "c"))
    frames = P(("y", "z", "x", "c"), None)
    weights = P(("x", "c"), ("y", "z"), None)
    in_specs = (frames, frames, frames, frames, P(), weights)
    out_specs = (frames, weights, frames)
    return jax.shard_map(local, mesh=grid, in_specs=in_specs, out_specs=out_specs, check_vma=False)
```

```python
import jax
import jax.numpy as jnp
from jax import lax
from jax.experimental import pallas as pl
from jax.experimental.pallas import tpu as pltpu
from jax.sharding import Mesh, PartitionSpec as P

BF = jnp.bfloat16
F32 = jnp.float32
SLOTS = 64
SPARE = 60
META = 8
STEP = 4


def dot(a, b, contract, batch=((), ())):
    return lax.dot_general(a, b, (contract, batch), preferred_element_type=F32)


def ring_gather(shard, axis, place, buffer):
    count = lax.axis_size(axis)
    me = lax.axis_index(axis)
    up = [(i, (i + 1) % count) for i in range(count)]
    down = [(target, source) for source, target in up]
    buffer = place(buffer, shard, me)
    right = left = shard
    for step in range(1, count // 2 + 1):
        right = lax.ppermute(right, axis, up)
        buffer = place(buffer, right, (me - step) % count)
        if step < count - step:
            left = lax.ppermute(left, axis, down)
            buffer = place(buffer, left, (me + step) % count)
    return buffer


def gather_weights(expert_weights):
    ny, nz = lax.axis_size("y"), lax.axis_size("z")
    rows, width = expert_weights.shape[1], expert_weights.shape[2]
    part = width // (3 * ny)
    sliced = expert_weights[0].reshape(rows, 3, ny, part).transpose(2, 0, 1, 3)
    sliced = sliced.reshape(ny, rows, 3 * part)
    mine = lax.all_to_all(sliced, "y", 0, 0, tiled=True)

    def place(buffer, shard, z):
        return lax.dynamic_update_slice(buffer, shard[:, None], (0, z, 0, 0))

    buffer = ring_gather(mine, "z", place, jnp.zeros((ny, nz, rows, 3 * part), BF))
    return buffer.reshape(ny * nz * rows, 3 * part)


def scatter_weight_grad(term):
    ny, nz = lax.axis_size("y"), lax.axis_size("z")
    rows = term.shape[0] // (ny * nz)
    part = term.shape[1] // 3
    blocks = term.reshape(ny, nz, rows, 3 * part).transpose(1, 0, 2, 3)
    mine = lax.psum_scatter(blocks.reshape(nz * ny * rows, 3 * part), "z", scatter_dimension=0, tiled=True)
    back = lax.all_to_all(mine.reshape(ny, rows, 3 * part), "y", 0, 0, tiled=True)
    back = back.reshape(ny, rows, 3, part).transpose(1, 2, 0, 3)
    return back.reshape(1, rows, 3 * ny * part)


def slots_of(chosen):
    frames = chosen.shape[-1]
    before = (jnp.arange(frames)[:, None] < jnp.arange(frames)[None, :]).astype(BF)
    ranks = dot(chosen.astype(BF), before, ((chosen.ndim - 1,), (0,))).astype(jnp.int32)
    return chosen[..., None, :] & (ranks[..., None, :] == jnp.arange(SLOTS)[:, None])


def with_halo(block, width):
    axes = ("y", "z", "x", "c")
    count = 1
    for axis in axes:
        count *= lax.axis_size(axis)
    forward = [(i, i + 1) for i in range(count - 1)]
    backward = [(target, source) for source, target in forward]
    low = lax.ppermute(block[block.shape[0] - width :], axes, forward)
    high = lax.ppermute(block[:width], axes, backward)
    return jnp.concatenate([low, block, high], axis=0)


def rows_kernel(expert, x_ref, w_ref, wt_ref, r_ref, u_ref, q_ref, pre_ref, h_ref):
    steps, rows, wide = x_ref.shape
    frames, width = rows - META, wide // 2
    part = h_ref.shape[1]
    name = expert[0].astype(F32)
    earlier = lax.broadcasted_iota(jnp.int32, (frames, frames), 0)
    before = (earlier < lax.broadcasted_iota(jnp.int32, (frames, frames), 1)).astype(F32).astype(BF)
    slot = lax.broadcasted_iota(jnp.int32, (SLOTS, frames), 0).astype(F32)
    for j in range(steps):
        meta = x_ref[j, frames:rows, :frames].astype(F32)
        named = (meta == name).astype(F32)
        chosen = named[0:1] + named[1:2]
        ranks = dot(jnp.broadcast_to(chosen, (8, frames)).astype(BF), before, ((1,), (0,)))[0:1]
        gate = named[0:1] * meta[2:3] + named[1:2] * meta[3:4]
        here = jnp.where((slot == ranks) & (chosen > 0.0), 1.0, 0.0)
        place = pl.ds(j * SLOTS, SLOTS)
        u = dot(here.astype(BF), x_ref[j, :frames, :width], ((1,), (0,)))
        u_ref[place] = u.astype(BF)
        q = dot((here * gate).astype(BF), x_ref[j, :frames, width:], ((1,), (0,)))
        q_ref[place] = q.astype(BF)
    projected = dot(u_ref[...], w_ref[:, : 2 * part], ((1,), (0,)))
    hidden_grad = dot(q_ref[...], w_ref[:, 2 * part :], ((1,), (0,)))
    gate_in, up_in = projected[:, :part], projected[:, part:]
    sigmoid = jax.nn.sigmoid(gate_in)
    activated = gate_in * sigmoid
    hidden = (activated * up_in).astype(BF)
    h_ref[...] = hidden
    pre_ref[:, :part] = (hidden_grad * up_in * (sigmoid * (1.0 + gate_in * (1.0 - sigmoid)))).astype(BF)
    pre_ref[:, part:] = (hidden_grad * activated).astype(BF)
    gate_part = jnp.sum(hidden.astype(F32) * hidden_grad, axis=1, keepdims=True)
    r_ref[...] = dot(pre_ref[...], wt_ref[...], ((1,), (0,))).astype(BF)
    row = lax.broadcasted_iota(jnp.int32, (SLOTS, 128), 0)
    lane = lax.broadcasted_iota(jnp.int32, (SLOTS, 128), 1)
    for j in range(steps):
        place = pl.ds(j * SLOTS, SLOTS)
        diagonal = jnp.where(row == lane, gate_part[j * SLOTS : (j + 1) * SLOTS], 0.0)
        line = jnp.sum(diagonal, axis=0, keepdims=True)
        r_ref[place, :128] = jnp.where(row == SPARE, line, r_ref[place, :128].astype(F32)).astype(BF)


def expert_rows(expert, everything, weights):
    blocks, rows, wide = everything.shape
    width, part = wide // 2, weights.shape[1] // 3
    turned = weights[:, : 2 * part].T
    rows_step = STEP * SLOTS
    total = blocks * SLOTS

    def rowwise(columns):
        return pl.BlockSpec((rows_step, columns), lambda i: (i, 0))

    def whole(array):
        return pl.BlockSpec(array.shape, lambda i: (0, 0))

    widths = (width, width, width, 2 * part, part)
    return pl.pallas_call(
        rows_kernel,
        grid=(blocks // STEP,),
        in_specs=[
            pl.BlockSpec(memory_space=pltpu.SMEM),
            pl.BlockSpec((STEP, rows, wide), lambda i: (i, 0, 0)),
            whole(weights),
            whole(turned),
        ],
        out_specs=[rowwise(columns) for columns in widths],
        out_shape=[jax.ShapeDtypeStruct((total, columns), BF) for columns in widths],
        compiler_params=pltpu.CompilerParams(vmem_limit_bytes=52 * 1024 * 1024),
    )(expert.reshape(1).astype(jnp.int32), everything, weights, turned)


def local(block_in, out_grad, gate_values, expert_ids, conv_kernel, expert_weights):
    frames, width = block_in.shape
    ny, experts = lax.axis_size("y"), lax.axis_size("x") * lax.axis_size("c")
    group = ("y", "x", "c")
    expert = lax.axis_index("x") * lax.axis_size("c") + lax.axis_index("c")

    meta = jnp.concatenate([expert_ids.astype(BF).T, gate_values.T], axis=0)
    meta = jnp.pad(meta, ((0, META - 4), (0, 2 * width - frames)))
    packed = jnp.concatenate([jnp.concatenate([block_in, out_grad], axis=1), meta], axis=0)
    everything = lax.all_gather(packed, group, axis=0, tiled=False)
    weights = gather_weights(expert_weights)
    row_grad, rows_in, rows_q, pre_grads, hidden = expert_rows(expert, everything, weights)

    parts = lax.all_to_all(row_grad.reshape(ny, experts * SLOTS, width), "y", 0, 0, tiled=True)
    summed = jnp.sum(parts.astype(F32), axis=0).astype(BF)
    returned = lax.all_to_all(summed.reshape(experts, SLOTS, width), ("x", "c"), 0, 0, tiled=True)

    term = jnp.concatenate(
        [dot(rows_in, pre_grads, ((0,), (0,))), dot(rows_q, hidden, ((0,), (0,)))], axis=1
    ).astype(BF)
    weight_grad = scatter_weight_grad(term)

    own_ids = expert_ids.T[None] == jnp.arange(experts, dtype=jnp.int32)[:, None, None]
    own = slots_of(own_ids[:, 0] | own_ids[:, 1])
    own_placing = own.astype(BF)
    flat = own_placing.reshape(experts * SLOTS, frames)
    frame_grad = out_grad.astype(F32) + dot(
        flat, returned.reshape(experts * SLOTS, width), ((0,), (0,))
    )
    gate_sums = jnp.einsum(
        "es,est,ekt->tk",
        returned[:, SPARE, :SLOTS].astype(F32),
        own.astype(F32),
        own_ids.astype(F32),
        precision="highest",
    )
    gate_out = (gate_sums / gate_values.astype(F32)).astype(BF)

    taps = conv_kernel.shape[0]
    half = (taps - 1) // 2
    kernel_rows = conv_kernel.astype(F32)
    padded = with_halo(frame_grad.astype(BF), half).astype(F32)
    conv_part = jnp.zeros((frames, width), F32)
    for offset in range(taps):
        conv_part = conv_part + kernel_rows[offset] * padded[2 * half - offset : 2 * half - offset + frames]
    input_grad = (frame_grad + conv_part).astype(BF)
    return input_grad, weight_grad, gate_out


def solution(mesh):
    grid = Mesh(mesh.devices.reshape(4, 8, 4, 2), ("y", "z", "x", "c"))
    frames = P(("y", "z", "x", "c"), None)
    weights = P(("x", "c"), ("y", "z"), None)
    in_specs = (frames, frames, frames, frames, P(), weights)
    out_specs = (frames, weights, frames)
    return jax.shard_map(local, mesh=grid, in_specs=in_specs, out_specs=out_specs, check_vma=False)
```

```python
import jax
import jax.numpy as jnp
from jax import lax
from jax.experimental import pallas as pl
from jax.experimental.pallas import tpu as pltpu
from jax.sharding import Mesh, PartitionSpec as P

BF = jnp.bfloat16
F32 = jnp.float32
SLOTS = 64
SPARE = 60
META = 8
STEP = 4


def dot(a, b, contract, batch=((), ())):
    return lax.dot_general(a, b, (contract, batch), preferred_element_type=F32)


def ring_gather(shard, axis, place, buffer):
    count = lax.axis_size(axis)
    me = lax.axis_index(axis)
    up = [(i, (i + 1) % count) for i in range(count)]
    down = [(target, source) for source, target in up]
    buffer = place(buffer, shard, me)
    right = left = shard
    for step in range(1, count // 2 + 1):
        right = lax.ppermute(right, axis, up)
        buffer = place(buffer, right, (me - step) % count)
        if step < count - step:
            left = lax.ppermute(left, axis, down)
            buffer = place(buffer, left, (me + step) % count)
    return buffer


def gather_weights(expert_weights):
    ny, nz = lax.axis_size("y"), lax.axis_size("z")
    rows, width = expert_weights.shape[1], expert_weights.shape[2]
    part = width // (3 * ny)
    sliced = expert_weights[0].reshape(rows, 3, ny, part).transpose(2, 0, 1, 3)
    sliced = sliced.reshape(ny, rows, 3 * part)
    mine = lax.all_to_all(sliced, "y", 0, 0, tiled=True)

    def place(buffer, shard, z):
        return lax.dynamic_update_slice(buffer, shard[:, None], (0, z, 0, 0))

    buffer = ring_gather(mine, "z", place, jnp.zeros((ny, nz, rows, 3 * part), BF))
    return buffer.reshape(ny * nz * rows, 3 * part)


def scatter_weight_grad(term):
    ny, nz = lax.axis_size("y"), lax.axis_size("z")
    rows = term.shape[0] // (ny * nz)
    part = term.shape[1] // 3
    blocks = term.reshape(ny, nz, rows, 3 * part).transpose(1, 0, 2, 3)
    mine = lax.psum_scatter(blocks.reshape(nz * ny * rows, 3 * part), "z", scatter_dimension=0, tiled=True)
    back = lax.all_to_all(mine.reshape(ny, rows, 3 * part), "y", 0, 0, tiled=True)
    back = back.reshape(ny, rows, 3, part).transpose(1, 2, 0, 3)
    return back.reshape(1, rows, 3 * ny * part)


def slots_of(chosen):
    frames = chosen.shape[-1]
    before = (jnp.arange(frames)[:, None] < jnp.arange(frames)[None, :]).astype(BF)
    ranks = dot(chosen.astype(BF), before, ((chosen.ndim - 1,), (0,))).astype(jnp.int32)
    return chosen[..., None, :] & (ranks[..., None, :] == jnp.arange(SLOTS)[:, None])


def with_halo(block, width):
    axes = ("y", "z", "x", "c")
    count = 1
    for axis in axes:
        count *= lax.axis_size(axis)
    forward = [(i, i + 1) for i in range(count - 1)]
    backward = [(target, source) for source, target in forward]
    low = lax.ppermute(block[block.shape[0] - width :], axes, forward)
    high = lax.ppermute(block[:width], axes, backward)
    return jnp.concatenate([low, block, high], axis=0)


def rows_kernel(info, x_ref, w_ref, wt_ref, *refs):
    low_ref, high_ref, u_ref, q_ref, pre_ref, h_ref = refs[-6:]
    steps, rows, wide = x_ref.shape
    frames, width = rows - META, wide // 2
    part, half = h_ref.shape[1], low_ref.shape[1]
    name = info[0].astype(F32)
    earlier = lax.broadcasted_iota(jnp.int32, (frames, frames), 0)
    before = (earlier < lax.broadcasted_iota(jnp.int32, (frames, frames), 1)).astype(F32).astype(BF)
    slot = lax.broadcasted_iota(jnp.int32, (SLOTS, frames), 0).astype(F32)
    for j in range(steps):
        meta = x_ref[j, frames:rows, :frames].astype(F32)
        named = (meta == name).astype(F32)
        chosen = named[0:1] + named[1:2]
        ranks = dot(jnp.broadcast_to(chosen, (8, frames)).astype(BF), before, ((1,), (0,)))[0:1]
        gate = named[0:1] * meta[2:3] + named[1:2] * meta[3:4]
        here = jnp.where((slot == ranks) & (chosen > 0.0), 1.0, 0.0)
        place = pl.ds(j * SLOTS, SLOTS)
        u = dot(here.astype(BF), x_ref[j, :frames, :width], ((1,), (0,)))
        u_ref[place] = u.astype(BF)
        q = dot((here * gate).astype(BF), x_ref[j, :frames, width:], ((1,), (0,)))
        q_ref[place] = q.astype(BF)
    projected = dot(u_ref[...], w_ref[:, : 2 * part], ((1,), (0,)))
    hidden_grad = dot(q_ref[...], w_ref[:, 2 * part :], ((1,), (0,)))
    gate_in, up_in = projected[:, :part], projected[:, part:]
    sigmoid = jax.nn.sigmoid(gate_in)
    activated = gate_in * sigmoid
    hidden = (activated * up_in).astype(BF)
    h_ref[...] = hidden
    pre_ref[:, :part] = (hidden_grad * up_in * (sigmoid * (1.0 + gate_in * (1.0 - sigmoid)))).astype(BF)
    pre_ref[:, part:] = (hidden_grad * activated).astype(BF)
    gate_part = jnp.sum(hidden.astype(F32) * hidden_grad, axis=1, keepdims=True)
    row_grad = dot(pre_ref[...], wt_ref[...], ((1,), (0,))).astype(BF)
    low_ref[...] = row_grad[:, :half]
    high_ref[...] = row_grad[:, half:]
    row = lax.broadcasted_iota(jnp.int32, (SLOTS, 128), 0)
    lane = lax.broadcasted_iota(jnp.int32, (SLOTS, 128), 1)
    for j in range(steps):
        place = pl.ds(j * SLOTS, SLOTS)
        diagonal = jnp.where(row == lane, gate_part[j * SLOTS : (j + 1) * SLOTS], 0.0)
        line = jnp.sum(diagonal, axis=0, keepdims=True)
        low_ref[place, :128] = jnp.where(row == SPARE, line, low_ref[place, :128].astype(F32)).astype(BF)


def expert_rows(expert, group, turn, everything, weights, turned, kept):
    blocks, rows, wide = everything.shape
    groups = lax.axis_size("y")
    width, part = wide // 2, weights.shape[1] // 3
    rows_step = STEP * SLOTS
    steps = blocks // (groups * STEP)
    total, mine = blocks * SLOTS, blocks * SLOTS // groups
    info = jnp.stack([expert, group * steps]).astype(jnp.int32)

    def rowwise(columns, first):
        return pl.BlockSpec((rows_step, columns), lambda i, info: (i + first, 0))

    def whole(array):
        return pl.BlockSpec(array.shape, lambda i, info: (0, 0))

    widths = (width, width, 2 * part, part)
    shapes = [jax.ShapeDtypeStruct((mine, width // 2), BF)] * 2
    shapes += [jax.ShapeDtypeStruct((total, columns), BF) for columns in widths]
    low, high, *kept = pl.pallas_call(
        rows_kernel,
        grid_spec=pltpu.PrefetchScalarGridSpec(
            num_scalar_prefetch=1,
            grid=(steps,),
            in_specs=[
                pl.BlockSpec((STEP, rows, wide), lambda i, info: (info[1] + i, 0, 0)),
                whole(weights),
                whole(turned),
            ]
            + [pl.BlockSpec(memory_space=pl.ANY) for _ in kept],
            out_specs=[rowwise(width // 2, 0)] * 2 + [rowwise(columns, turn * steps) for columns in widths],
        ),
        out_shape=shapes,
        input_output_aliases={4 + k: 2 + k for k in range(len(kept))},
        compiler_params=pltpu.CompilerParams(vmem_limit_bytes=52 * 1024 * 1024),
    )(info, everything, weights, turned, *kept)
    return low, high, kept


def add(*parts):
    return sum(part.astype(F32) for part in parts)


def rows_backward(expert, everything, weights):
    ny = lax.axis_size("y")
    me = lax.axis_index("y")
    up = [(i, (i + 1) % ny) for i in range(ny)]
    down = [(target, source) for source, target in up]
    turned = weights[:, : 2 * (weights.shape[1] // 3)].T

    def send(rows, way):
        return lax.ppermute(rows, "y", way)

    def run(offset, turn, kept):
        return expert_rows(expert, (me + offset) % ny, turn, everything, weights, turned, kept)

    far_low, far_high, kept = run(2, 0, [])
    low_via, high_via = send(far_low, up), send(far_high, down)
    up_low, up_high, kept = run(1, 1, kept)
    from_below_high = send(up_high, up)
    down_low, down_high, kept = run(ny - 1, 2, kept)
    from_above_low = send(down_low, down)
    from_below_low = send(add(up_low, low_via).astype(BF), up)
    from_above_high = send(add(down_high, high_via).astype(BF), down)
    own_low, own_high, kept = run(0, 3, kept)
    low = add(own_low, from_below_low, from_above_low).astype(BF)
    high = add(own_high, from_below_high, from_above_high).astype(BF)
    return jnp.concatenate([low, high], axis=1), kept


def local(block_in, out_grad, gate_values, expert_ids, conv_kernel, expert_weights):
    frames, width = block_in.shape
    ny, experts = lax.axis_size("y"), lax.axis_size("x") * lax.axis_size("c")
    group = ("y", "x", "c")
    expert = lax.axis_index("x") * lax.axis_size("c") + lax.axis_index("c")

    meta = jnp.concatenate([expert_ids.astype(BF).T, gate_values.T], axis=0)
    meta = jnp.pad(meta, ((0, META - 4), (0, 2 * width - frames)))
    packed = jnp.concatenate([jnp.concatenate([block_in, out_grad], axis=1), meta], axis=0)
    everything = lax.all_gather(packed, group, axis=0, tiled=False)
    weights = gather_weights(expert_weights)
    summed, (rows_in, rows_q, pre_grads, hidden) = rows_backward(expert, everything, weights)

    returned = lax.all_to_all(summed.reshape(experts, SLOTS, width), ("x", "c"), 0, 0, tiled=True)

    term = jnp.concatenate(
        [dot(rows_in, pre_grads, ((0,), (0,))), dot(rows_q, hidden, ((0,), (0,)))], axis=1
    ).astype(BF)
    weight_grad = scatter_weight_grad(term)

    own_ids = expert_ids.T[None] == jnp.arange(experts, dtype=jnp.int32)[:, None, None]
    own = slots_of(own_ids[:, 0] | own_ids[:, 1])
    own_placing = own.astype(BF)
    flat = own_placing.reshape(experts * SLOTS, frames)
    frame_grad = out_grad.astype(F32) + dot(
        flat, returned.reshape(experts * SLOTS, width), ((0,), (0,))
    )
    gate_sums = jnp.einsum(
        "es,est,ekt->tk",
        returned[:, SPARE, :SLOTS].astype(F32),
        own.astype(F32),
        own_ids.astype(F32),
        precision="highest",
    )
    gate_out = (gate_sums / gate_values.astype(F32)).astype(BF)

    taps = conv_kernel.shape[0]
    half = (taps - 1) // 2
    kernel_rows = conv_kernel.astype(F32)
    padded = with_halo(frame_grad.astype(BF), half).astype(F32)
    conv_part = jnp.zeros((frames, width), F32)
    for offset in range(taps):
        conv_part = conv_part + kernel_rows[offset] * padded[2 * half - offset : 2 * half - offset + frames]
    input_grad = (frame_grad + conv_part).astype(BF)
    return input_grad, weight_grad, gate_out


def solution(mesh):
    grid = Mesh(mesh.devices.reshape(4, 8, 4, 2), ("y", "z", "x", "c"))
    frames = P(("y", "z", "x", "c"), None)
    weights = P(("x", "c"), ("y", "z"), None)
    in_specs = (frames, frames, frames, frames, P(), weights)
    out_specs = (frames, weights, frames)
    return jax.shard_map(local, mesh=grid, in_specs=in_specs, out_specs=out_specs, check_vma=False)
```

```python
import jax
import jax.numpy as jnp
from jax import lax
from jax.experimental import pallas as pl
from jax.experimental.pallas import tpu as pltpu
from jax.sharding import Mesh, PartitionSpec as P

BF = jnp.bfloat16
F32 = jnp.float32
SLOTS = 64
SPARE = 60
META = 8
STEP = 4


def dot(a, b, contract, batch=((), ())):
    return lax.dot_general(a, b, (contract, batch), preferred_element_type=F32)


def ring_gather(shard, axis, place, buffer):
    count = lax.axis_size(axis)
    me = lax.axis_index(axis)
    up = [(i, (i + 1) % count) for i in range(count)]
    down = [(target, source) for source, target in up]
    buffer = place(buffer, shard, me)
    right = left = shard
    for step in range(1, count // 2 + 1):
        right = lax.ppermute(right, axis, up)
        buffer = place(buffer, right, (me - step) % count)
        if step < count - step:
            left = lax.ppermute(left, axis, down)
            buffer = place(buffer, left, (me + step) % count)
    return buffer


def gather_weights(expert_weights):
    ny, nz = lax.axis_size("y"), lax.axis_size("z")
    rows, width = expert_weights.shape[1], expert_weights.shape[2]
    part = width // (3 * ny)
    sliced = expert_weights[0].reshape(rows, 3, ny, part).transpose(2, 0, 1, 3)
    sliced = sliced.reshape(ny, rows, 3 * part)
    mine = lax.all_to_all(sliced, "y", 0, 0, tiled=True)

    def place(buffer, shard, z):
        return lax.dynamic_update_slice(buffer, shard[:, None], (0, z, 0, 0))

    buffer = ring_gather(mine, "z", place, jnp.zeros((ny, nz, rows, 3 * part), BF))
    return buffer.reshape(ny * nz * rows, 3 * part)


def scatter_weight_grad(term):
    ny, nz = lax.axis_size("y"), lax.axis_size("z")
    rows = term.shape[0] // (ny * nz)
    part = term.shape[1] // 3
    blocks = term.reshape(ny, nz, rows, 3 * part).transpose(1, 0, 2, 3)
    mine = lax.psum_scatter(blocks.reshape(nz * ny * rows, 3 * part), "z", scatter_dimension=0, tiled=True)
    back = lax.all_to_all(mine.reshape(ny, rows, 3 * part), "y", 0, 0, tiled=True)
    back = back.reshape(ny, rows, 3, part).transpose(1, 2, 0, 3)
    return back.reshape(1, rows, 3 * ny * part)


def slots_of(chosen):
    frames = chosen.shape[-1]
    before = (jnp.arange(frames)[:, None] < jnp.arange(frames)[None, :]).astype(BF)
    ranks = dot(chosen.astype(BF), before, ((chosen.ndim - 1,), (0,))).astype(jnp.int32)
    return chosen[..., None, :] & (ranks[..., None, :] == jnp.arange(SLOTS)[:, None])


def with_halo(block, width):
    axes = ("y", "z", "x", "c")
    count = 1
    for axis in axes:
        count *= lax.axis_size(axis)
    forward = [(i, i + 1) for i in range(count - 1)]
    backward = [(target, source) for source, target in forward]
    low = lax.ppermute(block[block.shape[0] - width :], axes, forward)
    high = lax.ppermute(block[:width], axes, backward)
    return jnp.concatenate([low, block, high], axis=0)


def rows_kernel(info, x_ref, w_ref, wt_ref, *refs):
    low_ref, high_ref, u_ref, q_ref, pre_ref, h_ref = refs[-6:]
    steps, rows, wide = x_ref.shape
    frames, width = rows - META, wide // 2
    part, half = h_ref.shape[1], low_ref.shape[1]
    name = info[0].astype(F32)
    earlier = lax.broadcasted_iota(jnp.int32, (frames, frames), 0)
    before = (earlier < lax.broadcasted_iota(jnp.int32, (frames, frames), 1)).astype(F32).astype(BF)
    slot = lax.broadcasted_iota(jnp.int32, (SLOTS, frames), 0).astype(F32)
    for j in range(steps):
        meta = x_ref[j, frames:rows, :frames].astype(F32)
        named = (meta == name).astype(F32)
        chosen = named[0:1] + named[1:2]
        ranks = dot(jnp.broadcast_to(chosen, (8, frames)).astype(BF), before, ((1,), (0,)))[0:1]
        gate = named[0:1] * meta[2:3] + named[1:2] * meta[3:4]
        here = jnp.where((slot == ranks) & (chosen > 0.0), 1.0, 0.0)
        place = pl.ds(j * SLOTS, SLOTS)
        u = dot(here.astype(BF), x_ref[j, :frames, :width], ((1,), (0,)))
        u_ref[place] = u.astype(BF)
        q = dot((here * gate).astype(BF), x_ref[j, :frames, width:], ((1,), (0,)))
        q_ref[place] = q.astype(BF)
    projected = dot(u_ref[...], w_ref[:, : 2 * part], ((1,), (0,)))
    hidden_grad = dot(q_ref[...], w_ref[:, 2 * part :], ((1,), (0,)))
    gate_in, up_in = projected[:, :part], projected[:, part:]
    sigmoid = jax.nn.sigmoid(gate_in)
    activated = gate_in * sigmoid
    hidden = (activated * up_in).astype(BF)
    h_ref[...] = hidden
    pre_ref[:, :part] = (hidden_grad * up_in * (sigmoid * (1.0 + gate_in * (1.0 - sigmoid)))).astype(BF)
    pre_ref[:, part:] = (hidden_grad * activated).astype(BF)
    gate_part = jnp.sum(hidden.astype(F32) * hidden_grad, axis=1, keepdims=True)
    row_grad = dot(pre_ref[...], wt_ref[...], ((1,), (0,))).astype(BF)
    low_ref[...] = row_grad[:, :half]
    high_ref[...] = row_grad[:, half:]
    row = lax.broadcasted_iota(jnp.int32, (SLOTS, 128), 0)
    lane = lax.broadcasted_iota(jnp.int32, (SLOTS, 128), 1)
    for j in range(steps):
        place = pl.ds(j * SLOTS, SLOTS)
        diagonal = jnp.where(row == lane, gate_part[j * SLOTS : (j + 1) * SLOTS], 0.0)
        line = jnp.sum(diagonal, axis=0, keepdims=True)
        low_ref[place, :128] = jnp.where(row == SPARE, line, low_ref[place, :128].astype(F32)).astype(BF)


def expert_rows(expert, targets, turn, everything, weights, turned, kept):
    blocks, rows, wide = everything.shape
    groups = lax.axis_size("y")
    width, part = wide // 2, weights.shape[1] // 3
    rows_step = STEP * SLOTS
    steps = blocks // (groups * STEP)
    count = len(targets) * steps
    total, mine = blocks * SLOTS, len(targets) * blocks * SLOTS // groups
    firsts = [target * steps + step for target in targets for step in range(steps)]
    info = jnp.stack([expert] + firsts).astype(jnp.int32)

    def rowwise(columns, first):
        return pl.BlockSpec((rows_step, columns), lambda i, info: (i + first, 0))

    whole = pl.BlockSpec(memory_space=pltpu.VMEM)
    widths = (width, width, 2 * part, part)
    shapes = [jax.ShapeDtypeStruct((mine, width // 2), BF)] * 2
    shapes += [jax.ShapeDtypeStruct((total, columns), BF) for columns in widths]
    low, high, *kept = pl.pallas_call(
        rows_kernel,
        grid_spec=pltpu.PrefetchScalarGridSpec(
            num_scalar_prefetch=1,
            grid=(count,),
            in_specs=[
                pl.BlockSpec((STEP, rows, wide), lambda i, info: (info[1 + i], 0, 0)),
                whole,
                whole,
            ]
            + [pl.BlockSpec(memory_space=pl.ANY) for _ in kept],
            out_specs=[rowwise(width // 2, 0)] * 2 + [rowwise(columns, turn * steps) for columns in widths],
        ),
        out_shape=shapes,
        input_output_aliases={4 + k: 2 + k for k in range(len(kept))},
        compiler_params=pltpu.CompilerParams(vmem_limit_bytes=52 * 1024 * 1024),
    )(info, everything, weights, turned, *kept)
    return low, high, kept


def add(*parts):
    return sum(part.astype(F32) for part in parts)


def rows_backward(expert, everything, weights):
    ny = lax.axis_size("y")
    me = lax.axis_index("y")
    up = [(i, (i + 1) % ny) for i in range(ny)]
    down = [(target, source) for source, target in up]
    turned = weights[:, : 2 * (weights.shape[1] // 3)].T

    def send(rows, way):
        return lax.ppermute(rows, "y", way)

    def run(offsets, turn, kept):
        return expert_rows(expert, [(me + offset) % ny for offset in offsets], turn, everything, weights, turned, kept)

    far_low, far_high, kept = run([2], 0, [])
    low_via, high_via = send(far_low, up), send(far_high, down)
    near_low, near_high, kept = run([1, ny - 1], 1, kept)
    low_via, high_via, kept = lax.optimization_barrier((low_via, high_via, kept))
    rows = far_low.shape[0]
    below_high, above_low = send(near_high[:rows], up), send(near_low[rows:], down)
    below_low = send(add(near_low[:rows], low_via).astype(BF), up)
    above_high = send(add(near_high[rows:], high_via).astype(BF), down)
    own_low, own_high, kept = run([0], 3, kept)
    rows_in, rows_q, pre_grads, hidden = kept
    first = dot(rows_in, pre_grads, ((0,), (0,))).astype(BF)
    rows_q, below_high, above_low, first = lax.optimization_barrier((rows_q, below_high, above_low, first))
    second = dot(rows_q, hidden, ((0,), (0,))).astype(BF)
    term = jnp.concatenate([first, second], axis=1)
    low = add(own_low, below_low, above_low).astype(BF)
    high = add(own_high, below_high, above_high).astype(BF)
    return low, high, term


def local(block_in, out_grad, gate_values, expert_ids, conv_kernel, expert_weights):
    frames, width = block_in.shape
    ny, experts = lax.axis_size("y"), lax.axis_size("x") * lax.axis_size("c")
    group = ("y", "x", "c")
    expert = lax.axis_index("x") * lax.axis_size("c") + lax.axis_index("c")

    meta = jnp.concatenate([expert_ids.astype(BF).T, gate_values.T], axis=0)
    meta = jnp.pad(meta, ((0, META - 4), (0, 2 * width - frames)))
    packed = jnp.concatenate([jnp.concatenate([block_in, out_grad], axis=1), meta], axis=0)
    everything = lax.all_gather(packed, group, axis=0, tiled=False)
    weights = gather_weights(expert_weights)
    low, high, term = rows_backward(expert, everything, weights)
    weight_grad = scatter_weight_grad(term)

    def give_back(rows):
        return lax.all_to_all(rows.reshape(experts, SLOTS, width // 2), ("x", "c"), 0, 0, tiled=True)

    back_low, back_high = give_back(low), give_back(high)
    returned = jnp.concatenate([back_low, back_high], axis=2)

    own_ids = expert_ids.T[None] == jnp.arange(experts, dtype=jnp.int32)[:, None, None]
    own = slots_of(own_ids[:, 0] | own_ids[:, 1])
    own_placing = own.astype(BF)
    flat = own_placing.reshape(experts * SLOTS, frames)
    frame_grad = out_grad.astype(F32) + dot(
        flat, returned.reshape(experts * SLOTS, width), ((0,), (0,))
    )
    gate_sums = jnp.einsum(
        "es,est,ekt->tk",
        returned[:, SPARE, :SLOTS].astype(F32),
        own.astype(F32),
        own_ids.astype(F32),
        precision="highest",
    )
    gate_out = (gate_sums / gate_values.astype(F32)).astype(BF)

    taps = conv_kernel.shape[0]
    half = (taps - 1) // 2
    kernel_rows = conv_kernel.astype(F32)
    padded = with_halo(frame_grad.astype(BF), half).astype(F32)
    conv_part = jnp.zeros((frames, width), F32)
    for offset in range(taps):
        conv_part = conv_part + kernel_rows[offset] * padded[2 * half - offset : 2 * half - offset + frames]
    input_grad = (frame_grad + conv_part).astype(BF)
    return input_grad, weight_grad, gate_out


def solution(mesh):
    grid = Mesh(mesh.devices.reshape(4, 8, 4, 2), ("y", "z", "x", "c"))
    frames = P(("y", "z", "x", "c"), None)
    weights = P(("x", "c"), ("y", "z"), None)
    in_specs = (frames, frames, frames, frames, P(), weights)
    out_specs = (frames, weights, frames)
    return jax.shard_map(local, mesh=grid, in_specs=in_specs, out_specs=out_specs, check_vma=False)
```

```python
import functools

import jax
import jax.numpy as jnp
from jax import lax
from jax.experimental import pallas as pl
from jax.experimental.pallas import tpu as pltpu
from jax.sharding import Mesh, PartitionSpec as P

BF = jnp.bfloat16
F32 = jnp.float32
SLOTS = 64
SPARE = 60
META = 8
STEP = 4
CHUNK = 256


def dot(a, b, contract, batch=((), ())):
    return lax.dot_general(a, b, (contract, batch), preferred_element_type=F32)


def ring_gather(shard, axis, place, buffer):
    count = lax.axis_size(axis)
    me = lax.axis_index(axis)
    up = [(i, (i + 1) % count) for i in range(count)]
    down = [(target, source) for source, target in up]
    buffer = place(buffer, shard, me)
    right = left = shard
    for step in range(1, count // 2 + 1):
        right = lax.ppermute(right, axis, up)
        buffer = place(buffer, right, (me - step) % count)
        if step < count - step:
            left = lax.ppermute(left, axis, down)
            buffer = place(buffer, left, (me + step) % count)
    return buffer


def gather_weights(expert_weights):
    ny, nz = lax.axis_size("y"), lax.axis_size("z")
    rows, width = expert_weights.shape[1], expert_weights.shape[2]
    part = width // (3 * ny)
    sliced = expert_weights[0].reshape(rows, 3, ny, part).transpose(2, 0, 1, 3)
    sliced = sliced.reshape(ny, rows, 3 * part)
    mine = lax.all_to_all(sliced, "y", 0, 0, tiled=True)

    def place(buffer, shard, z):
        return lax.dynamic_update_slice(buffer, shard[:, None], (0, z, 0, 0))

    buffer = ring_gather(mine, "z", place, jnp.zeros((ny, nz, rows, 3 * part), BF))
    return buffer.reshape(ny * nz * rows, 3 * part)


def scatter_weight_grad(term):
    ny, nz = lax.axis_size("y"), lax.axis_size("z")
    rows = term.shape[0] // (ny * nz)
    part = term.shape[1] // 3
    blocks = term.reshape(ny, nz, rows, 3 * part).transpose(1, 0, 2, 3)
    mine = lax.psum_scatter(blocks.reshape(nz * ny * rows, 3 * part), "z", scatter_dimension=0, tiled=True)
    back = lax.all_to_all(mine.reshape(ny, rows, 3 * part), "y", 0, 0, tiled=True)
    back = back.reshape(ny, rows, 3, part).transpose(1, 2, 0, 3)
    return back.reshape(1, rows, 3 * ny * part)


def slots_of(chosen):
    frames = chosen.shape[-1]
    before = (jnp.arange(frames)[:, None] < jnp.arange(frames)[None, :]).astype(BF)
    ranks = dot(chosen.astype(BF), before, ((chosen.ndim - 1,), (0,))).astype(jnp.int32)
    return chosen[..., None, :] & (ranks[..., None, :] == jnp.arange(SLOTS)[:, None])


def with_halo(block, width):
    axes = ("y", "z", "x", "c")
    count = 1
    for axis in axes:
        count *= lax.axis_size(axis)
    forward = [(i, i + 1) for i in range(count - 1)]
    backward = [(target, source) for source, target in forward]
    low = lax.ppermute(block[block.shape[0] - width :], axes, forward)
    high = lax.ppermute(block[:width], axes, backward)
    return jnp.concatenate([low, block, high], axis=0)


def route_kernel(scaled, x_ref, out_ref):
    rows, width = x_ref.shape[1:]
    frames, experts = rows - META, out_ref.shape[0]
    meta = x_ref[0, frames:rows, :frames].astype(F32)
    names = lax.broadcasted_iota(jnp.int32, (experts, frames), 0).astype(F32)
    first, second = (names == meta[0:1]).astype(F32), (names == meta[1:2]).astype(F32)
    chosen = first + second
    gate = first * meta[2:3] + second * meta[3:4] if scaled else chosen
    earlier = lax.broadcasted_iota(jnp.int32, (frames, frames), 0)
    before = (earlier < lax.broadcasted_iota(jnp.int32, (frames, frames), 1)).astype(F32).astype(BF)
    ranks = dot(chosen.astype(BF), before, ((1,), (0,)))
    slot = lax.broadcasted_iota(jnp.int32, (SLOTS, frames), 0).astype(F32)
    for e in range(experts):
        here = (slot == ranks[e : e + 1]) & (chosen[e : e + 1] > 0.0)
        placing = jnp.where(here, gate[e : e + 1], 0.0).astype(BF)
        out_ref[e, 0] = dot(placing, x_ref[0, :frames], ((1,), (0,))).astype(BF)


def route(packed, experts, scaled):
    groups, rows, width = packed.shape
    return pl.pallas_call(
        functools.partial(route_kernel, scaled),
        grid=(groups,),
        in_specs=[pl.BlockSpec((1, rows, width), lambda i: (i, 0, 0))],
        out_specs=pl.BlockSpec((experts, 1, SLOTS, width), lambda i: (0, i, 0, 0)),
        out_shape=jax.ShapeDtypeStruct((experts, groups, SLOTS, width), BF),
        compiler_params=pltpu.CompilerParams(vmem_limit_bytes=32 * 1024 * 1024),
    )(packed)


def rows_kernel(info, u_ref, q_ref, w_ref, *refs):
    low_ref, high_ref, pre_ref, h_ref = refs[-4:]
    steps, width, part, half = u_ref.shape[1], u_ref.shape[3], h_ref.shape[3], low_ref.shape[1]
    count = steps * SLOTS
    u, q = u_ref[0].reshape(count, width), q_ref[:, 0].reshape(count, width)
    gate_part = 0.0
    for c in range(0, part, CHUNK):
        gate_in = dot(u, w_ref[:, c : c + CHUNK], ((1,), (0,)))
        up_in = dot(u, w_ref[:, part + c : part + c + CHUNK], ((1,), (0,)))
        hidden_grad = dot(q, w_ref[:, 2 * part + c : 2 * part + c + CHUNK], ((1,), (0,)))
        sigmoid = jax.nn.sigmoid(gate_in)
        activated = gate_in * sigmoid
        hidden = (activated * up_in).astype(BF)
        h_ref[:, 0, :, c : c + CHUNK] = hidden.reshape(steps, SLOTS, CHUNK)
        slope = sigmoid * (1.0 + gate_in * (1.0 - sigmoid))
        pre_ref[:, c : c + CHUNK] = (hidden_grad * up_in * slope).astype(BF)
        pre_ref[:, part + c : part + c + CHUNK] = (hidden_grad * activated).astype(BF)
        gate_part += jnp.sum(hidden.astype(F32) * hidden_grad, axis=1, keepdims=True)
    row_grad = dot(pre_ref[...], w_ref[:, : 2 * part], ((1,), (1,)))
    high_ref[...] = row_grad[:, half:].astype(BF)
    low_ref[...] = row_grad[:, :half].astype(BF)
    row = lax.broadcasted_iota(jnp.int32, (SLOTS, 128), 0)
    lane = lax.broadcasted_iota(jnp.int32, (SLOTS, 128), 1)
    for j in range(steps):
        place = pl.ds(j * SLOTS, SLOTS)
        diagonal = jnp.where(row == lane, gate_part[j * SLOTS : (j + 1) * SLOTS], 0.0)
        line = jnp.sum(diagonal, axis=0, keepdims=True)
        low_ref[place, :128] = jnp.where(row == SPARE, line, low_ref[place, :128].astype(F32)).astype(BF)


def expert_rows(targets, rows_in, rows_q, weights, kept):
    groups, sources, _, width = rows_in.shape
    part = weights.shape[1] // 3
    steps = sources // STEP
    mine = len(targets) * sources * SLOTS
    info = jnp.stack(targets).astype(jnp.int32)
    by_group = lambda i, info: (info[i // steps], i % steps, 0, 0)
    by_source = lambda i, info: (i % steps, info[i // steps], 0, 0)
    in_order = lambda i, info: (i, 0)
    low, high, *kept = pl.pallas_call(
        rows_kernel,
        grid_spec=pltpu.PrefetchScalarGridSpec(
            num_scalar_prefetch=1,
            grid=(len(targets) * steps,),
            in_specs=[
                pl.BlockSpec((1, STEP, SLOTS, width), by_group),
                pl.BlockSpec((STEP, 1, SLOTS, width), by_source),
                pl.BlockSpec(weights.shape, lambda i, info: (0, 0)),
            ]
            + [pl.BlockSpec(memory_space=pl.ANY) for _ in kept],
            out_specs=[
                pl.BlockSpec((STEP * SLOTS, width // 2), in_order),
                pl.BlockSpec((STEP * SLOTS, width // 2), in_order),
                pl.BlockSpec((STEP * SLOTS, 2 * part), lambda i, info: (info[i // steps] * steps + i % steps, 0)),
                pl.BlockSpec((STEP, 1, SLOTS, part), by_source),
            ],
        ),
        out_shape=[
            jax.ShapeDtypeStruct((mine, width // 2), BF),
            jax.ShapeDtypeStruct((mine, width // 2), BF),
            jax.ShapeDtypeStruct((groups * sources * SLOTS, 2 * part), BF),
            jax.ShapeDtypeStruct((sources, groups, SLOTS, part), BF),
        ],
        input_output_aliases={4 + k: 2 + k for k in range(len(kept))},
        compiler_params=pltpu.CompilerParams(vmem_limit_bytes=52 * 1024 * 1024),
    )(info, rows_in, rows_q, weights, *kept)
    return low, high, kept


def add(*parts):
    return sum(part.astype(F32) for part in parts)


def rows_backward(rows_in, rows_q, weights):
    ny = lax.axis_size("y")
    me = lax.axis_index("y")
    width = rows_in.shape[3]
    up = [(i, (i + 1) % ny) for i in range(ny)]
    down = [(target, source) for source, target in up]

    def send(rows, way):
        return lax.ppermute(rows, "y", way)

    def run(offsets, kept):
        return expert_rows([(me + offset) % ny for offset in offsets], rows_in, rows_q, weights, kept)

    far_low, far_high, kept = run([2], [])
    low_via, high_via = send(far_low, up), send(far_high, down)
    near_low, near_high, kept = run([1, ny - 1], kept)
    low_via, high_via, kept = lax.optimization_barrier((low_via, high_via, kept))
    rows = far_low.shape[0]
    below_high, above_low = send(near_high[:rows], up), send(near_low[rows:], down)
    below_low = send(add(near_low[:rows], low_via).astype(BF), up)
    above_high = send(add(near_high[rows:], high_via).astype(BF), down)
    own_low, own_high, kept = run([0], kept)
    pre_grads, hidden = kept
    first = dot(rows_in.reshape(-1, width), pre_grads, ((0,), (0,))).astype(BF)
    rows_q, below_high, above_low, first = lax.optimization_barrier((rows_q, below_high, above_low, first))
    second = dot(rows_q.reshape(-1, width), hidden.reshape(-1, hidden.shape[3]), ((0,), (0,))).astype(BF)
    term = jnp.concatenate([first, second], axis=1)
    low = add(own_low, below_low, above_low).astype(BF)
    high = add(own_high, below_high, above_high).astype(BF)
    return low, high, term


def local(block_in, out_grad, gate_values, expert_ids, conv_kernel, expert_weights):
    frames, width = block_in.shape
    ny, experts = lax.axis_size("y"), lax.axis_size("x") * lax.axis_size("c")
    by_expert = ("x", "c")

    meta = jnp.concatenate([expert_ids.astype(BF).T, gate_values.T], axis=0)
    meta = jnp.pad(meta, ((0, META - 4), (0, width - frames)))
    all_grad = lax.all_gather(jnp.concatenate([out_grad, meta], axis=0), "y", axis=0, tiled=False)
    sent_in = route(jnp.concatenate([block_in, meta], axis=0)[None], experts, False)
    mine_in = lax.all_to_all(sent_in, by_expert, 0, 0, tiled=True)
    rows_in = lax.all_gather(mine_in[:, 0], "y", axis=0, tiled=False)
    sent_q = route(all_grad, experts, True)
    rows_q = lax.all_to_all(sent_q, by_expert, 0, 0, tiled=True)
    weights = gather_weights(expert_weights)
    low, high, term = rows_backward(rows_in, rows_q, weights)
    weight_grad = scatter_weight_grad(term)
    summed = jnp.concatenate([low, high], axis=1).reshape(experts, SLOTS, width)
    returned = lax.all_to_all(summed, by_expert, 0, 0, tiled=True)

    own_ids = expert_ids.T[None] == jnp.arange(experts, dtype=jnp.int32)[:, None, None]
    own = slots_of(own_ids[:, 0] | own_ids[:, 1])
    own_placing = own.astype(BF)
    flat = own_placing.reshape(experts * SLOTS, frames)
    frame_grad = out_grad.astype(F32) + dot(
        flat, returned.reshape(experts * SLOTS, width), ((0,), (0,))
    )
    gate_sums = jnp.einsum(
        "es,est,ekt->tk",
        returned[:, SPARE, :SLOTS].astype(F32),
        own.astype(F32),
        own_ids.astype(F32),
        precision="highest",
    )
    gate_out = (gate_sums / gate_values.astype(F32)).astype(BF)

    taps = conv_kernel.shape[0]
    half = (taps - 1) // 2
    kernel_rows = conv_kernel.astype(F32)
    padded = with_halo(frame_grad.astype(BF), half).astype(F32)
    conv_part = jnp.zeros((frames, width), F32)
    for offset in range(taps):
        conv_part = conv_part + kernel_rows[offset] * padded[2 * half - offset : 2 * half - offset + frames]
    input_grad = (frame_grad + conv_part).astype(BF)
    return input_grad, weight_grad, gate_out


def solution(mesh):
    grid = Mesh(mesh.devices.reshape(4, 8, 4, 2), ("y", "z", "x", "c"))
    frames = P(("y", "z", "x", "c"), None)
    weights = P(("x", "c"), ("y", "z"), None)
    in_specs = (frames, frames, frames, frames, P(), weights)
    out_specs = (frames, weights, frames)
    return jax.shard_map(local, mesh=grid, in_specs=in_specs, out_specs=out_specs, check_vma=False)
```

```python
import functools

import jax
import jax.numpy as jnp
from jax import lax
from jax.experimental import pallas as pl
from jax.experimental.pallas import tpu as pltpu
from jax.sharding import Mesh, PartitionSpec as P

BF = jnp.bfloat16
F32 = jnp.float32
SLOTS = 64
SPARE = 60
META = 8
STEP = 4
CHUNK = 256


def dot(a, b, contract, batch=((), ())):
    return lax.dot_general(a, b, (contract, batch), preferred_element_type=F32)


def ring_ways(axis):
    count = lax.axis_size(axis)
    up = [(i, (i + 1) % count) for i in range(count)]
    return up, [(target, source) for source, target in up]


def ring_step(right, left, axis):
    up, down = ring_ways(axis)
    return lax.ppermute(right, axis, up), lax.ppermute(left, axis, down)


def own_columns(expert_weights):
    ny = lax.axis_size("y")
    rows, width = expert_weights.shape[1], expert_weights.shape[2]
    part = width // (3 * ny)
    sliced = expert_weights[0].reshape(rows, 3, ny, part).transpose(2, 0, 1, 3)
    return lax.all_to_all(sliced.reshape(ny, rows, 3 * part), "y", 0, 0, tiled=True)


def gather_weights(mine, after):
    ny, rows, width = mine.shape
    nz = lax.axis_size("z")
    me = lax.axis_index("z")

    def place(buffer, shard, z):
        return lax.dynamic_update_slice(buffer, shard[:, None], (0, z % nz, 0, 0))

    buffer = place(jnp.zeros((ny, nz, rows, width), BF), mine, me)
    mine, after = lax.optimization_barrier((mine, after))
    right = left = mine
    for step in range(1, nz // 2):
        right, left = ring_step(right, left, "z")
        buffer = place(place(buffer, right, me - step), left, me + step)
    right = lax.ppermute(right, "z", ring_ways("z")[0])
    buffer = place(buffer, right, me - nz // 2)
    return buffer.reshape(ny * nz * rows, width)


def scatter_weight_grad(term):
    ny, nz = lax.axis_size("y"), lax.axis_size("z")
    rows, part = term.shape[2], term.shape[3] // 3
    mine = lax.psum_scatter(term.reshape(nz * ny * rows, 3 * part), "z", scatter_dimension=0, tiled=True)
    back = lax.all_to_all(mine.reshape(ny, rows, 3 * part), "y", 0, 0, tiled=True)
    back = back.reshape(ny, rows, 3, part).transpose(1, 2, 0, 3)
    return back.reshape(1, rows, 3 * ny * part)


def slots_of(chosen):
    frames = chosen.shape[-1]
    before = (jnp.arange(frames)[:, None] < jnp.arange(frames)[None, :]).astype(BF)
    ranks = dot(chosen.astype(BF), before, ((chosen.ndim - 1,), (0,))).astype(jnp.int32)
    return chosen[..., None, :] & (ranks[..., None, :] == jnp.arange(SLOTS)[:, None])


def with_halo(block, width):
    axes = ("y", "z", "x", "c")
    count = 1
    for axis in axes:
        count *= lax.axis_size(axis)
    forward = [(i, i + 1) for i in range(count - 1)]
    backward = [(target, source) for source, target in forward]
    low = lax.ppermute(block[block.shape[0] - width :], axes, forward)
    high = lax.ppermute(block[:width], axes, backward)
    return jnp.concatenate([low, block, high], axis=0)


def route_kernel(scaled, x_ref, out_ref):
    rows, width = x_ref.shape[1:]
    frames, experts = rows - META, out_ref.shape[0]
    meta = x_ref[0, frames:rows, :frames].astype(F32)
    names = lax.broadcasted_iota(jnp.int32, (experts, frames), 0).astype(F32)
    first, second = (names == meta[0:1]).astype(F32), (names == meta[1:2]).astype(F32)
    chosen = first + second
    gate = first * meta[2:3] + second * meta[3:4] if scaled else chosen
    earlier = lax.broadcasted_iota(jnp.int32, (frames, frames), 0)
    before = (earlier < lax.broadcasted_iota(jnp.int32, (frames, frames), 1)).astype(F32).astype(BF)
    ranks = dot(chosen.astype(BF), before, ((1,), (0,)))
    slot = lax.broadcasted_iota(jnp.int32, (SLOTS, frames), 0).astype(F32)
    for e in range(experts):
        here = (slot == ranks[e : e + 1]) & (chosen[e : e + 1] > 0.0)
        placing = jnp.where(here, gate[e : e + 1], 0.0).astype(BF)
        out_ref[e, 0] = dot(placing, x_ref[0, :frames], ((1,), (0,))).astype(BF)


def route(packed, experts, scaled):
    groups, rows, width = packed.shape
    return pl.pallas_call(
        functools.partial(route_kernel, scaled),
        grid=(groups,),
        in_specs=[pl.BlockSpec((1, rows, width), lambda i: (i, 0, 0))],
        out_specs=pl.BlockSpec((experts, 1, SLOTS, width), lambda i: (0, i, 0, 0)),
        out_shape=jax.ShapeDtypeStruct((experts, groups, SLOTS, width), BF),
        compiler_params=pltpu.CompilerParams(vmem_limit_bytes=32 * 1024 * 1024),
    )(packed)


def rows_of(u, q, w_ref, low_ref, high_ref, pre_ref, h_ref):
    steps, part, half = h_ref.shape[0], h_ref.shape[3], low_ref.shape[1]
    gate_part = 0.0
    for c in range(0, part, CHUNK):
        gate_in = dot(u, w_ref[:, c : c + CHUNK], ((1,), (0,)))
        up_in = dot(u, w_ref[:, part + c : part + c + CHUNK], ((1,), (0,)))
        hidden_grad = dot(q, w_ref[:, 2 * part + c : 2 * part + c + CHUNK], ((1,), (0,)))
        sigmoid = jax.nn.sigmoid(gate_in)
        activated = gate_in * sigmoid
        hidden = (activated * up_in).astype(BF)
        h_ref[:, 0, :, c : c + CHUNK] = hidden.reshape(steps, SLOTS, CHUNK)
        slope = sigmoid * (1.0 + gate_in * (1.0 - sigmoid))
        pre_ref[:, c : c + CHUNK] = (hidden_grad * up_in * slope).astype(BF)
        pre_ref[:, part + c : part + c + CHUNK] = (hidden_grad * activated).astype(BF)
        gate_part += jnp.sum(hidden.astype(F32) * hidden_grad, axis=1, keepdims=True)
    row_grad = dot(pre_ref[...], w_ref[:, : 2 * part], ((1,), (1,)))
    high_ref[...] = row_grad[:, half:].astype(BF)
    low_ref[...] = row_grad[:, :half].astype(BF)
    row = lax.broadcasted_iota(jnp.int32, (SLOTS, 128), 0)
    lane = lax.broadcasted_iota(jnp.int32, (SLOTS, 128), 1)
    for j in range(steps):
        place = pl.ds(j * SLOTS, SLOTS)
        diagonal = jnp.where(row == lane, gate_part[j * SLOTS : (j + 1) * SLOTS], 0.0)
        line = jnp.sum(diagonal, axis=0, keepdims=True)
        low_ref[place, :128] = jnp.where(row == SPARE, line, low_ref[place, :128].astype(F32)).astype(BF)


def rows_kernel(info, u_ref, q_ref, w_ref, *refs):
    count, width = u_ref.shape[1] * SLOTS, u_ref.shape[3]
    rows_of(u_ref[0].reshape(count, width), q_ref[:, 0].reshape(count, width), w_ref, *refs[-4:])


def last_kernel(info, u_ref, q_ref, w_ref, pre_ref, h_ref, low_ref, high_ref, term_ref, own_pre, own_h, total):
    step, last = pl.program_id(0), pl.num_programs(0) - 1
    count, width = u_ref.shape[1] * SLOTS, u_ref.shape[3]
    part, wide = h_ref.shape[3], pre_ref.shape[1]
    groups, each = term_ref.shape[1], term_ref.shape[0] * term_ref.shape[2]
    u, q = u_ref[0].reshape(count, width), q_ref[:, 0].reshape(count, width)

    @pl.when(step == 0)
    def _():
        rows_of(u, q, w_ref, low_ref, high_ref, own_pre, own_h)
        total[:, :wide] = dot(u, own_pre[...], ((0,), (0,)))
        total[:, wide:] = dot(q, own_h[:, 0].reshape(count, part), ((0,), (0,)))

    @pl.when(step > 0)
    def _():
        total[:, :wide] += dot(u, pre_ref[...], ((0,), (0,)))
        total[:, wide:] += dot(q, h_ref[:, 0].reshape(count, part), ((0,), (0,)))

    @pl.when(step == last)
    def _():
        for g in range(groups):
            block = total[g * each : (g + 1) * each].astype(BF)
            term_ref[:, g] = block.reshape(term_ref.shape[0], term_ref.shape[2], term_ref.shape[3])


def last_rows(targets, rows_in, rows_q, weights, pre_grads, hidden):
    groups, sources, _, width = rows_in.shape
    nz = lax.axis_size("z")
    part = weights.shape[1] // 3
    mine = sources * SLOTS
    each = width // (groups * nz)
    info = jnp.stack(targets).astype(jnp.int32)
    fixed = lambda i, info: (0, 0)
    return pl.pallas_call(
        last_kernel,
        grid_spec=pltpu.PrefetchScalarGridSpec(
            num_scalar_prefetch=1,
            grid=(groups,),
            in_specs=[
                pl.BlockSpec((1, sources, SLOTS, width), lambda i, info: (info[i], 0, 0, 0)),
                pl.BlockSpec((sources, 1, SLOTS, width), lambda i, info: (0, info[i], 0, 0)),
                pl.BlockSpec(weights.shape, fixed),
                pl.BlockSpec((mine, 2 * part), lambda i, info: (info[jnp.maximum(i, 1)], 0)),
                pl.BlockSpec((sources, 1, SLOTS, part), lambda i, info: (0, info[jnp.maximum(i, 1)], 0, 0)),
            ],
            out_specs=[
                pl.BlockSpec((mine, width // 2), fixed),
                pl.BlockSpec((mine, width // 2), fixed),
                pl.BlockSpec((nz, groups, each, 3 * part), lambda i, info: (0, 0, 0, 0)),
            ],
            scratch_shapes=[
                pltpu.VMEM((mine, 2 * part), BF),
                pltpu.VMEM((sources, 1, SLOTS, part), BF),
                pltpu.VMEM((width, 3 * part), F32),
            ],
        ),
        out_shape=[
            jax.ShapeDtypeStruct((mine, width // 2), BF),
            jax.ShapeDtypeStruct((mine, width // 2), BF),
            jax.ShapeDtypeStruct((nz, groups, each, 3 * part), BF),
        ],
        compiler_params=pltpu.CompilerParams(vmem_limit_bytes=56 * 1024 * 1024),
    )(info, rows_in, rows_q, weights, pre_grads, hidden)


def expert_rows(targets, rows_in, rows_q, weights, kept):
    groups, sources, _, width = rows_in.shape
    part = weights.shape[1] // 3
    steps = sources // STEP
    mine = len(targets) * sources * SLOTS
    info = jnp.stack(targets).astype(jnp.int32)
    by_group = lambda i, info: (info[i // steps], i % steps, 0, 0)
    by_source = lambda i, info: (i % steps, info[i // steps], 0, 0)
    in_order = lambda i, info: (i, 0)
    low, high, *kept = pl.pallas_call(
        rows_kernel,
        grid_spec=pltpu.PrefetchScalarGridSpec(
            num_scalar_prefetch=1,
            grid=(len(targets) * steps,),
            in_specs=[
                pl.BlockSpec((1, STEP, SLOTS, width), by_group),
                pl.BlockSpec((STEP, 1, SLOTS, width), by_source),
                pl.BlockSpec(weights.shape, lambda i, info: (0, 0)),
            ]
            + [pl.BlockSpec(memory_space=pl.ANY) for _ in kept],
            out_specs=[
                pl.BlockSpec((STEP * SLOTS, width // 2), in_order),
                pl.BlockSpec((STEP * SLOTS, width // 2), in_order),
                pl.BlockSpec((STEP * SLOTS, 2 * part), lambda i, info: (info[i // steps] * steps + i % steps, 0)),
                pl.BlockSpec((STEP, 1, SLOTS, part), by_source),
            ],
        ),
        out_shape=[
            jax.ShapeDtypeStruct((mine, width // 2), BF),
            jax.ShapeDtypeStruct((mine, width // 2), BF),
            jax.ShapeDtypeStruct((groups * sources * SLOTS, 2 * part), BF),
            jax.ShapeDtypeStruct((sources, groups, SLOTS, part), BF),
        ],
        input_output_aliases={4 + k: 2 + k for k in range(len(kept))},
        compiler_params=pltpu.CompilerParams(vmem_limit_bytes=52 * 1024 * 1024),
    )(info, rows_in, rows_q, weights, *kept)
    return low, high, kept


def add(*parts):
    return sum(part.astype(F32) for part in parts)


def rows_backward(rows_in, rows_q, weights):
    ny = lax.axis_size("y")
    me = lax.axis_index("y")
    up = [(i, (i + 1) % ny) for i in range(ny)]
    down = [(target, source) for source, target in up]

    def send(rows, way):
        return lax.ppermute(rows, "y", way)

    def run(offsets, kept):
        return expert_rows([(me + offset) % ny for offset in offsets], rows_in, rows_q, weights, kept)

    far_low, far_high, kept = run([2], [])
    low_via, high_via = send(far_low, up), send(far_high, down)
    near_low, near_high, kept = run([1, ny - 1], kept)
    low_via, high_via, kept = lax.optimization_barrier((low_via, high_via, kept))
    rows = far_low.shape[0]
    below_high, above_low = send(near_high[:rows], up), send(near_low[rows:], down)
    below_low = send(add(near_low[:rows], low_via).astype(BF), up)
    above_high = send(add(near_high[rows:], high_via).astype(BF), down)
    targets = [(me + offset) % ny for offset in (0, 2, 1, ny - 1)]
    own_low, own_high, term = last_rows(targets, rows_in, rows_q, weights, *kept)
    term, below_high, above_low = lax.optimization_barrier((term, below_high, above_low))
    low = add(own_low, below_low, above_low).astype(BF)
    high = add(own_high, below_high, above_high).astype(BF)
    return low, high, term


def local(block_in, out_grad, gate_values, expert_ids, conv_kernel, expert_weights):
    frames, width = block_in.shape
    ny, experts = lax.axis_size("y"), lax.axis_size("x") * lax.axis_size("c")
    by_expert = ("x", "c")

    meta = jnp.concatenate([expert_ids.astype(BF).T, gate_values.T], axis=0)
    meta = jnp.pad(meta, ((0, META - 4), (0, width - frames)))
    all_grad = lax.all_gather(jnp.concatenate([out_grad, meta], axis=0), "y", axis=0, tiled=False)
    columns = own_columns(expert_weights)
    columns, packed_in = lax.optimization_barrier((columns, jnp.concatenate([block_in, meta], axis=0)))
    sent_in = route(packed_in[None], experts, False)
    mine_in = lax.all_to_all(sent_in, by_expert, 0, 0, tiled=True)
    rows_in = lax.all_gather(mine_in[:, 0], "y", axis=0, tiled=False)
    sent_q = route(all_grad, experts, True)
    weights = gather_weights(columns, sent_q)
    rows_q = lax.all_to_all(sent_q, by_expert, 0, 0, tiled=True)
    low, high, term = rows_backward(rows_in, rows_q, weights)
    weight_grad = scatter_weight_grad(term)
    summed = jnp.concatenate([low, high], axis=1).reshape(experts, SLOTS, width)
    returned = lax.all_to_all(summed, by_expert, 0, 0, tiled=True)

    own_ids = expert_ids.T[None] == jnp.arange(experts, dtype=jnp.int32)[:, None, None]
    own = slots_of(own_ids[:, 0] | own_ids[:, 1])
    own_placing = own.astype(BF)
    flat = own_placing.reshape(experts * SLOTS, frames)
    frame_grad = out_grad.astype(F32) + dot(
        flat, returned.reshape(experts * SLOTS, width), ((0,), (0,))
    )
    gate_sums = jnp.einsum(
        "es,est,ekt->tk",
        returned[:, SPARE, :SLOTS].astype(F32),
        own.astype(F32),
        own_ids.astype(F32),
        precision="highest",
    )
    gate_out = (gate_sums / gate_values.astype(F32)).astype(BF)

    taps = conv_kernel.shape[0]
    half = (taps - 1) // 2
    kernel_rows = conv_kernel.astype(F32)
    padded = with_halo(frame_grad.astype(BF), half).astype(F32)
    conv_part = jnp.zeros((frames, width), F32)
    for offset in range(taps):
        conv_part = conv_part + kernel_rows[offset] * padded[2 * half - offset : 2 * half - offset + frames]
    input_grad = (frame_grad + conv_part).astype(BF)
    return input_grad, weight_grad, gate_out


def solution(mesh):
    grid = Mesh(mesh.devices.reshape(4, 8, 4, 2), ("y", "z", "x", "c"))
    frames = P(("y", "z", "x", "c"), None)
    weights = P(("x", "c"), ("y", "z"), None)
    in_specs = (frames, frames, frames, frames, P(), weights)
    out_specs = (frames, weights, frames)
    return jax.shard_map(local, mesh=grid, in_specs=in_specs, out_specs=out_specs, check_vma=False)
```

```python
import functools

import jax
import jax.numpy as jnp
from jax import lax
from jax.experimental import pallas as pl
from jax.experimental.pallas import tpu as pltpu
from jax.sharding import Mesh, PartitionSpec as P

BF = jnp.bfloat16
F32 = jnp.float32
SLOTS = 64
SPARE = 60
META = 8
STEP = 4
CHUNK = 256
EDGE = 16


def dot(a, b, contract, batch=((), ())):
    return lax.dot_general(a, b, (contract, batch), preferred_element_type=F32)


def ring_ways(axis):
    count = lax.axis_size(axis)
    up = [(i, (i + 1) % count) for i in range(count)]
    return up, [(target, source) for source, target in up]


def ring_step(right, left, axis):
    up, down = ring_ways(axis)
    return lax.ppermute(right, axis, up), lax.ppermute(left, axis, down)


def own_columns(expert_weights):
    ny = lax.axis_size("y")
    rows, width = expert_weights.shape[1], expert_weights.shape[2]
    part = width // (3 * ny)
    sliced = expert_weights[0].reshape(rows, 3, ny, part).transpose(2, 0, 1, 3)
    return lax.all_to_all(sliced.reshape(ny, rows, 3 * part), "y", 0, 0, tiled=True)


def gather_weights(mine, after):
    ny, rows, width = mine.shape
    nz = lax.axis_size("z")
    me = lax.axis_index("z")

    def place(buffer, shard, z):
        return lax.dynamic_update_slice(buffer, shard[:, None], (0, z % nz, 0, 0))

    buffer = place(jnp.zeros((ny, nz, rows, width), BF), mine, me)
    mine, after = lax.optimization_barrier((mine, after))
    right = left = mine
    for step in range(1, nz // 2):
        right, left = ring_step(right, left, "z")
        buffer = place(place(buffer, right, me - step), left, me + step)
    right = lax.ppermute(right, "z", ring_ways("z")[0])
    buffer = place(buffer, right, me - nz // 2)
    return buffer.reshape(ny * nz * rows, width)


def scatter_weight_grad(term):
    ny, nz = lax.axis_size("y"), lax.axis_size("z")
    rows, part = term.shape[2], term.shape[3] // 3
    mine = lax.psum_scatter(term.reshape(nz * ny * rows, 3 * part), "z", scatter_dimension=0, tiled=True)
    back = lax.all_to_all(mine.reshape(ny, rows, 3 * part), "y", 0, 0, tiled=True)
    back = back.reshape(ny, rows, 3, part).transpose(1, 2, 0, 3)
    return back.reshape(1, rows, 3 * ny * part)


def slots_of(chosen):
    frames = chosen.shape[-1]
    before = (jnp.arange(frames)[:, None] < jnp.arange(frames)[None, :]).astype(BF)
    ranks = dot(chosen.astype(BF), before, ((chosen.ndim - 1,), (0,))).astype(jnp.int32)
    return chosen[..., None, :] & (ranks[..., None, :] == jnp.arange(SLOTS)[:, None])


def halo_of(block, width):
    axes = ("y", "z", "x", "c")
    count = 1
    for axis in axes:
        count *= lax.axis_size(axis)
    forward = [(i, i + 1) for i in range(count - 1)]
    backward = [(target, source) for source, target in forward]
    low = lax.ppermute(block[block.shape[0] - width :], axes, forward)
    return low, lax.ppermute(block[:width], axes, backward)


def convolved(centre, rows, taps):
    total = centre
    count = taps.shape[0]
    for offset in range(count):
        first = count - 1 - offset
        total = total + taps[offset] * rows[first : first + centre.shape[0]]
    return total.astype(BF)


def route_kernel(scaled, x_ref, out_ref):
    rows, width = x_ref.shape[1:]
    frames, experts = rows - META, out_ref.shape[0]
    meta = x_ref[0, frames:rows, :frames].astype(F32)
    names = lax.broadcasted_iota(jnp.int32, (experts, frames), 0).astype(F32)
    first, second = (names == meta[0:1]).astype(F32), (names == meta[1:2]).astype(F32)
    chosen = first + second
    gate = first * meta[2:3] + second * meta[3:4] if scaled else chosen
    earlier = lax.broadcasted_iota(jnp.int32, (frames, frames), 0)
    before = (earlier < lax.broadcasted_iota(jnp.int32, (frames, frames), 1)).astype(F32).astype(BF)
    ranks = dot(chosen.astype(BF), before, ((1,), (0,)))
    slot = lax.broadcasted_iota(jnp.int32, (SLOTS, frames), 0).astype(F32)
    for e in range(experts):
        here = (slot == ranks[e : e + 1]) & (chosen[e : e + 1] > 0.0)
        placing = jnp.where(here, gate[e : e + 1], 0.0).astype(BF)
        out_ref[e, 0] = dot(placing, x_ref[0, :frames], ((1,), (0,))).astype(BF)


def route(packed, experts, scaled):
    groups, rows, width = packed.shape
    return pl.pallas_call(
        functools.partial(route_kernel, scaled),
        grid=(groups,),
        in_specs=[pl.BlockSpec((1, rows, width), lambda i: (i, 0, 0))],
        out_specs=pl.BlockSpec((experts, 1, SLOTS, width), lambda i: (0, i, 0, 0)),
        out_shape=pltpu.HBM((experts, groups, SLOTS, width), BF),
        compiler_params=pltpu.CompilerParams(vmem_limit_bytes=32 * 1024 * 1024),
    )(packed)


def rows_of(u, q, w_ref, low_ref, high_ref, pre_ref, h_ref):
    steps, part, half = h_ref.shape[0], h_ref.shape[3], low_ref.shape[1]
    gate_part = 0.0
    for c in range(0, part, CHUNK):
        gate_in = dot(u, w_ref[:, c : c + CHUNK], ((1,), (0,)))
        up_in = dot(u, w_ref[:, part + c : part + c + CHUNK], ((1,), (0,)))
        hidden_grad = dot(q, w_ref[:, 2 * part + c : 2 * part + c + CHUNK], ((1,), (0,)))
        sigmoid = jax.nn.sigmoid(gate_in)
        activated = gate_in * sigmoid
        hidden = (activated * up_in).astype(BF)
        h_ref[:, 0, :, c : c + CHUNK] = hidden.reshape(steps, SLOTS, CHUNK)
        slope = sigmoid * (1.0 + gate_in * (1.0 - sigmoid))
        pre_ref[:, c : c + CHUNK] = (hidden_grad * up_in * slope).astype(BF)
        pre_ref[:, part + c : part + c + CHUNK] = (hidden_grad * activated).astype(BF)
        gate_part += jnp.sum(hidden.astype(F32) * hidden_grad, axis=1, keepdims=True)
    row_grad = dot(pre_ref[...], w_ref[:, : 2 * part], ((1,), (1,)))
    high_ref[...] = row_grad[:, half:].astype(BF)
    low_ref[...] = row_grad[:, :half].astype(BF)
    row = lax.broadcasted_iota(jnp.int32, (SLOTS, 128), 0)
    lane = lax.broadcasted_iota(jnp.int32, (SLOTS, 128), 1)
    for j in range(steps):
        place = pl.ds(j * SLOTS, SLOTS)
        diagonal = jnp.where(row == lane, gate_part[j * SLOTS : (j + 1) * SLOTS], 0.0)
        line = jnp.sum(diagonal, axis=0, keepdims=True)
        low_ref[place, :128] = jnp.where(row == SPARE, line, low_ref[place, :128].astype(F32)).astype(BF)


def rows_kernel(targets, steps, info, u_ref, q_ref, w_ref, *refs):
    count, width = u_ref.shape[1] * SLOTS, u_ref.shape[3]
    pre_ref, h_ref = refs[-2:]
    pairs = refs[-2 - 2 * targets : -2]
    for t in range(targets):

        @pl.when(pl.program_id(0) // steps == t)
        def _():
            u, q = u_ref[0].reshape(count, width), q_ref[:, 0].reshape(count, width)
            rows_of(u, q, w_ref, pairs[2 * t], pairs[2 * t + 1], pre_ref, h_ref)


def last_kernel(info, u_ref, q_ref, w_ref, pre_ref, h_ref, low_ref, high_ref, term_ref, own_pre, own_h, total):
    step, last = pl.program_id(0), pl.num_programs(0) - 1
    count, width = u_ref.shape[1] * SLOTS, u_ref.shape[3]
    part, wide = h_ref.shape[3], pre_ref.shape[1]
    groups, each = term_ref.shape[1], term_ref.shape[0] * term_ref.shape[2]
    u, q = u_ref[0].reshape(count, width), q_ref[:, 0].reshape(count, width)

    @pl.when(step == 0)
    def _():
        rows_of(u, q, w_ref, low_ref, high_ref, own_pre, own_h)
        total[:, :wide] = dot(u, own_pre[...], ((0,), (0,)))
        total[:, wide:] = dot(q, own_h[:, 0].reshape(count, part), ((0,), (0,)))

    @pl.when(step > 0)
    def _():
        total[:, :wide] += dot(u, pre_ref[...], ((0,), (0,)))
        total[:, wide:] += dot(q, h_ref[:, 0].reshape(count, part), ((0,), (0,)))

    @pl.when(step == last)
    def _():
        for g in range(groups):
            block = total[g * each : (g + 1) * each].astype(BF)
            term_ref[:, g] = block.reshape(term_ref.shape[0], term_ref.shape[2], term_ref.shape[3])


def last_rows(targets, rows_in, rows_q, weights, pre_grads, hidden):
    groups, sources, _, width = rows_in.shape
    nz = lax.axis_size("z")
    part = weights.shape[1] // 3
    mine = sources * SLOTS
    each = width // (groups * nz)
    info = jnp.stack(targets).astype(jnp.int32)
    fixed = lambda i, info: (0, 0)
    return pl.pallas_call(
        last_kernel,
        grid_spec=pltpu.PrefetchScalarGridSpec(
            num_scalar_prefetch=1,
            grid=(groups,),
            in_specs=[
                pl.BlockSpec((1, sources, SLOTS, width), lambda i, info: (info[i], 0, 0, 0)),
                pl.BlockSpec((sources, 1, SLOTS, width), lambda i, info: (0, info[i], 0, 0)),
                pl.BlockSpec(weights.shape, fixed),
                pl.BlockSpec((mine, 2 * part), lambda i, info: (info[jnp.maximum(i, 1)], 0)),
                pl.BlockSpec((sources, 1, SLOTS, part), lambda i, info: (0, info[jnp.maximum(i, 1)], 0, 0)),
            ],
            out_specs=[
                pl.BlockSpec((mine, width // 2), fixed),
                pl.BlockSpec((mine, width // 2), fixed),
                pl.BlockSpec((nz, groups, each, 3 * part), lambda i, info: (0, 0, 0, 0)),
            ],
            scratch_shapes=[
                pltpu.VMEM((mine, 2 * part), BF),
                pltpu.VMEM((sources, 1, SLOTS, part), BF),
                pltpu.VMEM((width, 3 * part), F32),
            ],
        ),
        out_shape=[
            jax.ShapeDtypeStruct((mine, width // 2), BF),
            jax.ShapeDtypeStruct((mine, width // 2), BF),
            jax.ShapeDtypeStruct((nz, groups, each, 3 * part), BF),
        ],
        compiler_params=pltpu.CompilerParams(vmem_limit_bytes=56 * 1024 * 1024),
    )(info, rows_in, rows_q, weights, pre_grads, hidden)


def expert_rows(targets, rows_in, rows_q, weights, kept):
    groups, sources, _, width = rows_in.shape
    part = weights.shape[1] // 3
    steps = sources // STEP
    count = len(targets)
    info = jnp.stack(targets).astype(jnp.int32)
    by_group = lambda i, info: (info[i // steps], i % steps, 0, 0)
    by_source = lambda i, info: (i % steps, info[i // steps], 0, 0)
    half_rows = [
        pl.BlockSpec((STEP * SLOTS, width // 2), lambda i, info, t=t: (jnp.clip(i - t * steps, 0, steps - 1), 0))
        for t in range(count)
        for _ in range(2)
    ]
    *halves, pre_grads, hidden = pl.pallas_call(
        functools.partial(rows_kernel, count, steps),
        grid_spec=pltpu.PrefetchScalarGridSpec(
            num_scalar_prefetch=1,
            grid=(count * steps,),
            in_specs=[
                pl.BlockSpec((1, STEP, SLOTS, width), by_group),
                pl.BlockSpec((STEP, 1, SLOTS, width), by_source),
                pl.BlockSpec(weights.shape, lambda i, info: (0, 0)),
            ]
            + [pl.BlockSpec(memory_space=pl.ANY) for _ in kept],
            out_specs=half_rows
            + [
                pl.BlockSpec((STEP * SLOTS, 2 * part), lambda i, info: (info[i // steps] * steps + i % steps, 0)),
                pl.BlockSpec((STEP, 1, SLOTS, part), by_source),
            ],
        ),
        out_shape=[jax.ShapeDtypeStruct((sources * SLOTS, width // 2), BF)] * (2 * count)
        + [
            jax.ShapeDtypeStruct((groups * sources * SLOTS, 2 * part), BF),
            jax.ShapeDtypeStruct((sources, groups, SLOTS, part), BF),
        ],
        input_output_aliases={4 + k: 2 * count + k for k in range(len(kept))},
        compiler_params=pltpu.CompilerParams(vmem_limit_bytes=52 * 1024 * 1024),
    )(info, rows_in, rows_q, weights, *kept)
    return halves, [pre_grads, hidden]


def add(*parts):
    return sum(part.astype(F32) for part in parts)


def rows_backward(rows_in, rows_q, weights):
    ny = lax.axis_size("y")
    me = lax.axis_index("y")
    up = [(i, (i + 1) % ny) for i in range(ny)]
    down = [(target, source) for source, target in up]

    def send(rows, way):
        return lax.ppermute(rows, "y", way)

    def run(offsets, kept):
        return expert_rows([(me + offset) % ny for offset in offsets], rows_in, rows_q, weights, kept)

    (far_low, far_high), kept = run([2], [])
    low_via, high_via = send(far_low, up), send(far_high, down)
    (up_low, up_high, down_low, down_high), kept = run([1, ny - 1], kept)
    low_via, high_via, kept = lax.optimization_barrier((low_via, high_via, kept))
    below_high, above_low = send(up_high, up), send(down_low, down)
    below_low = send(add(up_low, low_via).astype(BF), up)
    above_high = send(add(down_high, high_via).astype(BF), down)
    targets = [(me + offset) % ny for offset in (0, 2, 1, ny - 1)]
    own_low, own_high, term = last_rows(targets, rows_in, rows_q, weights, *kept)
    term, below_high, above_low = lax.optimization_barrier((term, below_high, above_low))
    low = add(own_low, below_low, above_low).astype(BF)
    high = add(own_high, below_high, above_high).astype(BF)
    return low, high, term


def local(block_in, out_grad, gate_values, expert_ids, conv_kernel, expert_weights):
    frames, width = block_in.shape
    ny, experts = lax.axis_size("y"), lax.axis_size("x") * lax.axis_size("c")
    by_expert = ("x", "c")

    meta = jnp.concatenate([expert_ids.astype(BF).T, gate_values.T], axis=0)
    meta = jnp.pad(meta, ((0, META - 4), (0, width - frames)))
    all_grad = lax.all_gather(jnp.concatenate([out_grad, meta], axis=0), "y", axis=0, tiled=False)
    columns = own_columns(expert_weights)
    columns, packed_in = lax.optimization_barrier((columns, jnp.concatenate([block_in, meta], axis=0)))
    sent_in = route(packed_in[None], experts, False)
    mine_in = lax.all_to_all(sent_in, by_expert, 0, 0, tiled=True)
    rows_in = lax.all_gather(mine_in[:, 0], "y", axis=0, tiled=False)
    sent_q = route(all_grad, experts, True)
    weights = gather_weights(columns, sent_q)
    rows_q = lax.all_to_all(sent_q, by_expert, 0, 0, tiled=True)
    low, high, term = rows_backward(rows_in, rows_q, weights)
    weight_grad = scatter_weight_grad(term)
    summed = jnp.concatenate([low, high], axis=1).reshape(experts, SLOTS, width)
    returned = lax.all_to_all(summed, by_expert, 0, 0, tiled=True)

    own_ids = expert_ids.T[None] == jnp.arange(experts, dtype=jnp.int32)[:, None, None]
    own = slots_of(own_ids[:, 0] | own_ids[:, 1])
    own_placing = own.astype(BF)
    flat = own_placing.reshape(experts * SLOTS, frames)
    frame_grad = out_grad.astype(F32) + dot(
        flat, returned.reshape(experts * SLOTS, width), ((0,), (0,))
    )
    gate_sums = jnp.einsum(
        "es,est,ekt->tk",
        returned[:, SPARE, :SLOTS].astype(F32),
        own.astype(F32),
        own_ids.astype(F32),
        precision="highest",
    )
    gate_out = (gate_sums / gate_values.astype(F32)).astype(BF)

    taps = conv_kernel.astype(F32)
    half = taps.shape[0] // 2
    rounded = frame_grad.astype(BF)
    low, high = halo_of(rounded, half)
    rows = rounded.astype(F32)
    inner = convolved(frame_grad[EDGE : frames - EDGE], rows[EDGE - half : frames - EDGE + half], taps)
    low, high, inner, weight_grad = lax.optimization_barrier((low, high, inner, weight_grad))
    top = jnp.concatenate([low.astype(F32), rows[: EDGE + half]], axis=0)
    bottom = jnp.concatenate([rows[frames - EDGE - half :], high.astype(F32)], axis=0)
    first = convolved(frame_grad[:EDGE], top, taps)
    final = convolved(frame_grad[frames - EDGE :], bottom, taps)
    input_grad = jnp.concatenate([first, inner, final], axis=0)
    return input_grad, weight_grad, gate_out


def solution(mesh):
    grid = Mesh(mesh.devices.reshape(4, 8, 4, 2), ("y", "z", "x", "c"))
    frames = P(("y", "z", "x", "c"), None)
    weights = P(("x", "c"), ("y", "z"), None)
    in_specs = (frames, frames, frames, frames, P(), weights)
    out_specs = (frames, weights, frames)
    return jax.shard_map(local, mesh=grid, in_specs=in_specs, out_specs=out_specs, check_vma=False)
```

```python
import functools

import jax
import jax.numpy as jnp
from jax import lax
from jax.experimental import pallas as pl
from jax.experimental.pallas import tpu as pltpu
from jax.sharding import Mesh, PartitionSpec as P

BF = jnp.bfloat16
F32 = jnp.float32
SLOTS = 64
SPARE = 60
META = 8
STEP = 4
CHUNK = 256
EDGE = 16
EXTRA = 128


def dot(a, b, contract, batch=((), ())):
    return lax.dot_general(a, b, (contract, batch), preferred_element_type=F32)


def ring_ways(axis):
    count = lax.axis_size(axis)
    up = [(i, (i + 1) % count) for i in range(count)]
    return up, [(target, source) for source, target in up]


def ring_step(right, left, axis):
    up, down = ring_ways(axis)
    return lax.ppermute(right, axis, up), lax.ppermute(left, axis, down)


def own_columns(expert_weights):
    ny = lax.axis_size("y")
    rows, width = expert_weights.shape[1], expert_weights.shape[2]
    part = width // (3 * ny)
    sliced = expert_weights[0].reshape(rows, 3, ny, part).transpose(2, 0, 1, 3)
    return lax.all_to_all(sliced.reshape(ny, rows, 3 * part), "y", 0, 0, tiled=True)


def gather_weights(mine, after):
    ny, rows, width = mine.shape
    nz = lax.axis_size("z")
    me = lax.axis_index("z")

    def place(buffer, shard, z):
        return lax.dynamic_update_slice(buffer, shard[:, None], (0, z % nz, 0, 0))

    buffer = place(jnp.zeros((ny, nz, rows, width), BF), mine, me)
    mine, after = lax.optimization_barrier((mine, after))
    right = left = mine
    for step in range(1, nz // 2):
        right, left = ring_step(right, left, "z")
        buffer = place(place(buffer, right, me - step), left, me + step)
    right = lax.ppermute(right, "z", ring_ways("z")[0])
    buffer = place(buffer, right, me - nz // 2)
    return buffer.reshape(ny * nz * rows, width)


def merge_kernel(parts_ref, out_ref):
    ny, rows, wide = parts_ref.shape
    part = wide // 3
    for k in range(3):
        for y in range(ny):
            first = (k * ny + y) * part
            out_ref[:, first : first + part] = parts_ref[y, :, k * part : (k + 1) * part]


def merged(parts):
    ny, rows, wide = parts.shape
    return pl.pallas_call(merge_kernel, out_shape=jax.ShapeDtypeStruct((rows, ny * wide), BF))(parts)


def sum_kernel(*refs):
    out_ref = refs[-1]
    half = refs[0].shape[1]
    for side in range(2):
        own, below, above = (ref[...].astype(F32) for ref in refs[3 * side : 3 * side + 3])
        out_ref[:, side * half : (side + 1) * half] = (own + below + above).astype(BF)


def summed(*parts):
    rows, half = parts[0].shape
    shape = jax.ShapeDtypeStruct((rows, 2 * half), BF)
    limit = pltpu.CompilerParams(vmem_limit_bytes=32 * 1024 * 1024)
    return pl.pallas_call(sum_kernel, out_shape=shape, compiler_params=limit)(*parts)


def scatter_weight_grad(term):
    ny, nz = lax.axis_size("y"), lax.axis_size("z")
    rows, part = term.shape[2], term.shape[3] // 3
    mine = lax.psum_scatter(term.reshape(nz * ny * rows, 3 * part), "z", scatter_dimension=0, tiled=True)
    back = lax.all_to_all(mine.reshape(ny, rows, 3 * part), "y", 0, 0, tiled=True)
    return mine, merged(back)[None]


def slots_of(chosen):
    frames = chosen.shape[-1]
    before = (jnp.arange(frames)[:, None] < jnp.arange(frames)[None, :]).astype(BF)
    ranks = dot(chosen.astype(BF), before, ((chosen.ndim - 1,), (0,))).astype(jnp.int32)
    return chosen[..., None, :] & (ranks[..., None, :] == jnp.arange(SLOTS)[:, None])


def halo_of(block, width):
    axes = ("y", "z", "x", "c")
    count = 1
    for axis in axes:
        count *= lax.axis_size(axis)
    forward = [(i, i + 1) for i in range(count - 1)]
    backward = [(target, source) for source, target in forward]
    low = lax.ppermute(block[block.shape[0] - width :], axes, forward)
    return low, lax.ppermute(block[:width], axes, backward)


def convolved(centre, rows, taps):
    total = centre
    count = taps.shape[0]
    for offset in range(count):
        first = count - 1 - offset
        total = total + taps[offset] * rows[first : first + centre.shape[0]]
    return total.astype(BF)


def route_kernel(plain, x_ref, out_ref):
    rows, width = x_ref.shape[1:]
    frames, experts = rows - META, out_ref.shape[0]
    meta = x_ref[0, frames:rows, :frames].astype(F32)
    names = lax.broadcasted_iota(jnp.int32, (experts, frames), 0).astype(F32)
    first, second = (names == meta[0:1]).astype(F32), (names == meta[1:2]).astype(F32)
    chosen = first + second
    gate = first * meta[2:3] + second * meta[3:4]
    earlier = lax.broadcasted_iota(jnp.int32, (frames, frames), 0)
    before = (earlier < lax.broadcasted_iota(jnp.int32, (frames, frames), 1)).astype(F32).astype(BF)
    ranks = dot(chosen.astype(BF), before, ((1,), (0,)))
    slot = lax.broadcasted_iota(jnp.int32, (SLOTS, frames), 0).astype(F32)
    for e in range(experts):
        here = (slot == ranks[e : e + 1]) & (chosen[e : e + 1] > 0.0)
        if plain:
            placing = jnp.where(here, 1.0, 0.0).astype(BF)
            out_ref[e, 0, :, :plain] = dot(placing, x_ref[0, :frames, :plain], ((1,), (0,))).astype(BF)
        placing = jnp.where(here, gate[e : e + 1], 0.0).astype(BF)
        out_ref[e, 0, :, plain:] = dot(placing, x_ref[0, :frames, plain:], ((1,), (0,))).astype(BF)


def route(packed, experts, plain):
    groups, rows, width = packed.shape
    return pl.pallas_call(
        functools.partial(route_kernel, plain),
        grid=(groups,),
        in_specs=[pl.BlockSpec((1, rows, width), lambda i: (i, 0, 0))],
        out_specs=pl.BlockSpec((experts, 1, SLOTS, width), lambda i: (0, i, 0, 0)),
        out_shape=pltpu.HBM((experts, groups, SLOTS, width), BF),
        compiler_params=pltpu.CompilerParams(vmem_limit_bytes=32 * 1024 * 1024),
    )(packed)


def rows_of(u, q, w_ref, low_ref, high_ref, pre_ref, h_ref):
    steps, part, half = h_ref.shape[0], h_ref.shape[3], low_ref.shape[1]
    gate_part = 0.0
    for c in range(0, part, CHUNK):
        gate_in = dot(u, w_ref[:, c : c + CHUNK], ((1,), (0,)))
        up_in = dot(u, w_ref[:, part + c : part + c + CHUNK], ((1,), (0,)))
        hidden_grad = dot(q, w_ref[:, 2 * part + c : 2 * part + c + CHUNK], ((1,), (0,)))
        sigmoid = jax.nn.sigmoid(gate_in)
        activated = gate_in * sigmoid
        hidden = (activated * up_in).astype(BF)
        h_ref[:, 0, :, c : c + CHUNK] = hidden.reshape(steps, SLOTS, CHUNK)
        slope = sigmoid * (1.0 + gate_in * (1.0 - sigmoid))
        pre_ref[:, c : c + CHUNK] = (hidden_grad * up_in * slope).astype(BF)
        pre_ref[:, part + c : part + c + CHUNK] = (hidden_grad * activated).astype(BF)
        gate_part += jnp.sum(hidden.astype(F32) * hidden_grad, axis=1, keepdims=True)
    row_grad = dot(pre_ref[...], w_ref[:, : 2 * part], ((1,), (1,)))
    high_ref[...] = row_grad[:, half:].astype(BF)
    low_ref[...] = row_grad[:, :half].astype(BF)
    row = lax.broadcasted_iota(jnp.int32, (SLOTS, 128), 0)
    lane = lax.broadcasted_iota(jnp.int32, (SLOTS, 128), 1)
    for j in range(steps):
        place = pl.ds(j * SLOTS, SLOTS)
        diagonal = jnp.where(row == lane, gate_part[j * SLOTS : (j + 1) * SLOTS], 0.0)
        line = jnp.sum(diagonal, axis=0, keepdims=True)
        low_ref[place, :128] = jnp.where(row == SPARE, line, low_ref[place, :128].astype(F32)).astype(BF)


def both_rows(u_ref, q_ref, width):
    count = u_ref.shape[1] * SLOTS
    rows = u_ref[0].reshape(count, u_ref.shape[3])
    q = jnp.concatenate([rows[:, width:], q_ref[:, 0].reshape(count, q_ref.shape[3])], axis=1)
    return rows[:, :width], q


def rows_kernel(targets, steps, info, u_ref, q_ref, w_ref, *refs):
    pre_ref, h_ref = refs[-2:]
    pairs = refs[-2 - 2 * targets : -2]
    for t in range(targets):

        @pl.when(pl.program_id(0) // steps == t)
        def _():
            u, q = both_rows(u_ref, q_ref, w_ref.shape[0])
            rows_of(u, q, w_ref, pairs[2 * t], pairs[2 * t + 1], pre_ref, h_ref)


def last_kernel(info, u_ref, q_ref, w_ref, pre_ref, h_ref, low_ref, high_ref, term_ref, own_pre, own_h, total):
    step, last = pl.program_id(0), pl.num_programs(0) - 1
    count = u_ref.shape[1] * SLOTS
    part, wide = h_ref.shape[3], pre_ref.shape[1]
    groups, each = term_ref.shape[1], term_ref.shape[0] * term_ref.shape[2]
    u, q = both_rows(u_ref, q_ref, w_ref.shape[0])

    @pl.when(step == 0)
    def _():
        rows_of(u, q, w_ref, low_ref, high_ref, own_pre, own_h)
        total[:, :wide] = dot(u, own_pre[...], ((0,), (0,)))
        total[:, wide:] = dot(q, own_h[:, 0].reshape(count, part), ((0,), (0,)))

    @pl.when(step > 0)
    def _():
        total[:, :wide] += dot(u, pre_ref[...], ((0,), (0,)))
        total[:, wide:] += dot(q, h_ref[:, 0].reshape(count, part), ((0,), (0,)))

    @pl.when(step == last)
    def _():
        for g in range(groups):
            block = total[g * each : (g + 1) * each].astype(BF)
            term_ref[:, g] = block.reshape(term_ref.shape[0], term_ref.shape[2], term_ref.shape[3])


def last_rows(targets, rows_in, rows_q, weights, pre_grads, hidden):
    groups, sources = rows_in.shape[:2]
    width = weights.shape[0]
    nz = lax.axis_size("z")
    part = weights.shape[1] // 3
    mine = sources * SLOTS
    each = width // (groups * nz)
    info = jnp.stack(targets).astype(jnp.int32)
    fixed = lambda i, info: (0, 0)
    return pl.pallas_call(
        last_kernel,
        grid_spec=pltpu.PrefetchScalarGridSpec(
            num_scalar_prefetch=1,
            grid=(groups,),
            in_specs=[
                pl.BlockSpec((1, sources, SLOTS, rows_in.shape[3]), lambda i, info: (info[i], 0, 0, 0)),
                pl.BlockSpec((sources, 1, SLOTS, rows_q.shape[3]), lambda i, info: (0, info[i], 0, 0)),
                pl.BlockSpec(weights.shape, fixed),
                pl.BlockSpec((mine, 2 * part), lambda i, info: (info[jnp.maximum(i, 1)], 0)),
                pl.BlockSpec((sources, 1, SLOTS, part), lambda i, info: (0, info[jnp.maximum(i, 1)], 0, 0)),
            ],
            out_specs=[
                pl.BlockSpec((mine, width // 2), fixed),
                pl.BlockSpec((mine, width // 2), fixed),
                pl.BlockSpec((nz, groups, each, 3 * part), lambda i, info: (0, 0, 0, 0)),
            ],
            scratch_shapes=[
                pltpu.VMEM((mine, 2 * part), BF),
                pltpu.VMEM((sources, 1, SLOTS, part), BF),
                pltpu.VMEM((width, 3 * part), F32),
            ],
        ),
        out_shape=[
            jax.ShapeDtypeStruct((mine, width // 2), BF),
            jax.ShapeDtypeStruct((mine, width // 2), BF),
            jax.ShapeDtypeStruct((nz, groups, each, 3 * part), BF),
        ],
        compiler_params=pltpu.CompilerParams(vmem_limit_bytes=56 * 1024 * 1024),
    )(info, rows_in, rows_q, weights, pre_grads, hidden)


def expert_rows(targets, rows_in, rows_q, weights, kept):
    groups, sources = rows_in.shape[:2]
    width, part = weights.shape[0], weights.shape[1] // 3
    steps = sources // STEP
    count = len(targets)
    info = jnp.stack(targets).astype(jnp.int32)
    by_group = lambda i, info: (info[i // steps], i % steps, 0, 0)
    by_source = lambda i, info: (i % steps, info[i // steps], 0, 0)
    half_rows = [
        pl.BlockSpec((STEP * SLOTS, width // 2), lambda i, info, t=t: (jnp.clip(i - t * steps, 0, steps - 1), 0))
        for t in range(count)
        for _ in range(2)
    ]
    *halves, pre_grads, hidden = pl.pallas_call(
        functools.partial(rows_kernel, count, steps),
        grid_spec=pltpu.PrefetchScalarGridSpec(
            num_scalar_prefetch=1,
            grid=(count * steps,),
            in_specs=[
                pl.BlockSpec((1, STEP, SLOTS, rows_in.shape[3]), by_group),
                pl.BlockSpec((STEP, 1, SLOTS, rows_q.shape[3]), by_source),
                pl.BlockSpec(weights.shape, lambda i, info: (0, 0)),
            ]
            + [pl.BlockSpec(memory_space=pl.ANY) for _ in kept],
            out_specs=half_rows
            + [
                pl.BlockSpec((STEP * SLOTS, 2 * part), lambda i, info: (info[i // steps] * steps + i % steps, 0)),
                pl.BlockSpec((STEP, 1, SLOTS, part), by_source),
            ],
        ),
        out_shape=[jax.ShapeDtypeStruct((sources * SLOTS, width // 2), BF)] * (2 * count)
        + [
            jax.ShapeDtypeStruct((groups * sources * SLOTS, 2 * part), BF),
            jax.ShapeDtypeStruct((sources, groups, SLOTS, part), BF),
        ],
        input_output_aliases={4 + k: 2 * count + k for k in range(len(kept))},
        compiler_params=pltpu.CompilerParams(vmem_limit_bytes=52 * 1024 * 1024),
    )(info, rows_in, rows_q, weights, *kept)
    return halves, [pre_grads, hidden]


def add(*parts):
    return sum(part.astype(F32) for part in parts)


def rows_backward(rows_in, rows_q, weights):
    ny = lax.axis_size("y")
    me = lax.axis_index("y")
    up = [(i, (i + 1) % ny) for i in range(ny)]
    down = [(target, source) for source, target in up]

    def send(rows, way):
        return lax.ppermute(rows, "y", way)

    def run(offsets, kept):
        return expert_rows([(me + offset) % ny for offset in offsets], rows_in, rows_q, weights, kept)

    (far_low, far_high), kept = run([2], [])
    low_via, high_via = send(far_low, up), send(far_high, down)
    (up_low, up_high, down_low, down_high), kept = run([1, ny - 1], kept)
    low_via, high_via, kept = lax.optimization_barrier((low_via, high_via, kept))
    below_high, above_low = send(up_high, up), send(down_low, down)
    below_low = send(add(up_low, low_via).astype(BF), up)
    above_high = send(add(down_high, high_via).astype(BF), down)
    targets = [(me + offset) % ny for offset in (0, 2, 1, ny - 1)]
    own_low, own_high, term = last_rows(targets, rows_in, rows_q, weights, *kept)
    term, below_high, above_low = lax.optimization_barrier((term, below_high, above_low))
    return summed(own_low, below_low, above_low, own_high, below_high, above_high), term


def local(block_in, out_grad, gate_values, expert_ids, conv_kernel, expert_weights):
    frames, width = block_in.shape
    ny, experts = lax.axis_size("y"), lax.axis_size("x") * lax.axis_size("c")
    by_expert = ("x", "c")

    meta = jnp.concatenate([expert_ids.astype(BF).T, gate_values.T], axis=0)

    def packed(*arrays):
        rows = jnp.concatenate(arrays, axis=1)
        return jnp.concatenate([rows, jnp.pad(meta, ((0, META - 4), (0, rows.shape[1] - frames)))], axis=0)

    all_grad = lax.all_gather(packed(out_grad[:, EXTRA:]), "y", axis=0, tiled=False)
    columns = own_columns(expert_weights)
    columns, packed_in = lax.optimization_barrier((columns, packed(block_in, out_grad[:, :EXTRA])))
    sent_in = route(packed_in[None], experts, width)
    mine_in = lax.all_to_all(sent_in, by_expert, 0, 0, tiled=True)
    rows_in = lax.all_gather(mine_in[:, 0], "y", axis=0, tiled=False)
    sent_q = route(all_grad, experts, 0)
    weights = gather_weights(columns, sent_q)
    rows_q = lax.all_to_all(sent_q, by_expert, 0, 0, tiled=True)
    row_sums, term = rows_backward(rows_in, rows_q, weights)
    reduced, weight_grad = scatter_weight_grad(term)
    returned = lax.all_to_all(row_sums.reshape(experts, SLOTS, width), by_expert, 0, 0, tiled=True)

    own_ids = expert_ids.T[None] == jnp.arange(experts, dtype=jnp.int32)[:, None, None]
    own = slots_of(own_ids[:, 0] | own_ids[:, 1])
    own_placing = own.astype(BF)
    flat = own_placing.reshape(experts * SLOTS, frames)
    frame_grad = out_grad.astype(F32) + dot(
        flat, returned.reshape(experts * SLOTS, width), ((0,), (0,))
    )
    gate_sums = jnp.einsum(
        "es,est,ekt->tk",
        returned[:, SPARE, :SLOTS].astype(F32),
        own.astype(F32),
        own_ids.astype(F32),
        precision="highest",
    )
    gate_out = (gate_sums / gate_values.astype(F32)).astype(BF)

    taps = conv_kernel.astype(F32)
    half = taps.shape[0] // 2
    rounded = frame_grad.astype(BF)
    low, high = halo_of(rounded, half)
    frame_grad, rounded, reduced = lax.optimization_barrier((frame_grad, rounded, reduced))
    rows = rounded.astype(F32)
    inner = convolved(frame_grad[EDGE : frames - EDGE], rows[EDGE - half : frames - EDGE + half], taps)
    low, high, inner, weight_grad = lax.optimization_barrier((low, high, inner, weight_grad))
    top = jnp.concatenate([low.astype(F32), rows[: EDGE + half]], axis=0)
    bottom = jnp.concatenate([rows[frames - EDGE - half :], high.astype(F32)], axis=0)
    first = convolved(frame_grad[:EDGE], top, taps)
    final = convolved(frame_grad[frames - EDGE :], bottom, taps)
    input_grad = jnp.concatenate([first, inner, final], axis=0)
    return input_grad, weight_grad, gate_out


def solution(mesh):
    grid = Mesh(mesh.devices.reshape(4, 8, 4, 2), ("y", "z", "x", "c"))
    frames = P(("y", "z", "x", "c"), None)
    weights = P(("x", "c"), ("y", "z"), None)
    in_specs = (frames, frames, frames, frames, P(), weights)
    out_specs = (frames, weights, frames)
    return jax.shard_map(local, mesh=grid, in_specs=in_specs, out_specs=out_specs, check_vma=False)
```

```python
import functools

import jax
import jax.numpy as jnp
from jax import lax
from jax.experimental import pallas as pl
from jax.experimental.pallas import tpu as pltpu
from jax.sharding import Mesh, PartitionSpec as P

BF = jnp.bfloat16
F32 = jnp.float32
SLOTS = 64
SPARE = 60
META = 8
STEP = 4
CHUNK = 256
EDGE = 16


def dot(a, b, contract, batch=((), ())):
    return lax.dot_general(a, b, (contract, batch), preferred_element_type=F32)


def ring_ways(axis):
    count = lax.axis_size(axis)
    up = [(i, (i + 1) % count) for i in range(count)]
    return up, [(target, source) for source, target in up]


def ring_step(right, left, axis):
    up, down = ring_ways(axis)
    return lax.ppermute(right, axis, up), lax.ppermute(left, axis, down)


def own_columns(expert_weights):
    ny = lax.axis_size("y")
    rows, width = expert_weights.shape[1], expert_weights.shape[2]
    part = width // (3 * ny)
    sliced = expert_weights[0].reshape(rows, 3, ny, part).transpose(2, 0, 1, 3)
    return lax.all_to_all(sliced.reshape(ny, rows, 3 * part), "y", 0, 0, tiled=True)


def gather_weights(mine, after):
    ny, rows, width = mine.shape
    nz = lax.axis_size("z")
    me = lax.axis_index("z")

    def place(buffer, shard, z):
        return lax.dynamic_update_slice(buffer, shard[:, None], (0, z % nz, 0, 0))

    buffer = place(jnp.zeros((ny, nz, rows, width), BF), mine, me)
    mine, after = lax.optimization_barrier((mine, after))
    right = left = mine
    for step in range(1, nz // 2):
        right, left = ring_step(right, left, "z")
        buffer = place(place(buffer, right, me - step), left, me + step)
    up, down = ring_ways("z")
    across = [lax.ppermute(right[: ny // 2], "z", up), lax.ppermute(left[ny // 2 :], "z", down)]
    buffer = place(buffer, jnp.concatenate(across, axis=0), me + nz // 2)
    return buffer.reshape(ny * nz * rows, width)


def merge_kernel(parts_ref, out_ref):
    ny, rows, wide = parts_ref.shape
    part = wide // 3
    for k in range(3):
        for y in range(ny):
            first = (k * ny + y) * part
            out_ref[:, first : first + part] = parts_ref[y, :, k * part : (k + 1) * part]


def merged(parts):
    ny, rows, wide = parts.shape
    return pl.pallas_call(merge_kernel, out_shape=jax.ShapeDtypeStruct((rows, ny * wide), BF))(parts)


def sum_kernel(*refs):
    out_ref = refs[-1]
    half = refs[0].shape[1]
    for side in range(2):
        own, below, above = (ref[...].astype(F32) for ref in refs[3 * side : 3 * side + 3])
        out_ref[:, side * half : (side + 1) * half] = (own + below + above).astype(BF)


def summed(*parts):
    rows, half = parts[0].shape
    shape = jax.ShapeDtypeStruct((rows, 2 * half), BF)
    limit = pltpu.CompilerParams(vmem_limit_bytes=32 * 1024 * 1024)
    return pl.pallas_call(sum_kernel, out_shape=shape, compiler_params=limit)(*parts)


def scatter_weight_grad(term):
    ny, nz = lax.axis_size("y"), lax.axis_size("z")
    rows, part = term.shape[2], term.shape[3] // 3
    mine = lax.psum_scatter(term.reshape(nz * ny * rows, 3 * part), "z", scatter_dimension=0, tiled=True)
    back = lax.all_to_all(mine.reshape(ny, rows, 3 * part), "y", 0, 0, tiled=True)
    return mine, merged(back)[None]


def slots_of(chosen):
    frames = chosen.shape[-1]
    before = (jnp.arange(frames)[:, None] < jnp.arange(frames)[None, :]).astype(BF)
    ranks = dot(chosen.astype(BF), before, ((chosen.ndim - 1,), (0,))).astype(jnp.int32)
    return chosen[..., None, :] & (ranks[..., None, :] == jnp.arange(SLOTS)[:, None])


def halo_of(block, width):
    axes = ("y", "z", "x", "c")
    count = 1
    for axis in axes:
        count *= lax.axis_size(axis)
    forward = [(i, i + 1) for i in range(count - 1)]
    backward = [(target, source) for source, target in forward]
    low = lax.ppermute(block[block.shape[0] - width :], axes, forward)
    return low, lax.ppermute(block[:width], axes, backward)


def convolved(centre, rows, taps):
    total = centre
    count = taps.shape[0]
    for offset in range(count):
        first = count - 1 - offset
        total = total + taps[offset] * rows[first : first + centre.shape[0]]
    return total.astype(BF)


def route_kernel(scaled, x_ref, out_ref):
    rows, width = x_ref.shape[1:]
    frames, experts = rows - META, out_ref.shape[0]
    meta = x_ref[0, frames:rows, :frames].astype(F32)
    names = lax.broadcasted_iota(jnp.int32, (experts, frames), 0).astype(F32)
    first, second = (names == meta[0:1]).astype(F32), (names == meta[1:2]).astype(F32)
    chosen = first + second
    gate = first * meta[2:3] + second * meta[3:4] if scaled else chosen
    earlier = lax.broadcasted_iota(jnp.int32, (frames, frames), 0)
    before = (earlier < lax.broadcasted_iota(jnp.int32, (frames, frames), 1)).astype(F32).astype(BF)
    ranks = dot(chosen.astype(BF), before, ((1,), (0,)))
    slot = lax.broadcasted_iota(jnp.int32, (SLOTS, frames), 0).astype(F32)
    for e in range(experts):
        here = (slot == ranks[e : e + 1]) & (chosen[e : e + 1] > 0.0)
        placing = jnp.where(here, gate[e : e + 1], 0.0).astype(BF)
        out_ref[e, 0] = dot(placing, x_ref[0, :frames], ((1,), (0,))).astype(BF)


def route(packed, experts, scaled):
    groups, rows, width = packed.shape
    return pl.pallas_call(
        functools.partial(route_kernel, scaled),
        grid=(groups,),
        in_specs=[pl.BlockSpec((1, rows, width), lambda i: (i, 0, 0))],
        out_specs=pl.BlockSpec((experts, 1, SLOTS, width), lambda i: (0, i, 0, 0)),
        out_shape=pltpu.HBM((experts, groups, SLOTS, width), BF),
        compiler_params=pltpu.CompilerParams(vmem_limit_bytes=32 * 1024 * 1024),
    )(packed)


def rows_of(u, q, w_ref, low_ref, high_ref, pre_ref, h_ref):
    steps, part, half = h_ref.shape[0], h_ref.shape[3], low_ref.shape[1]
    gate_part = 0.0
    for c in range(0, part, CHUNK):
        gate_in = dot(u, w_ref[:, c : c + CHUNK], ((1,), (0,)))
        up_in = dot(u, w_ref[:, part + c : part + c + CHUNK], ((1,), (0,)))
        hidden_grad = dot(q, w_ref[:, 2 * part + c : 2 * part + c + CHUNK], ((1,), (0,)))
        sigmoid = jax.nn.sigmoid(gate_in)
        activated = gate_in * sigmoid
        hidden = (activated * up_in).astype(BF)
        h_ref[:, 0, :, c : c + CHUNK] = hidden.reshape(steps, SLOTS, CHUNK)
        slope = sigmoid * (1.0 + gate_in * (1.0 - sigmoid))
        pre_ref[:, c : c + CHUNK] = (hidden_grad * up_in * slope).astype(BF)
        pre_ref[:, part + c : part + c + CHUNK] = (hidden_grad * activated).astype(BF)
        gate_part += jnp.sum(hidden.astype(F32) * hidden_grad, axis=1, keepdims=True)
    row_grad = dot(pre_ref[...], w_ref[:, : 2 * part], ((1,), (1,)))
    high_ref[...] = row_grad[:, half:].astype(BF)
    low_ref[...] = row_grad[:, :half].astype(BF)
    row = lax.broadcasted_iota(jnp.int32, (SLOTS, 128), 0)
    lane = lax.broadcasted_iota(jnp.int32, (SLOTS, 128), 1)
    for j in range(steps):
        place = pl.ds(j * SLOTS, SLOTS)
        diagonal = jnp.where(row == lane, gate_part[j * SLOTS : (j + 1) * SLOTS], 0.0)
        line = jnp.sum(diagonal, axis=0, keepdims=True)
        low_ref[place, :128] = jnp.where(row == SPARE, line, low_ref[place, :128].astype(F32)).astype(BF)


def rows_kernel(targets, steps, info, u_ref, q_ref, w_ref, *refs):
    count, width = u_ref.shape[1] * SLOTS, u_ref.shape[3]
    pre_ref, h_ref = refs[-2:]
    pairs = refs[-2 - 2 * targets : -2]
    for t in range(targets):

        @pl.when(pl.program_id(0) // steps == t)
        def _():
            u, q = u_ref[0].reshape(count, width), q_ref[:, 0].reshape(count, width)
            rows_of(u, q, w_ref, pairs[2 * t], pairs[2 * t + 1], pre_ref, h_ref)


def last_kernel(info, u_ref, q_ref, w_ref, pre_ref, h_ref, low_ref, high_ref, term_ref, own_pre, own_h, total):
    step, last = pl.program_id(0), pl.num_programs(0) - 1
    count, width = u_ref.shape[1] * SLOTS, u_ref.shape[3]
    part, wide = h_ref.shape[3], pre_ref.shape[1]
    groups, each = term_ref.shape[1], term_ref.shape[0] * term_ref.shape[2]
    u, q = u_ref[0].reshape(count, width), q_ref[:, 0].reshape(count, width)

    @pl.when(step == 0)
    def _():
        rows_of(u, q, w_ref, low_ref, high_ref, own_pre, own_h)
        total[:, :wide] = dot(u, own_pre[...], ((0,), (0,)))
        total[:, wide:] = dot(q, own_h[:, 0].reshape(count, part), ((0,), (0,)))

    @pl.when(step > 0)
    def _():
        total[:, :wide] += dot(u, pre_ref[...], ((0,), (0,)))
        total[:, wide:] += dot(q, h_ref[:, 0].reshape(count, part), ((0,), (0,)))

    @pl.when(step == last)
    def _():
        for g in range(groups):
            block = total[g * each : (g + 1) * each].astype(BF)
            term_ref[:, g] = block.reshape(term_ref.shape[0], term_ref.shape[2], term_ref.shape[3])


def last_rows(targets, rows_in, rows_q, weights, pre_grads, hidden):
    groups, sources, _, width = rows_in.shape
    nz = lax.axis_size("z")
    part = weights.shape[1] // 3
    mine = sources * SLOTS
    each = width // (groups * nz)
    info = jnp.stack(targets).astype(jnp.int32)
    fixed = lambda i, info: (0, 0)
    return pl.pallas_call(
        last_kernel,
        grid_spec=pltpu.PrefetchScalarGridSpec(
            num_scalar_prefetch=1,
            grid=(groups,),
            in_specs=[
                pl.BlockSpec((1, sources, SLOTS, width), lambda i, info: (info[i], 0, 0, 0)),
                pl.BlockSpec((sources, 1, SLOTS, width), lambda i, info: (0, info[i], 0, 0)),
                pl.BlockSpec(weights.shape, fixed),
                pl.BlockSpec((mine, 2 * part), lambda i, info: (info[jnp.maximum(i, 1)], 0)),
                pl.BlockSpec((sources, 1, SLOTS, part), lambda i, info: (0, info[jnp.maximum(i, 1)], 0, 0)),
            ],
            out_specs=[
                pl.BlockSpec((mine, width // 2), fixed),
                pl.BlockSpec((mine, width // 2), fixed),
                pl.BlockSpec((nz, groups, each, 3 * part), lambda i, info: (0, 0, 0, 0)),
            ],
            scratch_shapes=[
                pltpu.VMEM((mine, 2 * part), BF),
                pltpu.VMEM((sources, 1, SLOTS, part), BF),
                pltpu.VMEM((width, 3 * part), F32),
            ],
        ),
        out_shape=[
            jax.ShapeDtypeStruct((mine, width // 2), BF),
            jax.ShapeDtypeStruct((mine, width // 2), BF),
            jax.ShapeDtypeStruct((nz, groups, each, 3 * part), BF),
        ],
        compiler_params=pltpu.CompilerParams(vmem_limit_bytes=56 * 1024 * 1024),
    )(info, rows_in, rows_q, weights, pre_grads, hidden)


def expert_rows(targets, rows_in, rows_q, weights, kept):
    groups, sources, _, width = rows_in.shape
    part = weights.shape[1] // 3
    steps = sources // STEP
    count = len(targets)
    info = jnp.stack(targets).astype(jnp.int32)
    by_group = lambda i, info: (info[i // steps], i % steps, 0, 0)
    by_source = lambda i, info: (i % steps, info[i // steps], 0, 0)
    half_rows = [
        pl.BlockSpec((STEP * SLOTS, width // 2), lambda i, info, t=t: (jnp.clip(i - t * steps, 0, steps - 1), 0))
        for t in range(count)
        for _ in range(2)
    ]
    *halves, pre_grads, hidden = pl.pallas_call(
        functools.partial(rows_kernel, count, steps),
        grid_spec=pltpu.PrefetchScalarGridSpec(
            num_scalar_prefetch=1,
            grid=(count * steps,),
            in_specs=[
                pl.BlockSpec((1, STEP, SLOTS, width), by_group),
                pl.BlockSpec((STEP, 1, SLOTS, width), by_source),
                pl.BlockSpec(weights.shape, lambda i, info: (0, 0)),
            ]
            + [pl.BlockSpec(memory_space=pl.ANY) for _ in kept],
            out_specs=half_rows
            + [
                pl.BlockSpec((STEP * SLOTS, 2 * part), lambda i, info: (info[i // steps] * steps + i % steps, 0)),
                pl.BlockSpec((STEP, 1, SLOTS, part), by_source),
            ],
        ),
        out_shape=[jax.ShapeDtypeStruct((sources * SLOTS, width // 2), BF)] * (2 * count)
        + [
            jax.ShapeDtypeStruct((groups * sources * SLOTS, 2 * part), BF),
            jax.ShapeDtypeStruct((sources, groups, SLOTS, part), BF),
        ],
        input_output_aliases={4 + k: 2 * count + k for k in range(len(kept))},
        compiler_params=pltpu.CompilerParams(vmem_limit_bytes=52 * 1024 * 1024),
    )(info, rows_in, rows_q, weights, *kept)
    return halves, [pre_grads, hidden]


def add(*parts):
    return sum(part.astype(F32) for part in parts)


def rows_backward(rows_in, rows_q, weights):
    ny = lax.axis_size("y")
    me = lax.axis_index("y")
    up = [(i, (i + 1) % ny) for i in range(ny)]
    down = [(target, source) for source, target in up]

    def send(rows, way):
        return lax.ppermute(rows, "y", way)

    def run(offsets, kept):
        return expert_rows([(me + offset) % ny for offset in offsets], rows_in, rows_q, weights, kept)

    (far_low, far_high), kept = run([2], [])
    low_via, high_via = send(far_low, up), send(far_high, down)
    (up_low, up_high, down_low, down_high), kept = run([1, ny - 1], kept)
    low_via, high_via, kept = lax.optimization_barrier((low_via, high_via, kept))
    below_high, above_low = send(up_high, up), send(down_low, down)
    below_low = send(add(up_low, low_via).astype(BF), up)
    above_high = send(add(down_high, high_via).astype(BF), down)
    targets = [(me + offset) % ny for offset in (0, 2, 1, ny - 1)]
    own_low, own_high, term = last_rows(targets, rows_in, rows_q, weights, *kept)
    term, below_high, above_low = lax.optimization_barrier((term, below_high, above_low))
    return summed(own_low, below_low, above_low, own_high, below_high, above_high), term


def local(block_in, out_grad, gate_values, expert_ids, conv_kernel, expert_weights):
    frames, width = block_in.shape
    ny, experts = lax.axis_size("y"), lax.axis_size("x") * lax.axis_size("c")
    by_expert = ("x", "c")

    meta = jnp.concatenate([expert_ids.astype(BF).T, gate_values.T], axis=0)
    meta = jnp.pad(meta, ((0, META - 4), (0, width - frames)))
    all_grad = lax.all_gather(jnp.concatenate([out_grad, meta], axis=0), "y", axis=0, tiled=False)
    columns = own_columns(expert_weights)
    columns, packed_in = lax.optimization_barrier((columns, jnp.concatenate([block_in, meta], axis=0)))
    sent_in = route(packed_in[None], experts, False)
    mine_in = lax.all_to_all(sent_in, by_expert, 0, 0, tiled=True)
    rows_in = lax.all_gather(mine_in[:, 0], "y", axis=0, tiled=False)
    sent_q = route(all_grad, experts, True)
    weights = gather_weights(columns, sent_q)
    rows_q = lax.all_to_all(sent_q, by_expert, 0, 0, tiled=True)
    row_sums, term = rows_backward(rows_in, rows_q, weights)
    reduced, weight_grad = scatter_weight_grad(term)
    returned = lax.all_to_all(row_sums.reshape(experts, SLOTS, width), by_expert, 0, 0, tiled=True)

    own_ids = expert_ids.T[None] == jnp.arange(experts, dtype=jnp.int32)[:, None, None]
    own = slots_of(own_ids[:, 0] | own_ids[:, 1])
    own_placing = own.astype(BF)
    flat = own_placing.reshape(experts * SLOTS, frames)
    frame_grad = out_grad.astype(F32) + dot(
        flat, returned.reshape(experts * SLOTS, width), ((0,), (0,))
    )
    gate_sums = jnp.einsum(
        "es,est,ekt->tk",
        returned[:, SPARE, :SLOTS].astype(F32),
        own.astype(F32),
        own_ids.astype(F32),
        precision="highest",
    )
    gate_out = (gate_sums / gate_values.astype(F32)).astype(BF)

    taps = conv_kernel.astype(F32)
    half = taps.shape[0] // 2
    rounded = frame_grad.astype(BF)
    low, high = halo_of(rounded, half)
    frame_grad, rounded, reduced = lax.optimization_barrier((frame_grad, rounded, reduced))
    rows = rounded.astype(F32)
    inner = convolved(frame_grad[EDGE : frames - EDGE], rows[EDGE - half : frames - EDGE + half], taps)
    low, high, inner, weight_grad = lax.optimization_barrier((low, high, inner, weight_grad))
    top = jnp.concatenate([low.astype(F32), rows[: EDGE + half]], axis=0)
    bottom = jnp.concatenate([rows[frames - EDGE - half :], high.astype(F32)], axis=0)
    first = convolved(frame_grad[:EDGE], top, taps)
    final = convolved(frame_grad[frames - EDGE :], bottom, taps)
    input_grad = jnp.concatenate([first, inner, final], axis=0)
    return input_grad, weight_grad, gate_out


def solution(mesh):
    grid = Mesh(mesh.devices.reshape(4, 8, 4, 2), ("y", "z", "x", "c"))
    frames = P(("y", "z", "x", "c"), None)
    weights = P(("x", "c"), ("y", "z"), None)
    in_specs = (frames, frames, frames, frames, P(), weights)
    out_specs = (frames, weights, frames)
    return jax.shard_map(local, mesh=grid, in_specs=in_specs, out_specs=out_specs, check_vma=False)
```

```python
import functools

import jax
import jax.numpy as jnp
from jax import lax
from jax.experimental import pallas as pl
from jax.experimental.pallas import tpu as pltpu
from jax.sharding import Mesh, PartitionSpec as P

BF = jnp.bfloat16
F32 = jnp.float32
SLOTS = 64
SPARE = 60
META = 8
STEP = 4
CHUNK = 256
EDGE = 16
EXTRA = 128


def dot(a, b, contract, batch=((), ())):
    return lax.dot_general(a, b, (contract, batch), preferred_element_type=F32)


def ring_ways(axis):
    count = lax.axis_size(axis)
    up = [(i, (i + 1) % count) for i in range(count)]
    return up, [(target, source) for source, target in up]


def ring_step(right, left, axis):
    up, down = ring_ways(axis)
    return lax.ppermute(right, axis, up), lax.ppermute(left, axis, down)


def own_columns(expert_weights):
    ny = lax.axis_size("y")
    rows, width = expert_weights.shape[1], expert_weights.shape[2]
    part = width // (3 * ny)
    sliced = expert_weights[0].reshape(rows, 3, ny, part).transpose(2, 0, 1, 3)
    return lax.all_to_all(sliced.reshape(ny, rows, 3 * part), "y", 0, 0, tiled=True)


def gather_weights(mine, after):
    ny, rows, width = mine.shape
    nz = lax.axis_size("z")
    me = lax.axis_index("z")

    def place(buffer, shard, z):
        return lax.dynamic_update_slice(buffer, shard[:, None], (0, z % nz, 0, 0))

    buffer = place(jnp.zeros((ny, nz, rows, width), BF), mine, me)
    mine, after = lax.optimization_barrier((mine, after))
    right = left = mine
    for step in range(1, nz // 2):
        right, left = ring_step(right, left, "z")
        buffer = place(place(buffer, right, me - step), left, me + step)
    up, down = ring_ways("z")
    across = [lax.ppermute(right[: ny // 2], "z", up), lax.ppermute(left[ny // 2 :], "z", down)]
    buffer = place(buffer, jnp.concatenate(across, axis=0), me + nz // 2)
    return buffer.reshape(ny * nz * rows, width)


def merge_kernel(parts_ref, out_ref):
    ny, rows, wide = parts_ref.shape
    part = wide // 3
    for k in range(3):
        for y in range(ny):
            first = (k * ny + y) * part
            out_ref[:, first : first + part] = parts_ref[y, :, k * part : (k + 1) * part]


def merged(parts):
    ny, rows, wide = parts.shape
    return pl.pallas_call(merge_kernel, out_shape=jax.ShapeDtypeStruct((rows, ny * wide), BF))(parts)


def sum_kernel(*refs):
    out_ref = refs[-1]
    half = refs[0].shape[1]
    for side in range(2):
        own, below, above = (ref[...].astype(F32) for ref in refs[3 * side : 3 * side + 3])
        out_ref[:, side * half : (side + 1) * half] = (own + below + above).astype(BF)


def summed(*parts):
    rows, half = parts[0].shape
    shape = jax.ShapeDtypeStruct((rows, 2 * half), BF)
    limit = pltpu.CompilerParams(vmem_limit_bytes=32 * 1024 * 1024)
    return pl.pallas_call(sum_kernel, out_shape=shape, compiler_params=limit)(*parts)


def scatter_weight_grad(term):
    ny, nz = lax.axis_size("y"), lax.axis_size("z")
    rows, part = term.shape[2], term.shape[3] // 3
    mine = lax.psum_scatter(term.reshape(nz * ny * rows, 3 * part), "z", scatter_dimension=0, tiled=True)
    back = lax.all_to_all(mine.reshape(ny, rows, 3 * part), "y", 0, 0, tiled=True)
    return mine, merged(back)[None]


def slots_of(chosen):
    frames = chosen.shape[-1]
    before = (jnp.arange(frames)[:, None] < jnp.arange(frames)[None, :]).astype(BF)
    ranks = dot(chosen.astype(BF), before, ((chosen.ndim - 1,), (0,))).astype(jnp.int32)
    return chosen[..., None, :] & (ranks[..., None, :] == jnp.arange(SLOTS)[:, None])


def halo_of(block, width):
    axes = ("y", "z", "x", "c")
    count = 1
    for axis in axes:
        count *= lax.axis_size(axis)
    forward = [(i, i + 1) for i in range(count - 1)]
    backward = [(target, source) for source, target in forward]
    low = lax.ppermute(block[block.shape[0] - width :], axes, forward)
    return low, lax.ppermute(block[:width], axes, backward)


def convolved(centre, rows, taps):
    total = centre
    count = taps.shape[0]
    for offset in range(count):
        first = count - 1 - offset
        total = total + taps[offset] * rows[first : first + centre.shape[0]]
    return total.astype(BF)


def route_kernel(plain, x_ref, out_ref):
    rows, width = x_ref.shape[1:]
    frames, experts = rows - META, out_ref.shape[0]
    meta = x_ref[0, frames:rows, :frames].astype(F32)
    names = lax.broadcasted_iota(jnp.int32, (experts, frames), 0).astype(F32)
    first, second = (names == meta[0:1]).astype(F32), (names == meta[1:2]).astype(F32)
    chosen = first + second
    gate = first * meta[2:3] + second * meta[3:4]
    earlier = lax.broadcasted_iota(jnp.int32, (frames, frames), 0)
    before = (earlier < lax.broadcasted_iota(jnp.int32, (frames, frames), 1)).astype(F32).astype(BF)
    ranks = dot(chosen.astype(BF), before, ((1,), (0,)))
    slot = lax.broadcasted_iota(jnp.int32, (SLOTS, frames), 0).astype(F32)
    for e in range(experts):
        here = (slot == ranks[e : e + 1]) & (chosen[e : e + 1] > 0.0)
        if plain:
            placing = jnp.where(here, 1.0, 0.0).astype(BF)
            out_ref[e, 0, :, :plain] = dot(placing, x_ref[0, :frames, :plain], ((1,), (0,))).astype(BF)
        placing = jnp.where(here, gate[e : e + 1], 0.0).astype(BF)
        out_ref[e, 0, :, plain:] = dot(placing, x_ref[0, :frames, plain:], ((1,), (0,))).astype(BF)


def route(packed, experts, plain):
    groups, rows, width = packed.shape
    return pl.pallas_call(
        functools.partial(route_kernel, plain),
        grid=(groups,),
        in_specs=[pl.BlockSpec((1, rows, width), lambda i: (i, 0, 0))],
        out_specs=pl.BlockSpec((experts, 1, SLOTS, width), lambda i: (0, i, 0, 0)),
        out_shape=pltpu.HBM((experts, groups, SLOTS, width), BF),
        compiler_params=pltpu.CompilerParams(vmem_limit_bytes=32 * 1024 * 1024),
    )(packed)


def rows_of(u, q, w_ref, low_ref, high_ref, pre_ref, h_ref):
    steps, part, half = h_ref.shape[0], h_ref.shape[3], low_ref.shape[1]
    gate_part = 0.0
    for c in range(0, part, CHUNK):
        gate_in = dot(u, w_ref[:, c : c + CHUNK], ((1,), (0,)))
        up_in = dot(u, w_ref[:, part + c : part + c + CHUNK], ((1,), (0,)))
        hidden_grad = dot(q, w_ref[:, 2 * part + c : 2 * part + c + CHUNK], ((1,), (0,)))
        sigmoid = jax.nn.sigmoid(gate_in)
        activated = gate_in * sigmoid
        hidden = (activated * up_in).astype(BF)
        h_ref[:, 0, :, c : c + CHUNK] = hidden.reshape(steps, SLOTS, CHUNK)
        slope = sigmoid * (1.0 + gate_in * (1.0 - sigmoid))
        pre_ref[:, c : c + CHUNK] = (hidden_grad * up_in * slope).astype(BF)
        pre_ref[:, part + c : part + c + CHUNK] = (hidden_grad * activated).astype(BF)
        gate_part += jnp.sum(hidden.astype(F32) * hidden_grad, axis=1, keepdims=True)
    row_grad = dot(pre_ref[...], w_ref[:, : 2 * part], ((1,), (1,)))
    high_ref[...] = row_grad[:, half:].astype(BF)
    low_ref[...] = row_grad[:, :half].astype(BF)
    row = lax.broadcasted_iota(jnp.int32, (SLOTS, 128), 0)
    lane = lax.broadcasted_iota(jnp.int32, (SLOTS, 128), 1)
    for j in range(steps):
        place = pl.ds(j * SLOTS, SLOTS)
        diagonal = jnp.where(row == lane, gate_part[j * SLOTS : (j + 1) * SLOTS], 0.0)
        line = jnp.sum(diagonal, axis=0, keepdims=True)
        low_ref[place, :128] = jnp.where(row == SPARE, line, low_ref[place, :128].astype(F32)).astype(BF)


def both_rows(u_ref, q_ref, width):
    count = u_ref.shape[1] * SLOTS
    rows = u_ref[0].reshape(count, u_ref.shape[3])
    q = jnp.concatenate([rows[:, width:], q_ref[:, 0].reshape(count, q_ref.shape[3])], axis=1)
    return rows[:, :width], q


def rows_kernel(targets, steps, info, u_ref, q_ref, w_ref, *refs):
    pre_ref, h_ref = refs[-2:]
    pairs = refs[-2 - 2 * targets : -2]
    for t in range(targets):

        @pl.when(pl.program_id(0) // steps == t)
        def _():
            u, q = both_rows(u_ref, q_ref, w_ref.shape[0])
            rows_of(u, q, w_ref, pairs[2 * t], pairs[2 * t + 1], pre_ref, h_ref)


def last_kernel(info, u_ref, q_ref, w_ref, pre_ref, h_ref, low_ref, high_ref, term_ref, own_pre, own_h, total):
    step, last = pl.program_id(0), pl.num_programs(0) - 1
    count = u_ref.shape[1] * SLOTS
    part, wide = h_ref.shape[3], pre_ref.shape[1]
    groups, each = term_ref.shape[1], term_ref.shape[0] * term_ref.shape[2]
    u, q = both_rows(u_ref, q_ref, w_ref.shape[0])

    @pl.when(step == 0)
    def _():
        rows_of(u, q, w_ref, low_ref, high_ref, own_pre, own_h)
        total[:, :wide] = dot(u, own_pre[...], ((0,), (0,)))
        total[:, wide:] = dot(q, own_h[:, 0].reshape(count, part), ((0,), (0,)))

    @pl.when(step > 0)
    def _():
        total[:, :wide] += dot(u, pre_ref[...], ((0,), (0,)))
        total[:, wide:] += dot(q, h_ref[:, 0].reshape(count, part), ((0,), (0,)))

    @pl.when(step == last)
    def _():
        for g in range(groups):
            block = total[g * each : (g + 1) * each].astype(BF)
            term_ref[:, g] = block.reshape(term_ref.shape[0], term_ref.shape[2], term_ref.shape[3])


def last_rows(targets, rows_in, rows_q, weights, pre_grads, hidden):
    groups, sources = rows_in.shape[:2]
    width = weights.shape[0]
    nz = lax.axis_size("z")
    part = weights.shape[1] // 3
    mine = sources * SLOTS
    each = width // (groups * nz)
    info = jnp.stack(targets).astype(jnp.int32)
    fixed = lambda i, info: (0, 0)
    return pl.pallas_call(
        last_kernel,
        grid_spec=pltpu.PrefetchScalarGridSpec(
            num_scalar_prefetch=1,
            grid=(groups,),
            in_specs=[
                pl.BlockSpec((1, sources, SLOTS, rows_in.shape[3]), lambda i, info: (info[i], 0, 0, 0)),
                pl.BlockSpec((sources, 1, SLOTS, rows_q.shape[3]), lambda i, info: (0, info[i], 0, 0)),
                pl.BlockSpec(weights.shape, fixed),
                pl.BlockSpec((mine, 2 * part), lambda i, info: (info[jnp.maximum(i, 1)], 0)),
                pl.BlockSpec((sources, 1, SLOTS, part), lambda i, info: (0, info[jnp.maximum(i, 1)], 0, 0)),
            ],
            out_specs=[
                pl.BlockSpec((mine, width // 2), fixed),
                pl.BlockSpec((mine, width // 2), fixed),
                pl.BlockSpec((nz, groups, each, 3 * part), lambda i, info: (0, 0, 0, 0)),
            ],
            scratch_shapes=[
                pltpu.VMEM((mine, 2 * part), BF),
                pltpu.VMEM((sources, 1, SLOTS, part), BF),
                pltpu.VMEM((width, 3 * part), F32),
            ],
        ),
        out_shape=[
            jax.ShapeDtypeStruct((mine, width // 2), BF),
            jax.ShapeDtypeStruct((mine, width // 2), BF),
            jax.ShapeDtypeStruct((nz, groups, each, 3 * part), BF),
        ],
        compiler_params=pltpu.CompilerParams(vmem_limit_bytes=56 * 1024 * 1024),
    )(info, rows_in, rows_q, weights, pre_grads, hidden)


def expert_rows(targets, rows_in, rows_q, weights, kept):
    groups, sources = rows_in.shape[:2]
    width, part = weights.shape[0], weights.shape[1] // 3
    steps = sources // STEP
    count = len(targets)
    info = jnp.stack(targets).astype(jnp.int32)
    by_group = lambda i, info: (info[i // steps], i % steps, 0, 0)
    by_source = lambda i, info: (i % steps, info[i // steps], 0, 0)
    half_rows = [
        pl.BlockSpec((STEP * SLOTS, width // 2), lambda i, info, t=t: (jnp.clip(i - t * steps, 0, steps - 1), 0))
        for t in range(count)
        for _ in range(2)
    ]
    *halves, pre_grads, hidden = pl.pallas_call(
        functools.partial(rows_kernel, count, steps),
        grid_spec=pltpu.PrefetchScalarGridSpec(
            num_scalar_prefetch=1,
            grid=(count * steps,),
            in_specs=[
                pl.BlockSpec((1, STEP, SLOTS, rows_in.shape[3]), by_group),
                pl.BlockSpec((STEP, 1, SLOTS, rows_q.shape[3]), by_source),
                pl.BlockSpec(weights.shape, lambda i, info: (0, 0)),
            ]
            + [pl.BlockSpec(memory_space=pl.ANY) for _ in kept],
            out_specs=half_rows
            + [
                pl.BlockSpec((STEP * SLOTS, 2 * part), lambda i, info: (info[i // steps] * steps + i % steps, 0)),
                pl.BlockSpec((STEP, 1, SLOTS, part), by_source),
            ],
        ),
        out_shape=[jax.ShapeDtypeStruct((sources * SLOTS, width // 2), BF)] * (2 * count)
        + [
            jax.ShapeDtypeStruct((groups * sources * SLOTS, 2 * part), BF),
            jax.ShapeDtypeStruct((sources, groups, SLOTS, part), BF),
        ],
        input_output_aliases={4 + k: 2 * count + k for k in range(len(kept))},
        compiler_params=pltpu.CompilerParams(vmem_limit_bytes=52 * 1024 * 1024),
    )(info, rows_in, rows_q, weights, *kept)
    return halves, [pre_grads, hidden]


def add(*parts):
    return sum(part.astype(F32) for part in parts)


def rows_backward(rows_in, rows_q, weights):
    ny = lax.axis_size("y")
    me = lax.axis_index("y")
    up = [(i, (i + 1) % ny) for i in range(ny)]
    down = [(target, source) for source, target in up]

    def send(rows, way):
        return lax.ppermute(rows, "y", way)

    def run(offsets, kept):
        return expert_rows([(me + offset) % ny for offset in offsets], rows_in, rows_q, weights, kept)

    (far_low, far_high), kept = run([2], [])
    low_via, high_via = send(far_low, up), send(far_high, down)
    (up_low, up_high, down_low, down_high), kept = run([1, ny - 1], kept)
    low_via, high_via, kept = lax.optimization_barrier((low_via, high_via, kept))
    below_high, above_low = send(up_high, up), send(down_low, down)
    below_low = send(add(up_low, low_via).astype(BF), up)
    above_high = send(add(down_high, high_via).astype(BF), down)
    targets = [(me + offset) % ny for offset in (0, 2, 1, ny - 1)]
    own_low, own_high, term = last_rows(targets, rows_in, rows_q, weights, *kept)
    term, below_high, above_low = lax.optimization_barrier((term, below_high, above_low))
    return summed(own_low, below_low, above_low, own_high, below_high, above_high), term


def local(block_in, out_grad, gate_values, expert_ids, conv_kernel, expert_weights):
    frames, width = block_in.shape
    ny, experts = lax.axis_size("y"), lax.axis_size("x") * lax.axis_size("c")
    by_expert = ("x", "c")

    meta = jnp.concatenate([expert_ids.astype(BF).T, gate_values.T], axis=0)

    def packed(*arrays):
        rows = jnp.concatenate(arrays, axis=1)
        return jnp.concatenate([rows, jnp.pad(meta, ((0, META - 4), (0, rows.shape[1] - frames)))], axis=0)

    all_grad = lax.all_gather(packed(out_grad[:, EXTRA:]), "y", axis=0, tiled=False)
    sent_in = route(packed(block_in, out_grad[:, :EXTRA])[None], experts, width)
    mine_in = lax.all_to_all(sent_in, by_expert, 0, 0, tiled=True)
    mine_in, expert_weights = lax.optimization_barrier((mine_in, expert_weights))
    columns = own_columns(expert_weights)
    all_grad, columns = lax.optimization_barrier((all_grad, columns))
    rows_in = lax.all_gather(mine_in[:, 0], "y", axis=0, tiled=False)
    sent_q = route(all_grad, experts, 0)
    weights = gather_weights(columns, sent_q)
    rows_q = lax.all_to_all(sent_q, by_expert, 0, 0, tiled=True)
    row_sums, term = rows_backward(rows_in, rows_q, weights)
    reduced, weight_grad = scatter_weight_grad(term)
    returned = lax.all_to_all(row_sums.reshape(experts, SLOTS, width), by_expert, 0, 0, tiled=True)

    own_ids = expert_ids.T[None] == jnp.arange(experts, dtype=jnp.int32)[:, None, None]
    own = slots_of(own_ids[:, 0] | own_ids[:, 1])
    own_placing = own.astype(BF)
    flat = own_placing.reshape(experts * SLOTS, frames)
    frame_grad = out_grad.astype(F32) + dot(
        flat, returned.reshape(experts * SLOTS, width), ((0,), (0,))
    )
    gate_sums = jnp.einsum(
        "es,est,ekt->tk",
        returned[:, SPARE, :SLOTS].astype(F32),
        own.astype(F32),
        own_ids.astype(F32),
        precision="highest",
    )
    gate_out = (gate_sums / gate_values.astype(F32)).astype(BF)

    taps = conv_kernel.astype(F32)
    half = taps.shape[0] // 2
    rounded = frame_grad.astype(BF)
    low, high = halo_of(rounded, half)
    frame_grad, rounded, reduced = lax.optimization_barrier((frame_grad, rounded, reduced))
    rows = rounded.astype(F32)
    inner = convolved(frame_grad[EDGE : frames - EDGE], rows[EDGE - half : frames - EDGE + half], taps)
    low, high, inner, weight_grad = lax.optimization_barrier((low, high, inner, weight_grad))
    top = jnp.concatenate([low.astype(F32), rows[: EDGE + half]], axis=0)
    bottom = jnp.concatenate([rows[frames - EDGE - half :], high.astype(F32)], axis=0)
    first = convolved(frame_grad[:EDGE], top, taps)
    final = convolved(frame_grad[frames - EDGE :], bottom, taps)
    input_grad = jnp.concatenate([first, inner, final], axis=0)
    return input_grad, weight_grad, gate_out


def solution(mesh):
    grid = Mesh(mesh.devices.reshape(4, 8, 4, 2), ("y", "z", "x", "c"))
    frames = P(("y", "z", "x", "c"), None)
    weights = P(("x", "c"), ("y", "z"), None)
    in_specs = (frames, frames, frames, frames, P(), weights)
    out_specs = (frames, weights, frames)
    return jax.shard_map(local, mesh=grid, in_specs=in_specs, out_specs=out_specs, check_vma=False)
```

```python
import functools

import jax
import jax.numpy as jnp
from jax import lax
from jax.experimental import pallas as pl
from jax.experimental.pallas import tpu as pltpu
from jax.sharding import Mesh, PartitionSpec as P

BF = jnp.bfloat16
F32 = jnp.float32
SLOTS = 64
SPARE = 60
META = 8
STEP = 4
CHUNK = 256
EDGE = 16
EXTRA = 128


def dot(a, b, contract, batch=((), ())):
    return lax.dot_general(a, b, (contract, batch), preferred_element_type=F32)


def ring_ways(axis):
    count = lax.axis_size(axis)
    up = [(i, (i + 1) % count) for i in range(count)]
    return up, [(target, source) for source, target in up]


def ring_step(right, left, axis):
    up, down = ring_ways(axis)
    return lax.ppermute(right, axis, up), lax.ppermute(left, axis, down)


def own_columns(expert_weights):
    ny = lax.axis_size("y")
    rows, width = expert_weights.shape[1], expert_weights.shape[2]
    part = width // (3 * ny)
    sliced = expert_weights[0].reshape(rows, 3, ny, part).transpose(2, 0, 1, 3)
    return lax.all_to_all(sliced.reshape(ny, rows, 3 * part), "y", 0, 0, tiled=True)


def gather_weights(mine, after):
    ny, rows, width = mine.shape
    nz = lax.axis_size("z")
    me = lax.axis_index("z")

    def place(buffer, shard, z):
        return lax.dynamic_update_slice(buffer, shard[:, None], (0, z % nz, 0, 0))

    up, down = ring_ways("z")
    mine, after = lax.optimization_barrier((mine, after))
    halves = [[mine[: ny // 2]] * 2, [mine[ny // 2 :]] * 2]
    held = {0: mine}
    for step in range(1, nz // 2):
        halves = [list(ring_step(right, left, "z")) for right, left in halves]
        for way, sign in enumerate((-1, 1)):
            held[sign * step] = jnp.concatenate([half[way] for half in halves], axis=0)
    across = [
        lax.ppermute(half[way][way : way + 1], "z", (up, down)[way]) for half in halves for way in range(2)
    ]
    held[nz // 2] = jnp.concatenate(across, axis=0)
    buffer = jnp.zeros((ny, nz, rows, width), BF)
    for offset, shard in held.items():
        buffer = place(buffer, shard, me + offset)
    return buffer.reshape(ny * nz * rows, width)


def merge_kernel(parts_ref, out_ref):
    ny, rows, wide = parts_ref.shape
    part = wide // 3
    for k in range(3):
        for y in range(ny):
            first = (k * ny + y) * part
            out_ref[:, first : first + part] = parts_ref[y, :, k * part : (k + 1) * part]


def merged(parts):
    ny, rows, wide = parts.shape
    return pl.pallas_call(merge_kernel, out_shape=jax.ShapeDtypeStruct((rows, ny * wide), BF))(parts)


def sum_kernel(*refs):
    out_ref = refs[-1]
    half = refs[0].shape[1]
    for side in range(2):
        own, below, above = (ref[...].astype(F32) for ref in refs[3 * side : 3 * side + 3])
        out_ref[:, side * half : (side + 1) * half] = (own + below + above).astype(BF)


def summed(*parts):
    rows, half = parts[0].shape
    shape = jax.ShapeDtypeStruct((rows, 2 * half), BF)
    limit = pltpu.CompilerParams(vmem_limit_bytes=32 * 1024 * 1024)
    return pl.pallas_call(sum_kernel, out_shape=shape, compiler_params=limit)(*parts)


def scatter_weight_grad(term):
    ny, nz = lax.axis_size("y"), lax.axis_size("z")
    rows, part = term.shape[2], term.shape[3] // 3
    mine = lax.psum_scatter(term.reshape(nz * ny * rows, 3 * part), "z", scatter_dimension=0, tiled=True)
    back = lax.all_to_all(mine.reshape(ny, rows, 3 * part), "y", 0, 0, tiled=True)
    return mine, merged(back)[None]


def slots_of(chosen):
    frames = chosen.shape[-1]
    before = (jnp.arange(frames)[:, None] < jnp.arange(frames)[None, :]).astype(BF)
    ranks = dot(chosen.astype(BF), before, ((chosen.ndim - 1,), (0,))).astype(jnp.int32)
    return chosen[..., None, :] & (ranks[..., None, :] == jnp.arange(SLOTS)[:, None])


def halo_of(block, width):
    axes = ("y", "z", "x", "c")
    count = 1
    for axis in axes:
        count *= lax.axis_size(axis)
    forward = [(i, i + 1) for i in range(count - 1)]
    backward = [(target, source) for source, target in forward]
    low = lax.ppermute(block[block.shape[0] - width :], axes, forward)
    return low, lax.ppermute(block[:width], axes, backward)


def convolved(centre, rows, taps):
    total = centre
    count = taps.shape[0]
    for offset in range(count):
        first = count - 1 - offset
        total = total + taps[offset] * rows[first : first + centre.shape[0]]
    return total.astype(BF)


def route_kernel(plain, x_ref, out_ref):
    rows, width = x_ref.shape[1:]
    frames, experts = rows - META, out_ref.shape[0]
    meta = x_ref[0, frames:rows, :frames].astype(F32)
    names = lax.broadcasted_iota(jnp.int32, (experts, frames), 0).astype(F32)
    first, second = (names == meta[0:1]).astype(F32), (names == meta[1:2]).astype(F32)
    chosen = first + second
    gate = first * meta[2:3] + second * meta[3:4]
    earlier = lax.broadcasted_iota(jnp.int32, (frames, frames), 0)
    before = (earlier < lax.broadcasted_iota(jnp.int32, (frames, frames), 1)).astype(F32).astype(BF)
    ranks = dot(chosen.astype(BF), before, ((1,), (0,)))
    slot = lax.broadcasted_iota(jnp.int32, (SLOTS, frames), 0).astype(F32)
    for e in range(experts):
        here = (slot == ranks[e : e + 1]) & (chosen[e : e + 1] > 0.0)
        if plain:
            placing = jnp.where(here, 1.0, 0.0).astype(BF)
            out_ref[e, 0, :, :plain] = dot(placing, x_ref[0, :frames, :plain], ((1,), (0,))).astype(BF)
        placing = jnp.where(here, gate[e : e + 1], 0.0).astype(BF)
        out_ref[e, 0, :, plain:] = dot(placing, x_ref[0, :frames, plain:], ((1,), (0,))).astype(BF)


def route(packed, experts, plain):
    groups, rows, width = packed.shape
    return pl.pallas_call(
        functools.partial(route_kernel, plain),
        grid=(groups,),
        in_specs=[pl.BlockSpec((1, rows, width), lambda i: (i, 0, 0))],
        out_specs=pl.BlockSpec((experts, 1, SLOTS, width), lambda i: (0, i, 0, 0)),
        out_shape=pltpu.HBM((experts, groups, SLOTS, width), BF),
        compiler_params=pltpu.CompilerParams(vmem_limit_bytes=32 * 1024 * 1024),
    )(packed)


def rows_of(u, q, w_ref, low_ref, high_ref, pre_ref, h_ref):
    steps, part, half = h_ref.shape[0], h_ref.shape[3], low_ref.shape[1]
    gate_part = 0.0
    for c in range(0, part, CHUNK):
        gate_in = dot(u, w_ref[:, c : c + CHUNK], ((1,), (0,)))
        up_in = dot(u, w_ref[:, part + c : part + c + CHUNK], ((1,), (0,)))
        hidden_grad = dot(q, w_ref[:, 2 * part + c : 2 * part + c + CHUNK], ((1,), (0,)))
        sigmoid = jax.nn.sigmoid(gate_in)
        activated = gate_in * sigmoid
        hidden = (activated * up_in).astype(BF)
        h_ref[:, 0, :, c : c + CHUNK] = hidden.reshape(steps, SLOTS, CHUNK)
        slope = sigmoid * (1.0 + gate_in * (1.0 - sigmoid))
        pre_ref[:, c : c + CHUNK] = (hidden_grad * up_in * slope).astype(BF)
        pre_ref[:, part + c : part + c + CHUNK] = (hidden_grad * activated).astype(BF)
        gate_part += jnp.sum(hidden.astype(F32) * hidden_grad, axis=1, keepdims=True)
    row_grad = dot(pre_ref[...], w_ref[:, : 2 * part], ((1,), (1,)))
    high_ref[...] = row_grad[:, half:].astype(BF)
    low_ref[...] = row_grad[:, :half].astype(BF)
    row = lax.broadcasted_iota(jnp.int32, (SLOTS, 128), 0)
    lane = lax.broadcasted_iota(jnp.int32, (SLOTS, 128), 1)
    for j in range(steps):
        place = pl.ds(j * SLOTS, SLOTS)
        diagonal = jnp.where(row == lane, gate_part[j * SLOTS : (j + 1) * SLOTS], 0.0)
        line = jnp.sum(diagonal, axis=0, keepdims=True)
        low_ref[place, :128] = jnp.where(row == SPARE, line, low_ref[place, :128].astype(F32)).astype(BF)


def both_rows(u_ref, q_ref, width):
    count = u_ref.shape[1] * SLOTS
    rows = u_ref[0].reshape(count, u_ref.shape[3])
    q = jnp.concatenate([rows[:, width:], q_ref[:, 0].reshape(count, q_ref.shape[3])], axis=1)
    return rows[:, :width], q


def rows_kernel(targets, steps, info, u_ref, q_ref, w_ref, *refs):
    pre_ref, h_ref = refs[-2:]
    pairs = refs[-2 - 2 * targets : -2]
    for t in range(targets):

        @pl.when(pl.program_id(0) // steps == t)
        def _():
            u, q = both_rows(u_ref, q_ref, w_ref.shape[0])
            rows_of(u, q, w_ref, pairs[2 * t], pairs[2 * t + 1], pre_ref, h_ref)


def last_kernel(info, u_ref, q_ref, w_ref, pre_ref, h_ref, low_ref, high_ref, term_ref, own_pre, own_h, total):
    step, last = pl.program_id(0), pl.num_programs(0) - 1
    count = u_ref.shape[1] * SLOTS
    part, wide = h_ref.shape[3], pre_ref.shape[1]
    groups, each = term_ref.shape[1], term_ref.shape[0] * term_ref.shape[2]
    u, q = both_rows(u_ref, q_ref, w_ref.shape[0])

    @pl.when(step == 0)
    def _():
        rows_of(u, q, w_ref, low_ref, high_ref, own_pre, own_h)
        total[:, :wide] = dot(u, own_pre[...], ((0,), (0,)))
        total[:, wide:] = dot(q, own_h[:, 0].reshape(count, part), ((0,), (0,)))

    @pl.when(step > 0)
    def _():
        total[:, :wide] += dot(u, pre_ref[...], ((0,), (0,)))
        total[:, wide:] += dot(q, h_ref[:, 0].reshape(count, part), ((0,), (0,)))

    @pl.when(step == last)
    def _():
        for g in range(groups):
            block = total[g * each : (g + 1) * each].astype(BF)
            term_ref[:, g] = block.reshape(term_ref.shape[0], term_ref.shape[2], term_ref.shape[3])


def last_rows(targets, rows_in, rows_q, weights, pre_grads, hidden):
    groups, sources = rows_in.shape[:2]
    width = weights.shape[0]
    nz = lax.axis_size("z")
    part = weights.shape[1] // 3
    mine = sources * SLOTS
    each = width // (groups * nz)
    info = jnp.stack(targets).astype(jnp.int32)
    fixed = lambda i, info: (0, 0)
    return pl.pallas_call(
        last_kernel,
        grid_spec=pltpu.PrefetchScalarGridSpec(
            num_scalar_prefetch=1,
            grid=(groups,),
            in_specs=[
                pl.BlockSpec((1, sources, SLOTS, rows_in.shape[3]), lambda i, info: (info[i], 0, 0, 0)),
                pl.BlockSpec((sources, 1, SLOTS, rows_q.shape[3]), lambda i, info: (0, info[i], 0, 0)),
                pl.BlockSpec(weights.shape, fixed),
                pl.BlockSpec((mine, 2 * part), lambda i, info: (info[jnp.maximum(i, 1)], 0)),
                pl.BlockSpec((sources, 1, SLOTS, part), lambda i, info: (0, info[jnp.maximum(i, 1)], 0, 0)),
            ],
            out_specs=[
                pl.BlockSpec((mine, width // 2), fixed),
                pl.BlockSpec((mine, width // 2), fixed),
                pl.BlockSpec((nz, groups, each, 3 * part), lambda i, info: (0, 0, 0, 0)),
            ],
            scratch_shapes=[
                pltpu.VMEM((mine, 2 * part), BF),
                pltpu.VMEM((sources, 1, SLOTS, part), BF),
                pltpu.VMEM((width, 3 * part), F32),
            ],
        ),
        out_shape=[
            jax.ShapeDtypeStruct((mine, width // 2), BF),
            jax.ShapeDtypeStruct((mine, width // 2), BF),
            jax.ShapeDtypeStruct((nz, groups, each, 3 * part), BF),
        ],
        compiler_params=pltpu.CompilerParams(vmem_limit_bytes=56 * 1024 * 1024),
    )(info, rows_in, rows_q, weights, pre_grads, hidden)


def expert_rows(targets, rows_in, rows_q, weights, kept):
    groups, sources = rows_in.shape[:2]
    width, part = weights.shape[0], weights.shape[1] // 3
    steps = sources // STEP
    count = len(targets)
    info = jnp.stack(targets).astype(jnp.int32)
    by_group = lambda i, info: (info[i // steps], i % steps, 0, 0)
    by_source = lambda i, info: (i % steps, info[i // steps], 0, 0)
    half_rows = [
        pl.BlockSpec((STEP * SLOTS, width // 2), lambda i, info, t=t: (jnp.clip(i - t * steps, 0, steps - 1), 0))
        for t in range(count)
        for _ in range(2)
    ]
    *halves, pre_grads, hidden = pl.pallas_call(
        functools.partial(rows_kernel, count, steps),
        grid_spec=pltpu.PrefetchScalarGridSpec(
            num_scalar_prefetch=1,
            grid=(count * steps,),
            in_specs=[
                pl.BlockSpec((1, STEP, SLOTS, rows_in.shape[3]), by_group),
                pl.BlockSpec((STEP, 1, SLOTS, rows_q.shape[3]), by_source),
                pl.BlockSpec(weights.shape, lambda i, info: (0, 0)),
            ]
            + [pl.BlockSpec(memory_space=pl.ANY) for _ in kept],
            out_specs=half_rows
            + [
                pl.BlockSpec((STEP * SLOTS, 2 * part), lambda i, info: (info[i // steps] * steps + i % steps, 0)),
                pl.BlockSpec((STEP, 1, SLOTS, part), by_source),
            ],
        ),
        out_shape=[jax.ShapeDtypeStruct((sources * SLOTS, width // 2), BF)] * (2 * count)
        + [
            jax.ShapeDtypeStruct((groups * sources * SLOTS, 2 * part), BF),
            jax.ShapeDtypeStruct((sources, groups, SLOTS, part), BF),
        ],
        input_output_aliases={4 + k: 2 * count + k for k in range(len(kept))},
        compiler_params=pltpu.CompilerParams(vmem_limit_bytes=52 * 1024 * 1024),
    )(info, rows_in, rows_q, weights, *kept)
    return halves, [pre_grads, hidden]


def add(*parts):
    return sum(part.astype(F32) for part in parts)


def rows_backward(rows_in, rows_q, weights):
    ny = lax.axis_size("y")
    me = lax.axis_index("y")
    up = [(i, (i + 1) % ny) for i in range(ny)]
    down = [(target, source) for source, target in up]

    def send(rows, way):
        return lax.ppermute(rows, "y", way)

    def run(offsets, kept):
        return expert_rows([(me + offset) % ny for offset in offsets], rows_in, rows_q, weights, kept)

    (far_low, far_high), kept = run([2], [])
    low_via, high_via = send(far_low, up), send(far_high, down)
    (up_low, up_high, down_low, down_high), kept = run([1, ny - 1], kept)
    low_via, high_via, kept = lax.optimization_barrier((low_via, high_via, kept))
    below_high, above_low = send(up_high, up), send(down_low, down)
    below_low = send(add(up_low, low_via).astype(BF), up)
    above_high = send(add(down_high, high_via).astype(BF), down)
    targets = [(me + offset) % ny for offset in (0, 2, 1, ny - 1)]
    own_low, own_high, term = last_rows(targets, rows_in, rows_q, weights, *kept)
    term, below_high, above_low = lax.optimization_barrier((term, below_high, above_low))
    return summed(own_low, below_low, above_low, own_high, below_high, above_high), term


def local(block_in, out_grad, gate_values, expert_ids, conv_kernel, expert_weights):
    frames, width = block_in.shape
    ny, experts = lax.axis_size("y"), lax.axis_size("x") * lax.axis_size("c")
    by_expert = ("x", "c")

    meta = jnp.concatenate([expert_ids.astype(BF).T, gate_values.T], axis=0)

    def packed(*arrays):
        rows = jnp.concatenate(arrays, axis=1)
        return jnp.concatenate([rows, jnp.pad(meta, ((0, META - 4), (0, rows.shape[1] - frames)))], axis=0)

    all_grad = lax.all_gather(packed(out_grad[:, EXTRA:]), "y", axis=0, tiled=False)
    sent_in = route(packed(block_in, out_grad[:, :EXTRA])[None], experts, width)
    mine_in = lax.all_to_all(sent_in, by_expert, 0, 0, tiled=True)
    mine_in, expert_weights = lax.optimization_barrier((mine_in, expert_weights))
    columns = own_columns(expert_weights)
    all_grad, columns = lax.optimization_barrier((all_grad, columns))
    rows_in = lax.all_gather(mine_in[:, 0], "y", axis=0, tiled=False)
    sent_q = route(all_grad, experts, 0)
    weights = gather_weights(columns, sent_q)
    rows_q = lax.all_to_all(sent_q, by_expert, 0, 0, tiled=True)
    row_sums, term = rows_backward(rows_in, rows_q, weights)
    reduced, weight_grad = scatter_weight_grad(term)
    returned = lax.all_to_all(row_sums.reshape(experts, SLOTS, width), by_expert, 0, 0, tiled=True)

    own_ids = expert_ids.T[None] == jnp.arange(experts, dtype=jnp.int32)[:, None, None]
    own = slots_of(own_ids[:, 0] | own_ids[:, 1])
    own_placing = own.astype(BF)
    flat = own_placing.reshape(experts * SLOTS, frames)
    frame_grad = out_grad.astype(F32) + dot(
        flat, returned.reshape(experts * SLOTS, width), ((0,), (0,))
    )
    gate_sums = jnp.einsum(
        "es,est,ekt->tk",
        returned[:, SPARE, :SLOTS].astype(F32),
        own.astype(F32),
        own_ids.astype(F32),
        precision="highest",
    )
    gate_out = (gate_sums / gate_values.astype(F32)).astype(BF)

    taps = conv_kernel.astype(F32)
    half = taps.shape[0] // 2
    rounded = frame_grad.astype(BF)
    low, high = halo_of(rounded, half)
    frame_grad, rounded, reduced = lax.optimization_barrier((frame_grad, rounded, reduced))
    rows = rounded.astype(F32)
    inner = convolved(frame_grad[EDGE : frames - EDGE], rows[EDGE - half : frames - EDGE + half], taps)
    low, high, inner, weight_grad = lax.optimization_barrier((low, high, inner, weight_grad))
    top = jnp.concatenate([low.astype(F32), rows[: EDGE + half]], axis=0)
    bottom = jnp.concatenate([rows[frames - EDGE - half :], high.astype(F32)], axis=0)
    first = convolved(frame_grad[:EDGE], top, taps)
    final = convolved(frame_grad[frames - EDGE :], bottom, taps)
    input_grad = jnp.concatenate([first, inner, final], axis=0)
    return input_grad, weight_grad, gate_out


def solution(mesh):
    grid = Mesh(mesh.devices.reshape(4, 8, 4, 2), ("y", "z", "x", "c"))
    frames = P(("y", "z", "x", "c"), None)
    weights = P(("x", "c"), ("y", "z"), None)
    in_specs = (frames, frames, frames, frames, P(), weights)
    out_specs = (frames, weights, frames)
    return jax.shard_map(local, mesh=grid, in_specs=in_specs, out_specs=out_specs, check_vma=False)
```

```python
import functools

import jax
import jax.numpy as jnp
from jax import lax
from jax.experimental import pallas as pl
from jax.experimental.pallas import tpu as pltpu
from jax.sharding import Mesh, PartitionSpec as P

BF = jnp.bfloat16
F32 = jnp.float32
SLOTS = 64
SPARE = 60
META = 8
STEP = 4
CHUNK = 256
EDGE = 16
EXTRA = 128


def dot(a, b, contract, batch=((), ())):
    return lax.dot_general(a, b, (contract, batch), preferred_element_type=F32)


def ring_ways(axis):
    count = lax.axis_size(axis)
    up = [(i, (i + 1) % count) for i in range(count)]
    return up, [(target, source) for source, target in up]


def ring_step(right, left, axis):
    up, down = ring_ways(axis)
    return lax.ppermute(right, axis, up), lax.ppermute(left, axis, down)


def own_columns(expert_weights):
    ny = lax.axis_size("y")
    rows, width = expert_weights.shape[1], expert_weights.shape[2]
    part = width // (3 * ny)
    sliced = expert_weights[0].reshape(rows, 3, ny, part).transpose(2, 0, 1, 3)
    return lax.all_to_all(sliced.reshape(ny, rows, 3 * part), "y", 0, 0, tiled=True)


def gather_weights(mine, after):
    ny, rows, width = mine.shape
    nz = lax.axis_size("z")
    me = lax.axis_index("z")

    def place(buffer, shard, z):
        return lax.dynamic_update_slice(buffer, shard[:, None], (0, z % nz, 0, 0))

    up, down = ring_ways("z")
    mine, after = lax.optimization_barrier((mine, after))
    halves = [[mine[: ny // 2]] * 2, [mine[ny // 2 :]] * 2]
    held = {0: mine}
    for step in range(1, nz // 2):
        halves = [list(ring_step(right, left, "z")) for right, left in halves]
        for way, sign in enumerate((-1, 1)):
            held[sign * step] = jnp.concatenate([half[way] for half in halves], axis=0)
    across = [
        lax.ppermute(half[way][way : way + 1], "z", (up, down)[way]) for half in halves for way in range(2)
    ]
    held[nz // 2] = jnp.concatenate(across, axis=0)
    buffer = jnp.zeros((ny, nz, rows, width), BF)
    for offset, shard in held.items():
        buffer = place(buffer, shard, me + offset)
    return buffer.reshape(ny * nz * rows, width)


def merge_kernel(parts_ref, out_ref):
    ny, rows, wide = parts_ref.shape
    part = wide // 3
    for k in range(3):
        for y in range(ny):
            first = (k * ny + y) * part
            out_ref[:, first : first + part] = parts_ref[y, :, k * part : (k + 1) * part]


def merged(parts):
    ny, rows, wide = parts.shape
    return pl.pallas_call(merge_kernel, out_shape=jax.ShapeDtypeStruct((rows, ny * wide), BF))(parts)


def sum_kernel(*refs):
    out_ref = refs[-1]
    half = refs[0].shape[1]
    for side in range(2):
        own, below, above = (ref[...].astype(F32) for ref in refs[3 * side : 3 * side + 3])
        out_ref[:, side * half : (side + 1) * half] = (own + below + above).astype(BF)


def summed(*parts):
    rows, half = parts[0].shape
    shape = jax.ShapeDtypeStruct((rows, 2 * half), BF)
    limit = pltpu.CompilerParams(vmem_limit_bytes=32 * 1024 * 1024)
    return pl.pallas_call(sum_kernel, out_shape=shape, compiler_params=limit)(*parts)


def scatter_weight_grad(term):
    ny, nz = lax.axis_size("y"), lax.axis_size("z")
    rows, part = term.shape[2], term.shape[3] // 3
    mine = lax.psum_scatter(term.reshape(nz * ny * rows, 3 * part), "z", scatter_dimension=0, tiled=True)
    back = lax.all_to_all(mine.reshape(ny, rows, 3 * part), "y", 0, 0, tiled=True)
    return mine, merged(back)[None]


def slots_of(chosen):
    frames = chosen.shape[-1]
    before = (jnp.arange(frames)[:, None] < jnp.arange(frames)[None, :]).astype(BF)
    ranks = dot(chosen.astype(BF), before, ((chosen.ndim - 1,), (0,))).astype(jnp.int32)
    return chosen[..., None, :] & (ranks[..., None, :] == jnp.arange(SLOTS)[:, None])


def halo_of(block, width):
    axes = ("y", "z", "x", "c")
    count = 1
    for axis in axes:
        count *= lax.axis_size(axis)
    forward = [(i, i + 1) for i in range(count - 1)]
    backward = [(target, source) for source, target in forward]
    low = lax.ppermute(block[block.shape[0] - width :], axes, forward)
    return low, lax.ppermute(block[:width], axes, backward)


def convolved(centre, rows, taps):
    total = centre
    count = taps.shape[0]
    for offset in range(count):
        first = count - 1 - offset
        total = total + taps[offset] * rows[first : first + centre.shape[0]]
    return total.astype(BF)


def route_kernel(plain, x_ref, out_ref):
    rows, width = x_ref.shape[1:]
    frames, experts = rows - META, out_ref.shape[0]
    meta = x_ref[0, frames:rows, :frames].astype(F32)
    names = lax.broadcasted_iota(jnp.int32, (experts, frames), 0).astype(F32)
    first, second = (names == meta[0:1]).astype(F32), (names == meta[1:2]).astype(F32)
    chosen = first + second
    gate = first * meta[2:3] + second * meta[3:4]
    earlier = lax.broadcasted_iota(jnp.int32, (frames, frames), 0)
    before = (earlier < lax.broadcasted_iota(jnp.int32, (frames, frames), 1)).astype(F32).astype(BF)
    ranks = dot(chosen.astype(BF), before, ((1,), (0,)))
    slot = lax.broadcasted_iota(jnp.int32, (SLOTS, frames), 0).astype(F32)
    for e in range(experts):
        here = (slot == ranks[e : e + 1]) & (chosen[e : e + 1] > 0.0)
        if plain:
            placing = jnp.where(here, 1.0, 0.0).astype(BF)
            out_ref[e, 0, :, :plain] = dot(placing, x_ref[0, :frames, :plain], ((1,), (0,))).astype(BF)
        placing = jnp.where(here, gate[e : e + 1], 0.0).astype(BF)
        out_ref[e, 0, :, plain:] = dot(placing, x_ref[0, :frames, plain:], ((1,), (0,))).astype(BF)


def route(packed, experts, plain):
    groups, rows, width = packed.shape
    return pl.pallas_call(
        functools.partial(route_kernel, plain),
        grid=(groups,),
        in_specs=[pl.BlockSpec((1, rows, width), lambda i: (i, 0, 0))],
        out_specs=pl.BlockSpec((experts, 1, SLOTS, width), lambda i: (0, i, 0, 0)),
        out_shape=pltpu.HBM((experts, groups, SLOTS, width), BF),
        compiler_params=pltpu.CompilerParams(vmem_limit_bytes=32 * 1024 * 1024),
    )(packed)


def rows_of(u, q, w_ref, low_ref, high_ref, pre_ref, h_ref):
    steps, part, half = h_ref.shape[0], h_ref.shape[3], low_ref.shape[1]
    gate_part = 0.0
    for c in range(0, part, CHUNK):
        gate_in = dot(u, w_ref[:, c : c + CHUNK], ((1,), (0,)))
        up_in = dot(u, w_ref[:, part + c : part + c + CHUNK], ((1,), (0,)))
        hidden_grad = dot(q, w_ref[:, 2 * part + c : 2 * part + c + CHUNK], ((1,), (0,)))
        sigmoid = jax.nn.sigmoid(gate_in)
        activated = gate_in * sigmoid
        hidden = (activated * up_in).astype(BF)
        h_ref[:, 0, :, c : c + CHUNK] = hidden.reshape(steps, SLOTS, CHUNK)
        slope = sigmoid * (1.0 + gate_in * (1.0 - sigmoid))
        pre_ref[:, c : c + CHUNK] = (hidden_grad * up_in * slope).astype(BF)
        pre_ref[:, part + c : part + c + CHUNK] = (hidden_grad * activated).astype(BF)
        gate_part += jnp.sum(hidden.astype(F32) * hidden_grad, axis=1, keepdims=True)
    row_grad = dot(pre_ref[...], w_ref[:, : 2 * part], ((1,), (1,)))
    high_ref[...] = row_grad[:, half:].astype(BF)
    low_ref[...] = row_grad[:, :half].astype(BF)
    row = lax.broadcasted_iota(jnp.int32, (SLOTS, 128), 0)
    lane = lax.broadcasted_iota(jnp.int32, (SLOTS, 128), 1)
    for j in range(steps):
        place = pl.ds(j * SLOTS, SLOTS)
        diagonal = jnp.where(row == lane, gate_part[j * SLOTS : (j + 1) * SLOTS], 0.0)
        line = jnp.sum(diagonal, axis=0, keepdims=True)
        low_ref[place, :128] = jnp.where(row == SPARE, line, low_ref[place, :128].astype(F32)).astype(BF)


def both_rows(u_ref, q_ref, width):
    count = u_ref.shape[1] * SLOTS
    rows = u_ref[0].reshape(count, u_ref.shape[3])
    q = jnp.concatenate([rows[:, width:], q_ref[:, 0].reshape(count, q_ref.shape[3])], axis=1)
    return rows[:, :width], q


def rows_kernel(targets, steps, info, u_ref, q_ref, w_ref, *refs):
    pre_ref, h_ref = refs[-2:]
    pairs = refs[-2 - 2 * targets : -2]
    for t in range(targets):

        @pl.when(pl.program_id(0) // steps == t)
        def _():
            u, q = both_rows(u_ref, q_ref, w_ref.shape[0])
            rows_of(u, q, w_ref, pairs[2 * t], pairs[2 * t + 1], pre_ref, h_ref)


def last_kernel(info, u_ref, q_ref, w_ref, pre_ref, h_ref, low_ref, high_ref, term_ref, own_pre, own_h, total):
    step, last = pl.program_id(0), pl.num_programs(0) - 1
    count = u_ref.shape[1] * SLOTS
    part, wide = h_ref.shape[3], pre_ref.shape[1]
    groups, each = term_ref.shape[1], term_ref.shape[0] * term_ref.shape[2]
    u, q = both_rows(u_ref, q_ref, w_ref.shape[0])

    @pl.when(step == 0)
    def _():
        rows_of(u, q, w_ref, low_ref, high_ref, own_pre, own_h)
        total[:, :wide] = dot(u, own_pre[...], ((0,), (0,)))
        total[:, wide:] = dot(q, own_h[:, 0].reshape(count, part), ((0,), (0,)))

    @pl.when(step > 0)
    def _():
        total[:, :wide] += dot(u, pre_ref[...], ((0,), (0,)))
        total[:, wide:] += dot(q, h_ref[:, 0].reshape(count, part), ((0,), (0,)))

    @pl.when(step == last)
    def _():
        for g in range(groups):
            block = total[g * each : (g + 1) * each].astype(BF)
            term_ref[:, g] = block.reshape(term_ref.shape[0], term_ref.shape[2], term_ref.shape[3])


def last_rows(targets, rows_in, rows_q, weights, pre_grads, hidden):
    groups, sources = rows_in.shape[:2]
    width = weights.shape[0]
    nz = lax.axis_size("z")
    part = weights.shape[1] // 3
    mine = sources * SLOTS
    each = width // (groups * nz)
    info = jnp.stack(targets).astype(jnp.int32)
    fixed = lambda i, info: (0, 0)
    return pl.pallas_call(
        last_kernel,
        grid_spec=pltpu.PrefetchScalarGridSpec(
            num_scalar_prefetch=1,
            grid=(groups,),
            in_specs=[
                pl.BlockSpec((1, sources, SLOTS, rows_in.shape[3]), lambda i, info: (info[i], 0, 0, 0)),
                pl.BlockSpec((sources, 1, SLOTS, rows_q.shape[3]), lambda i, info: (0, info[i], 0, 0)),
                pl.BlockSpec(weights.shape, fixed),
                pl.BlockSpec((mine, 2 * part), lambda i, info: (info[jnp.maximum(i, 1)], 0)),
                pl.BlockSpec((sources, 1, SLOTS, part), lambda i, info: (0, info[jnp.maximum(i, 1)], 0, 0)),
            ],
            out_specs=[
                pl.BlockSpec((mine, width // 2), fixed),
                pl.BlockSpec((mine, width // 2), fixed),
                pl.BlockSpec((nz, groups, each, 3 * part), lambda i, info: (0, 0, 0, 0)),
            ],
            scratch_shapes=[
                pltpu.VMEM((mine, 2 * part), BF),
                pltpu.VMEM((sources, 1, SLOTS, part), BF),
                pltpu.VMEM((width, 3 * part), F32),
            ],
        ),
        out_shape=[
            jax.ShapeDtypeStruct((mine, width // 2), BF),
            jax.ShapeDtypeStruct((mine, width // 2), BF),
            jax.ShapeDtypeStruct((nz, groups, each, 3 * part), BF),
        ],
        compiler_params=pltpu.CompilerParams(vmem_limit_bytes=56 * 1024 * 1024),
    )(info, rows_in, rows_q, weights, pre_grads, hidden)


def expert_rows(targets, rows_in, rows_q, weights, kept):
    groups, sources = rows_in.shape[:2]
    width, part = weights.shape[0], weights.shape[1] // 3
    steps = sources // STEP
    count = len(targets)
    info = jnp.stack(targets).astype(jnp.int32)
    by_group = lambda i, info: (info[i // steps], i % steps, 0, 0)
    by_source = lambda i, info: (i % steps, info[i // steps], 0, 0)
    half_rows = [
        pl.BlockSpec((STEP * SLOTS, width // 2), lambda i, info, t=t: (jnp.clip(i - t * steps, 0, steps - 1), 0))
        for t in range(count)
        for _ in range(2)
    ]
    *halves, pre_grads, hidden = pl.pallas_call(
        functools.partial(rows_kernel, count, steps),
        grid_spec=pltpu.PrefetchScalarGridSpec(
            num_scalar_prefetch=1,
            grid=(count * steps,),
            in_specs=[
                pl.BlockSpec((1, STEP, SLOTS, rows_in.shape[3]), by_group),
                pl.BlockSpec((STEP, 1, SLOTS, rows_q.shape[3]), by_source),
                pl.BlockSpec(weights.shape, lambda i, info: (0, 0)),
            ]
            + [pl.BlockSpec(memory_space=pl.ANY) for _ in kept],
            out_specs=half_rows
            + [
                pl.BlockSpec((STEP * SLOTS, 2 * part), lambda i, info: (info[i // steps] * steps + i % steps, 0)),
                pl.BlockSpec((STEP, 1, SLOTS, part), by_source),
            ],
        ),
        out_shape=[jax.ShapeDtypeStruct((sources * SLOTS, width // 2), BF)] * (2 * count)
        + [
            jax.ShapeDtypeStruct((groups * sources * SLOTS, 2 * part), BF),
            jax.ShapeDtypeStruct((sources, groups, SLOTS, part), BF),
        ],
        input_output_aliases={4 + k: 2 * count + k for k in range(len(kept))},
        compiler_params=pltpu.CompilerParams(vmem_limit_bytes=52 * 1024 * 1024),
    )(info, rows_in, rows_q, weights, *kept)
    return halves, [pre_grads, hidden]


def add(*parts):
    return sum(part.astype(F32) for part in parts)


def rows_backward(rows_in, rows_q, weights):
    ny = lax.axis_size("y")
    me = lax.axis_index("y")
    up = [(i, (i + 1) % ny) for i in range(ny)]
    down = [(target, source) for source, target in up]

    def send(rows, way):
        return lax.ppermute(rows, "y", way)

    def run(offsets, kept):
        return expert_rows([(me + offset) % ny for offset in offsets], rows_in, rows_q, weights, kept)

    (far_low, far_high), kept = run([2], [])
    low_via, high_via = send(far_low, up), send(far_high, down)
    (up_low, up_high, down_low, down_high), kept = run([1, ny - 1], kept)
    low_via, high_via, kept = lax.optimization_barrier((low_via, high_via, kept))
    below_high, above_low = send(up_high, up), send(down_low, down)
    below_low = send(add(up_low, low_via).astype(BF), up)
    above_high = send(add(down_high, high_via).astype(BF), down)
    targets = [(me + offset) % ny for offset in (0, 2, 1, ny - 1)]
    own_low, own_high, term = last_rows(targets, rows_in, rows_q, weights, *kept)
    term, below_high, above_low = lax.optimization_barrier((term, below_high, above_low))
    return summed(own_low, below_low, above_low, own_high, below_high, above_high), term


def local(block_in, out_grad, gate_values, expert_ids, conv_kernel, expert_weights):
    frames, width = block_in.shape
    ny, experts = lax.axis_size("y"), lax.axis_size("x") * lax.axis_size("c")
    by_expert = ("x", "c")

    meta = jnp.concatenate([expert_ids.astype(BF).T, gate_values.T], axis=0)

    def packed(*arrays):
        rows = jnp.concatenate(arrays, axis=1)
        return jnp.concatenate([rows, jnp.pad(meta, ((0, META - 4), (0, rows.shape[1] - frames)))], axis=0)

    all_grad = lax.all_gather(packed(out_grad[:, EXTRA:]), "y", axis=0, tiled=False)
    sent_in = route(packed(block_in, out_grad[:, :EXTRA])[None], experts, width)
    mine_in = lax.all_to_all(sent_in, by_expert, 0, 0, tiled=True)
    mine_in, expert_weights = lax.optimization_barrier((mine_in, expert_weights))
    columns = own_columns(expert_weights)
    rows_in = lax.all_gather(mine_in[:, 0], "y", axis=0, tiled=False)
    sent_q = route(all_grad, experts, 0)
    columns, sent_q = lax.optimization_barrier((columns, sent_q))
    weights = gather_weights(columns, sent_q)
    rows_q = lax.all_to_all(sent_q, by_expert, 0, 0, tiled=True)
    row_sums, term = rows_backward(rows_in, rows_q, weights)
    reduced, weight_grad = scatter_weight_grad(term)
    returned = lax.all_to_all(row_sums.reshape(experts, SLOTS, width), by_expert, 0, 0, tiled=True)

    own_ids = expert_ids.T[None] == jnp.arange(experts, dtype=jnp.int32)[:, None, None]
    own = slots_of(own_ids[:, 0] | own_ids[:, 1])
    own_placing = own.astype(BF)
    flat = own_placing.reshape(experts * SLOTS, frames)
    frame_grad = out_grad.astype(F32) + dot(
        flat, returned.reshape(experts * SLOTS, width), ((0,), (0,))
    )
    gate_sums = jnp.einsum(
        "es,est,ekt->tk",
        returned[:, SPARE, :SLOTS].astype(F32),
        own.astype(F32),
        own_ids.astype(F32),
        precision="highest",
    )
    gate_out = (gate_sums / gate_values.astype(F32)).astype(BF)

    taps = conv_kernel.astype(F32)
    half = taps.shape[0] // 2
    rounded = frame_grad.astype(BF)
    low, high = halo_of(rounded, half)
    frame_grad, rounded, reduced = lax.optimization_barrier((frame_grad, rounded, reduced))
    rows = rounded.astype(F32)
    inner = convolved(frame_grad[EDGE : frames - EDGE], rows[EDGE - half : frames - EDGE + half], taps)
    low, high, inner, weight_grad = lax.optimization_barrier((low, high, inner, weight_grad))
    top = jnp.concatenate([low.astype(F32), rows[: EDGE + half]], axis=0)
    bottom = jnp.concatenate([rows[frames - EDGE - half :], high.astype(F32)], axis=0)
    first = convolved(frame_grad[:EDGE], top, taps)
    final = convolved(frame_grad[frames - EDGE :], bottom, taps)
    input_grad = jnp.concatenate([first, inner, final], axis=0)
    return input_grad, weight_grad, gate_out


def solution(mesh):
    grid = Mesh(mesh.devices.reshape(4, 8, 4, 2), ("y", "z", "x", "c"))
    frames = P(("y", "z", "x", "c"), None)
    weights = P(("x", "c"), ("y", "z"), None)
    in_specs = (frames, frames, frames, frames, P(), weights)
    out_specs = (frames, weights, frames)
    return jax.shard_map(local, mesh=grid, in_specs=in_specs, out_specs=out_specs, check_vma=False)
```
